32 devices in a mesh: img: 16 (over z, y, x), ch: 2 (over core).
Axes of the slice: x: 2, y: 2, z: 4, core: 2. Of those that a mesh axis runs over, the one named last changes fastest.
Arguments:
- pixels: bfloat16 [24064, 2016], P('img', 'ch'), may hold values from -30 to 30
- crop_counts: int32 [128], replicated, may hold values from 2 to 10, as said below
- first_weight: bfloat16 [2016, 2016], P(None, 'ch'), may hold values from -0.125 to 0.125
- first_gain: float32 [2016], P('ch'), may hold values from 0.5 to 1.5
- first_shift: float32 [2016], P('ch'), may hold values from -2 to 2
- group_weight: bfloat16 [3, 3, 56, 2016], P(None, None, None, 'ch'), may hold values from -0.25 to 0.25
- group_gain: float32 [2016], P('ch'), may hold values from 0.5 to 1.5
- group_shift: float32 [2016], P('ch'), may hold values from -2 to 2
- squeeze_weight: float32 [2016, 504], P(None, 'ch'), may hold values from -0.5 to 0.5
- squeeze_bias: float32 [504], P('ch'), may hold values from -3 to 3
- excite_weight: float32 [504, 2016], P(None, 'ch'), may hold values from -0.5 to 0.5
- excite_bias: float32 [2016], P('ch'), may hold values from -3 to 3
- last_weight: bfloat16 [2016, 2016], P(None, 'ch'), may hold values from -0.125 to 0.125
- last_gain: float32 [2016], P('ch'), may hold values from 0.5 to 1.5
- last_shift: float32 [2016], P('ch'), may hold values from -2 to 2
- output_grad: bfloat16 [24064, 2016], P('img', 'ch'), may hold values from -6 to 6
Outputs:
- block_out: bfloat16 [24064, 2016], P('img', 'ch')
- pixels_grad: float32 [24064, 2016], P('img', 'ch')
- first_weight_grad: float32 [2016, 2016], P(None, 'ch')
- first_gain_grad: float32 [2016], P('ch')
- first_shift_grad: float32 [2016], P('ch')
- group_weight_grad: float32 [3, 3, 56, 2016], P(None, None, None, 'ch')
- group_gain_grad: float32 [2016], P('ch')
- group_shift_grad: float32 [2016], P('ch')
- squeeze_weight_grad: float32 [2016, 504], P(None, 'ch')
- squeeze_bias_grad: float32 [504], P('ch')
- excite_weight_grad: float32 [504, 2016], P(None, 'ch')
- excite_bias_grad: float32 [2016], P('ch')
- last_weight_grad: float32 [2016, 2016], P(None, 'ch')
- last_gain_grad: float32 [2016], P('ch')
- last_shift_grad: float32 [2016], P('ch')
The draws below stay inside these ranges and needn't reach their ends.
Inputs may be any that keep to these rules, and one draw needn't show every extreme that they name: `crop_counts`: every image has at least 2 and at most 10 small crops; some image has 10 and some image 2.
All inputs are finite; a program needn't handle non-finite values.
Results may differ from the reference program's by a relative error of at most 0.0095.
Values may be sent and summed in bfloat16 or wider, within the bound.
A program may use at most 320 MiB of HBM per device.

```python
import jax
import jax.numpy as jnp
from jax import lax

C = 2016
GROUP_WIDTH = 56
SE_WIDTH = 504
GROUPS = 36
BIG_SIDE = 7
SMALL_SIDE = 3
BIG_CROPS = 2
SMALL_MOST = 10
ROWS_IMG = 188
IMAGES = 128


def draw_crop_counts(key, part):
    key = jax.random.fold_in(key, 11)
    first_key, second_key, third_key = jax.random.split(key, 3)
    drawn = jax.random.randint(first_key, (IMAGES,), 2, SMALL_MOST + 1)
    busiest = jax.random.randint(second_key, (), 0, IMAGES)
    lightest = (busiest + 1 + jax.random.randint(third_key, (), 0, IMAGES - 1)) % IMAGES
    return drawn.at[busiest].set(SMALL_MOST).at[lightest].set(2).astype(jnp.int32)


def draw_pixels(key, part):
    key = jax.random.fold_in(key, 5)
    base_key, image_key, column_key = jax.random.split(key, 3)
    position = jnp.arange(IMAGES, dtype=jnp.float32) / (IMAGES - 1)
    image_scale = jnp.exp((position - 0.5) * jnp.log(3.0) + jax.random.uniform(image_key, (IMAGES,), minval=-0.25, maxval=0.25))
    column_scale = jnp.exp(jax.random.uniform(column_key, (C,), minval=-0.5, maxval=0.5))
    base = jnp.clip(jax.random.normal(base_key, (IMAGES, ROWS_IMG, C)), -6.0, 6.0)
    values = base * image_scale[:, None, None] * column_scale[None, None, :]
    return values.reshape(IMAGES * ROWS_IMG, C).astype(jnp.bfloat16)


def block_levels(rng, dims, cuts, least, top_value):
    loudness, own = 1.0, jax.random.fold_in(rng, 6)
    for dim, blocks in cuts:
        steps = jnp.exp(jax.random.uniform(jax.random.fold_in(own, dim), (blocks,), jnp.float32, least / len(cuts), top_value / len(cuts)))
        loudness = loudness * jnp.repeat(steps, dims[dim] // blocks).reshape([-1 if axis == dim else 1 for axis in range(len(dims))])
    return loudness


def noise(key, extent, deviation, reach, pieces=(), kind=jnp.bfloat16):
    entries = deviation * jax.random.normal(key, extent, jnp.float32)
    if pieces:
        entries = entries * block_levels(key, extent, pieces, -0.22, 0.18)
    return jnp.clip(entries, -reach, reach).astype(kind)


def setup_inputs(seed: int = 0) -> dict:
    key_of = jax.random.split(jax.random.key(seed), 17)
    return {
        "pixels": draw_pixels(jax.random.fold_in(key_of[16], 71), 0),
        "crop_counts": draw_crop_counts(jax.random.fold_in(key_of[16], 71), 0),
        "first_weight": noise(key_of[2], (C, C), C ** -0.5, 0.125, ((1, 2),)),
        "first_gain": jnp.clip(1.0 + 0.1 * jax.random.normal(key_of[3], (C,), jnp.float32), 0.5, 1.5),
        "first_shift": noise(key_of[4], (C,), 0.3, 2.0, ((0, 2),), jnp.float32),
        "group_weight": noise(key_of[5], (3, 3, GROUP_WIDTH, C), (9 * GROUP_WIDTH) ** -0.5, 0.25, ((3, 2),)),
        "group_gain": jnp.clip(1.0 + 0.1 * jax.random.normal(key_of[6], (C,), jnp.float32), 0.5, 1.5),
        "group_shift": noise(key_of[7], (C,), 0.3, 2.0, ((0, 2),), jnp.float32),
        "squeeze_weight": noise(key_of[8], (C, SE_WIDTH), (C // 16) ** -0.5, 0.5, ((1, 2),), jnp.float32),
        "squeeze_bias": noise(key_of[9], (SE_WIDTH,), 0.5, 3.0, ((0, 2),), jnp.float32),
        "excite_weight": noise(key_of[10], (SE_WIDTH, C), (SE_WIDTH // 4) ** -0.5, 0.5, ((1, 2),), jnp.float32),
        "excite_bias": noise(key_of[11], (C,), 0.5, 3.0, ((0, 2),), jnp.float32),
        "last_weight": noise(key_of[12], (C, C), C ** -0.5, 0.125, ((1, 2),)),
        "last_gain": jnp.clip(1.0 + 0.1 * jax.random.normal(key_of[13], (C,), jnp.float32), 0.5, 1.5),
        "last_shift": noise(key_of[14], (C,), 0.3, 2.0, ((0, 2),), jnp.float32),
        "output_grad": noise(key_of[15], (IMAGES * ROWS_IMG, C), 1.0, 6.0, ((0, 16), (1, 2))),
    }


EPSILON = 1e-05
HIGHEST = lax.Precision.HIGHEST

@jax.custom_vjp
def low(v):
    return lax.optimization_barrier(v.astype(jnp.bfloat16)).astype(jnp.float32)

@jax.custom_vjp
def low_back(v):
    return v

def low_keep(v):
    return (low(v), None)

def low_pass(kept, grad):
    return (grad,)

def back_keep(v):
    return (v, None)

def back_low(kept, grad):
    return (low(grad),)
low.defvjp(low_keep, low_pass)
low_back.defvjp(back_keep, back_low)

def live_mask(image_counts):
    big_rows = BIG_CROPS * BIG_SIDE * BIG_SIDE
    places = jnp.arange(ROWS_IMG, dtype=jnp.int32)
    slot_index = (places - big_rows) // (SMALL_SIDE * SMALL_SIDE)
    living = (places[None, :] < big_rows) | (slot_index[None, :] < image_counts[:, None])
    return living.astype(jnp.float32).reshape(-1)

def split_crops(activation):
    channels = activation.shape[-1]
    per_image = activation.reshape(-1, ROWS_IMG, channels)
    big_rows = BIG_CROPS * BIG_SIDE * BIG_SIDE
    larger = per_image[:, :big_rows].reshape(-1, BIG_SIDE, BIG_SIDE, channels)
    smaller = per_image[:, big_rows:].reshape(-1, SMALL_SIDE, SMALL_SIDE, channels)
    return (larger, smaller)

def join_crops(larger, smaller, images):
    channels = larger.shape[-1]
    joined = jnp.concatenate([larger.reshape(images, -1, channels), smaller.reshape(images, -1, channels)], axis=1)
    return joined.reshape(-1, channels)

def group_conv(activation, kernel, images):
    outputs = []
    for crop_tiles in split_crops(activation):
        outputs.append(lax.conv_general_dilated(crop_tiles, kernel, (1, 1), ((1, 1), (1, 1)), dimension_numbers=('NHWC', 'HWIO', 'NHWC'), feature_group_count=GROUPS, precision=HIGHEST))
    return join_crops(outputs[0], outputs[1], images)

def batch_norm(values_in, norm_gain, norm_shift, row_mask, live_total):
    average = lax.optimization_barrier(jnp.sum(values_in * row_mask, axis=0)) / live_total
    centred = values_in - average
    variance = lax.optimization_barrier(jnp.sum(row_mask * centred * centred, axis=0)) / live_total
    return centred * lax.rsqrt(variance + EPSILON) * norm_gain + norm_shift

def reference(pixels, crop_counts, first_weight, first_gain, first_shift, group_weight, group_gain, group_shift, squeeze_weight, squeeze_bias, excite_weight, excite_bias, last_weight, last_gain, last_shift, output_grad):
    images = crop_counts.shape[0]
    row_mask = live_mask(crop_counts)[:, None]
    per_image = (BIG_CROPS * BIG_SIDE * BIG_SIDE + SMALL_SIDE * SMALL_SIDE * crop_counts).astype(jnp.float32)
    live_total = jnp.sum(per_image)
    image_mask = row_mask.reshape(images, ROWS_IMG, 1)

    def forward(source, weight_one, gain_one, shift_one, weight_group, gain_group, shift_group, squeeze_matrix, squeeze_offset, excite_matrix, excite_offset, weight_last, gain_last, shift_last):
        first_out = low_back(jnp.dot(source, weight_one, precision=HIGHEST))
        first_act = low(jax.nn.silu(batch_norm(first_out, gain_one, shift_one, row_mask, live_total)))
        group_out = low_back(group_conv(first_act, weight_group, images))
        group_act = jax.nn.silu(batch_norm(group_out, gain_group, shift_group, row_mask, live_total))
        by_image = group_act.reshape(images, ROWS_IMG, -1)
        pooled = lax.optimization_barrier(jnp.sum(by_image * image_mask, axis=1)) / per_image[:, None]
        squeezed = jax.nn.silu(jnp.dot(pooled, squeeze_matrix, precision=HIGHEST) + squeeze_offset)
        excited = jax.nn.sigmoid(jnp.dot(squeezed, excite_matrix, precision=HIGHEST) + excite_offset)
        scaled = low((by_image * excited[:, None, :]).reshape(images * ROWS_IMG, -1))
        last_out = low_back(jnp.dot(scaled, weight_last, precision=HIGHEST))
        merged = source + batch_norm(last_out, gain_last, shift_last, row_mask, live_total)
        return jax.nn.silu(merged) * row_mask
    floats = [member.astype(jnp.float32) for member in (pixels, first_weight, first_gain, first_shift, group_weight, group_gain, group_shift, squeeze_weight, squeeze_bias, excite_weight, excite_bias, last_weight, last_gain, last_shift)]
    result, pullback = jax.vjp(forward, *floats)
    grads = pullback(output_grad.astype(jnp.float32))
    return (result.astype(jnp.bfloat16), grads[0], grads[1], grads[2], grads[3], grads[4], grads[5], grads[6], grads[7], grads[8], grads[9], grads[10], grads[11], grads[12], grads[13])
```

```python
import functools

import jax
import jax.numpy as jnp
from jax import lax
from jax.experimental import pallas as pl
from jax.experimental.pallas import tpu as pltpu
from jax.sharding import PartitionSpec as P


GROUP_WIDTH = 56
ROWS_IMG = 188
BIG_ROWS = 98
IMGS = 8
ROWS = IMGS * ROWS_IMG
HALF = 1008
TILES = 8
LAST = HALF - 7 * 128
EPSILON = 1e-05
F32 = jnp.float32
BF16 = jnp.bfloat16
HIGHEST = lax.Precision.HIGHEST
MESH = pl.DeviceIdType.MESH
VMEM = pl.BlockSpec(memory_space=pltpu.VMEM)
ANY = pl.BlockSpec(memory_space=pl.ANY)
VMEM_LIMIT = 60 * 1024 * 1024
SPANS = ((0, 256), (256, 512), (512, 768), (768, 1008))
WINDOWS = ((0, 3), (1, 5), (3, 7), (5, 8))
BIG_PAD = 73 * 16
PAD_ROWS = BIG_PAD + 21 * 80
TAPS = tuple((dy, dx) for dy in (-1, 0, 1) for dx in (-1, 0, 1))
DMA = pltpu.SemaphoreType.DMA


def big_place(y, x):
    return (1 + (y + 1) * 8 + x) * 16


def small_place(y, x):
    return BIG_PAD + (1 + (y + 1) * 4 + x) * 80


def natural_row(tile):
    if tile < BIG_ROWS:
        return (tile % 2) * 49 + tile // 2
    tile = tile - BIG_ROWS
    return BIG_ROWS + (tile % 10) * 9 + tile // 10


def padded_row(tile):
    if tile < BIG_ROWS:
        pixel = tile // 2
        return big_place(pixel // 7, pixel % 7) + (tile % 2) * 8
    tile = tile - BIG_ROWS
    pixel = tile // 10
    return small_place(pixel // 3, pixel % 3) + (tile % 10) * 8


REAL_ROWS = frozenset(padded_row(tile) for tile in range(0, ROWS_IMG, 2))
ZERO_ROWS = tuple(row for row in range(0, PAD_ROWS, 16) if row not in REAL_ROWS)


def sigmoid(v):
    return 0.5 + 0.5 * jnp.tanh(0.5 * v)


def slope_of(v, s):
    return s * (1.0 + v * (1.0 - s))


def dot(a, b, dims=((1,), (0,)), **kw):
    return lax.dot_general(a, b, (dims, ((), ())), preferred_element_type=F32, **kw)


def for_each(count, step):
    if count <= 16:
        for index in range(count):
            step(index)
    else:
        lax.fori_loop(0, count, lambda index, _: (step(index), 0)[1], 0)


def for_tiles(step):
    lax.fori_loop(0, TILES, lambda j, _: (step(j), 0)[1], 0)


def for_ragged_tiles(step):
    def full(j, _):
        step(j, pl.ds(pl.multiple_of(j * 128, 128), 128), 128)
        return 0

    lax.fori_loop(0, TILES - 1, full, 0)
    step(TILES - 1, pl.ds(7 * 128, LAST), LAST)


def greet(n, all_images=True, partner=True):
    barrier = pltpu.get_barrier_semaphore()
    me = lax.axis_index("img")
    count = 0
    if all_images:
        for_each(
            n - 1,
            lambda d: pl.semaphore_signal(
                barrier, 1, device_id={"img": lax.rem(me + d + 1, n)}, device_id_type=MESH
            ),
        )
        count += n - 1
    if partner:
        pl.semaphore_signal(
            barrier, 1, device_id={"ch": 1 - lax.axis_index("ch")}, device_id_type=MESH
        )
        count += 1
    return lambda: pl.semaphore_wait(barrier, count)


class Gather:
    def __init__(self, n, source, target, send, recv):
        self.n, self.source, self.target, self.send, self.recv = n, source, target, send, recv
        self.me = lax.axis_index("img")

    def copy(self, d):
        return pltpu.make_async_remote_copy(
            src_ref=self.source,
            dst_ref=self.target.at[self.me],
            send_sem=self.send.at[d],
            recv_sem=self.recv.at[d],
            device_id={"img": lax.rem(self.me + d + 1, self.n)},
            device_id_type=MESH,
        )

    def start(self):
        for_each(self.n - 1, lambda d: self.copy(d).start())
        self.target[self.me] = self.source[...]

    def wait(self):
        for_each(self.n - 1, lambda d: self.copy(d).wait())


def swap(source, target, send, recv):
    return pltpu.make_async_remote_copy(
        src_ref=source,
        dst_ref=target,
        send_sem=send,
        recv_sem=recv,
        device_id={"ch": 1 - lax.axis_index("ch")},
        device_id_type=MESH,
    )


def put_span(ref, span, rows, value, add=False):
    left, right = value[:, :128], value[:, 128:]
    width = right.shape[1]
    if add:
        ref[2 * span, rows, :] += left
        ref[2 * span + 1, rows, 0:width] += right
    else:
        ref[2 * span, rows, :] = left
        ref[2 * span + 1, rows, 0:width] = right


def norm_constants(n, stats, live, gain_shift, consts):
    def total(step):
        return lax.fori_loop(0, n, lambda i, acc: acc + step(i), jnp.zeros((TILES, 128), F32))

    number = total(lambda i: live[i])
    average = total(lambda i: live[i] * stats[i, 0]) / number

    def centred(i):
        off = stats[i, 0] - average
        return stats[i, 1] + live[i] * off * off

    variance = total(centred) / number
    consts[0] = average
    consts[1] = lax.rsqrt(variance + EPSILON)
    consts[2] = gain_shift[0]
    consts[3] = gain_shift[1]
    consts[4] = number


def back_constants(n, sums, consts, grads):
    shift_grad = lax.fori_loop(
        0, n, lambda i, acc: acc + sums[i, 0], jnp.zeros((TILES, 128), F32)
    )
    gain_grad = lax.fori_loop(
        0, n, lambda i, acc: acc + sums[i, 1], jnp.zeros((TILES, 128), F32)
    )
    grads[0] = gain_grad
    grads[1] = shift_grad
    consts[5] = shift_grad / consts[4]
    consts[6] = gain_grad / consts[4]
    consts[7] = consts[1] * consts[2]


def row_of(consts, k, j):
    return consts[k, pl.ds(j, 1), :]


def natural_stats(ref, mask, count, local):
    def step(j):
        x = ref[j]
        m = mask[...]
        average = jnp.sum(x * m, axis=0, keepdims=True) / count
        off = x - average
        local[0, pl.ds(j, 1), :] = average
        local[1, pl.ds(j, 1), :] = jnp.sum(m * off * off, axis=0, keepdims=True)

    for_tiles(step)


def crop_sum(value, mask10):
    big = jnp.sum(value[:BIG_ROWS], axis=0)
    small = jnp.sum(value[BIG_ROWS:].reshape(9, 10, IMGS, 128), axis=0)
    return big + jnp.sum(small * mask10[...], axis=0)


def crop_stats(ref, mask10, count, local):
    def step(j):
        x = ref[j].reshape(ROWS_IMG, IMGS, 128)
        average = jnp.sum(crop_sum(x, mask10), axis=0, keepdims=True) / count
        off = x - average[None]
        local[0, pl.ds(j, 1), :] = average
        local[1, pl.ds(j, 1), :] = jnp.sum(crop_sum(off * off, mask10), axis=0, keepdims=True)

    for_tiles(step)


def window(ref, tiles, dy, dx, big):
    pieces = []
    for y in range(7 if big else 3):
        start = big_place(y + dy, dx) if big else small_place(y + dy, dx)
        rows = slice(start, start + (112 if big else 240))
        pieces.append(jnp.concatenate([ref[t, rows, :] for t in tiles], axis=1))
    return jnp.concatenate(pieces, axis=0)


def build_bands(kernel, bands):
    for span, (first, end) in enumerate(WINDOWS):
        base = first * 128
        depth = (end - first) * 128
        lane = lax.broadcasted_iota(jnp.int32, (GROUP_WIDTH, 256), 1) + span * 256
        groups = range(span * 256 // GROUP_WIDTH, min(18, (span * 256 + 255) // GROUP_WIDTH + 1))
        masks = [
            (lane >= g * GROUP_WIDTH) & (lane < (g + 1) * GROUP_WIDTH) for g in groups
        ]
        head = groups[0] * GROUP_WIDTH - base
        tail = depth - head - len(groups) * GROUP_WIDTH
        for tap in range(9):
            piece = kernel[
                tap * GROUP_WIDTH : (tap + 1) * GROUP_WIDTH, span * 256 : span * 256 + 256
            ]
            parts = [jnp.where(m, piece, 0.0) for m in masks]
            if head:
                parts.insert(0, jnp.zeros((head, 256), F32))
            if tail:
                parts.append(jnp.zeros((tail, 256), F32))
            bands[span][:, tap * 256 : tap * 256 + 256] = jnp.concatenate(parts, axis=0).astype(
                BF16
            )


def zero_pads(ref, j):
    for row in ZERO_ROWS:
        ref[j, row : row + 16, :] = jnp.zeros((16, 128), BF16)


def first_kernel(
    n, count, pixels, weight, mask, first, other, stats, local, swap_s, swap_r, send, recv
):
    ch = lax.axis_index("ch")
    wait_all = greet(n)
    own = pl.multiple_of(ch * HALF, 16)
    far = pl.multiple_of((1 - ch) * HALF, 16)
    wait_all()
    chunks = ((0, 384), (384, 384), (768, 384), (1152, 352))
    swaps = []
    for k, (start, size) in enumerate(chunks):
        rows = pl.ds(start, size)
        swaps.append(swap(pixels.at[rows], other.at[rows], swap_s.at[k], swap_r.at[k]))
        swaps[-1].start()
    first[7, :, LAST:128] = jnp.zeros((ROWS, 128 - LAST), F32)
    for t, (a, b) in enumerate(SPANS):
        put_span(first, t, slice(0, ROWS), dot(pixels[...], weight[pl.ds(own, HALF), a:b]))
    for k, (start, size) in enumerate(chunks):
        swaps[k].wait()
        rows = slice(start, start + size)
        for t, (a, b) in enumerate(SPANS):
            put_span(first, t, rows, dot(other[rows, :], weight[pl.ds(far, HALF), a:b]), add=True)
    natural_stats(first, mask, count[0, 0], local)
    gather = Gather(n, local, stats, send, recv)
    gather.start()
    gather.wait()


def group_kernel(
    n,
    count,
    first,
    stats1,
    live,
    norm1,
    mask10,
    kernel,
    weight1,
    weight3,
    padded,
    group,
    stats2,
    far1,
    far3,
    consts,
    local,
    band0,
    band1,
    band2,
    band3,
    swap_s,
    swap_r,
    send,
    recv,
):
    wait_all = greet(n)
    norm_constants(n, stats1, live, norm1, consts)
    wait_all()
    far = pl.multiple_of((1 - lax.axis_index("ch")) * HALF, 16)
    swaps = [
        swap(w.at[pl.ds(far, HALF)], f, swap_s.at[k], swap_r.at[k])
        for k, (w, f) in enumerate(((weight1, far1), (weight3, far3)))
    ]
    for s in swaps:
        s.start()
    bands = (band0, band1, band2, band3)
    build_bands(kernel, bands)

    def step(j):
        average = row_of(consts, 0, j)
        scale = row_of(consts, 1, j) * row_of(consts, 2, j)
        shift = row_of(consts, 3, j)
        zero_pads(padded, j)
        for tile in range(0, ROWS_IMG, 2):
            both = []
            for half in range(2):
                x = first[j, pl.ds(natural_row(tile + half), IMGS, stride=ROWS_IMG), :]
                pre = (x - average) * scale + shift
                both.append(pre * sigmoid(pre))
            row = padded_row(tile)
            padded[j, row : row + 16, :] = jnp.concatenate(both, axis=0).astype(BF16)

    for_tiles(step)
    for span, (start, end) in enumerate(WINDOWS):
        tiles = range(start, end)
        right = jnp.concatenate(
            [bands[span][:, tap * 256 : tap * 256 + 256] for tap in range(9)], axis=0
        )
        for big in (True, False):
            left = jnp.concatenate([window(padded, tiles, dy, dx, big) for dy, dx in TAPS], axis=1)
            rows = slice(0, 784) if big else slice(784, ROWS)
            put_span(group, span, rows, dot(left, right))
    crop_stats(group, mask10, count[0, 0], local)
    gather = Gather(n, local, stats2, send, recv)
    gather.start()
    for s in swaps:
        s.wait()
    gather.wait()


def gate_kernel(
    n,
    count,
    group,
    stats2,
    live,
    norm2,
    mask10,
    inverse,
    squeeze_w,
    squeeze_b,
    excite_w,
    excite_b,
    mask,
    weight,
    scaled,
    scaled_far,
    last,
    stats3,
    pooled,
    pooled_far,
    squeezed,
    squeezed_far,
    squeeze_pre,
    excited,
    consts,
    local,
    act,
    turned,
    swap_s,
    swap_r,
    small_s,
    small_r,
    send,
    recv,
):
    ch = lax.axis_index("ch")
    wait_all = greet(n)
    norm_constants(n, stats2, live, norm2, consts)

    def activate(j):
        average = row_of(consts, 0, j)
        scale = row_of(consts, 1, j) * row_of(consts, 2, j)
        pre = (group[j] - average) * scale + row_of(consts, 3, j)
        value = pre * sigmoid(pre)
        act[j] = value
        pooled[j] = crop_sum(value.reshape(ROWS_IMG, IMGS, 128), mask10) * inverse[...]

    for_tiles(activate)
    wait_all()
    pool_swap = swap(pooled, pooled_far, small_s.at[0], small_r.at[0])
    pool_swap.start()
    pool_swap.wait()
    mine = jnp.concatenate([pooled[j] for j in range(TILES)], axis=1)[:, :HALF]
    theirs = jnp.concatenate([pooled_far[j] for j in range(TILES)], axis=1)[:, :HALF]
    is_low = ch == 0
    pre = (
        dot(jnp.where(is_low, mine, theirs), squeeze_w[0:HALF, :], precision=HIGHEST)
        + dot(jnp.where(is_low, theirs, mine), squeeze_w[HALF:, :], precision=HIGHEST)
        + squeeze_b[...]
    )
    squeeze_pre[...] = pre
    squeezed[...] = pre * sigmoid(pre)
    squeeze_swap = swap(squeezed, squeezed_far, small_s.at[1], small_r.at[1])
    squeeze_swap.start()
    squeeze_swap.wait()
    mine, theirs = squeezed[...], squeezed_far[...]
    width = mine.shape[1]
    gate = sigmoid(
        dot(jnp.where(is_low, mine, theirs), excite_w[0:width, :], precision=HIGHEST)
        + dot(jnp.where(is_low, theirs, mine), excite_w[width:, :], precision=HIGHEST)
        + excite_b[...]
    )
    excited[7] = jnp.zeros((IMGS, 128), F32)
    for j in range(TILES - 1):
        excited[j] = gate[:, j * 128 : j * 128 + 128]
    excited[7, :, 0:LAST] = gate[:, 7 * 128 :]

    def apply(j):
        gate_j = excited[j]
        for tile in range(ROWS_IMG):
            turned[pl.ds(natural_row(tile), IMGS, stride=ROWS_IMG), :] = (
                act[j, tile * 8 : tile * 8 + 8, :] * gate_j
            )
        scaled[j] = turned[...].astype(BF16)
        swap(scaled.at[j], scaled_far.at[j], swap_s.at[j], swap_r.at[j]).start()

    for_tiles(apply)
    own = pl.multiple_of(ch * HALF, 16)
    far = pl.multiple_of((1 - ch) * HALF, 16)
    last[7, :, LAST:128] = jnp.zeros((ROWS, 128 - LAST), F32)
    for t, (a, b) in enumerate(SPANS):
        left = jnp.concatenate([scaled[j] for j in range(TILES)], axis=1)[:, :HALF]
        put_span(last, t, slice(0, ROWS), dot(left, weight[pl.ds(own, HALF), a:b]))
    for_tiles(lambda j: swap(scaled.at[j], scaled_far.at[j], swap_s.at[j], swap_r.at[j]).wait())
    for t, (a, b) in enumerate(SPANS):
        left = jnp.concatenate([scaled_far[j] for j in range(TILES)], axis=1)[:, :HALF]
        put_span(last, t, slice(0, ROWS), dot(left, weight[pl.ds(far, HALF), a:b]), add=True)
    natural_stats(last, mask, count[0, 0], local)
    gather = Gather(n, local, stats3, send, recv)
    gather.start()
    gather.wait()


def merge_kernel(
    n, last, stats3, live, norm3, mask, pixels, output_grad, block, merged_grad, sums3, consts, local, send, recv
):
    wait_all = greet(n, partner=False)
    norm_constants(n, stats3, live, norm3, consts)
    merged_grad[7, :, LAST:128] = jnp.zeros((ROWS, 128 - LAST), F32)
    local[...] = jnp.zeros_like(local)

    def step(j, lanes, width):
        def vec(k):
            return consts[k, pl.ds(j, 1), 0:width]

        m = mask[:, 0:width]
        normed = (last[j, :, 0:width] - vec(0)) * vec(1)
        merged = pixels[:, lanes].astype(F32) + normed * vec(2) + vec(3)
        s = sigmoid(merged)
        block[:, lanes] = (merged * s * m).astype(BF16)
        grad = output_grad[:, lanes].astype(F32) * m * slope_of(merged, s)
        merged_grad[j, :, 0:width] = grad
        local[0, pl.ds(j, 1), 0:width] = jnp.sum(grad, axis=0, keepdims=True)
        local[1, pl.ds(j, 1), 0:width] = jnp.sum(grad * normed, axis=0, keepdims=True)

    for_ragged_tiles(step)
    wait_all()
    gather = Gather(n, local, sums3, send, recv)
    gather.start()
    gather.wait()


def weight_grad(left_tiles, right_tiles, target):
    for a, b in SPANS:
        tiles = range(a // 128, (b + 127) // 128)
        left = jnp.concatenate([left_tiles(t) for t in tiles], axis=1)[:, : b - a]
        for span in range(4):
            right = jnp.concatenate([right_tiles(2 * span), right_tiles(2 * span + 1)], axis=1)
            value = dot(left, right, ((0,), (0,))).astype(BF16)
            target[2 * span, a:b, :] = value[:, :128]
            target[2 * span + 1, a:b, :] = value[:, 128:]


def last_grad_kernel(
    n,
    last,
    stats3,
    live,
    norm3,
    sums3,
    mask,
    merged_grad,
    scaled,
    scaled_far,
    weight,
    weight_far,
    grad_own,
    grad_far,
    scaled_grad,
    vectors,
    consts,
    low,
    low_far,
    swap_s,
    swap_r,
):
    ch = lax.axis_index("ch")
    wait_partner = greet(n, all_images=False)
    norm_constants(n, stats3, live, norm3, consts)
    back_constants(n, sums3, consts, vectors)
    wait_partner()

    def step(j):
        normed = (last[j] - row_of(consts, 0, j)) * row_of(consts, 1, j)
        inner = merged_grad[j] - row_of(consts, 5, j) - normed * row_of(consts, 6, j)
        low[j] = (mask[...] * row_of(consts, 7, j) * inner).astype(BF16)
        swap(low.at[j], low_far.at[j], swap_s.at[j], swap_r.at[j]).start()

    for_tiles(step)
    weight_grad(lambda t: scaled[t], lambda t: low[t], grad_own)
    weight_grad(lambda t: scaled_far[t], lambda t: low[t], grad_far)
    own = pl.multiple_of(ch * HALF, 16)
    scaled_grad[7, :, LAST:128] = jnp.zeros((ROWS, 128 - LAST), F32)
    for t, (a, b) in enumerate(SPANS):
        left = jnp.concatenate([low[j] for j in range(TILES)], axis=1)[:, :HALF]
        right = weight[pl.ds(own + a, b - a), :]
        put_span(scaled_grad, t, slice(0, ROWS), dot(left, right, ((1,), (1,))))
    for_tiles(lambda j: swap(low.at[j], low_far.at[j], swap_s.at[j], swap_r.at[j]).wait())
    for t, (a, b) in enumerate(SPANS):
        left = jnp.concatenate([low_far[j] for j in range(TILES)], axis=1)[:, :HALF]
        put_span(
            scaled_grad,
            t,
            slice(0, ROWS),
            dot(left, weight_far[a:b, :], ((1,), (1,))),
            add=True,
        )


def gate_grad_kernel(
    n,
    scaled_grad,
    group,
    stats2,
    live,
    norm2,
    mask10,
    inverse,
    excited,
    squeeze_pre,
    squeeze_w,
    excite_w,
    pre_grad,
    sums2,
    excite_grad,
    squeeze_grad,
    consts,
    local,
    terms,
    terms_in,
    pool_terms,
    pool_in,
    pool_tiles,
    small_s,
    small_r,
    send,
    recv,
):
    ch = lax.axis_index("ch")
    wait_all = greet(n)
    norm_constants(n, stats2, live, norm2, consts)

    def gate_sum(j):
        average = row_of(consts, 0, j)
        scale = row_of(consts, 1, j) * row_of(consts, 2, j)
        shift = row_of(consts, 3, j)
        total = jnp.zeros((IMGS, 128), F32)
        for tile in range(ROWS_IMG):
            pre = (group[j, tile * 8 : tile * 8 + 8, :] - average) * scale + shift
            act = pre * sigmoid(pre)
            total = total + act * scaled_grad[j, pl.ds(natural_row(tile), IMGS, stride=ROWS_IMG), :]
        gate = excited[j]
        excite_grad[j] = total * gate * (1.0 - gate)

    for_tiles(gate_sum)
    wide = jnp.concatenate([excite_grad[j] for j in range(TILES)], axis=1)[:, :HALF]
    width = squeeze_w.shape[1]
    is_low = ch == 0
    part0 = dot(wide, excite_w[0:width, :], ((1,), (1,)), precision=HIGHEST)
    part1 = dot(wide, excite_w[width:, :], ((1,), (1,)), precision=HIGHEST)
    terms[...] = jnp.where(is_low, part1, part0)
    wait_all()
    term_swap = swap(terms, terms_in, small_s.at[0], small_r.at[0])
    term_swap.start()
    term_swap.wait()
    pre = squeeze_pre[...]
    grad = (jnp.where(is_low, part0, part1) + terms_in[...]) * slope_of(pre, sigmoid(pre))
    squeeze_grad[...] = grad
    pool0 = dot(grad, squeeze_w[0:HALF, :], ((1,), (1,)), precision=HIGHEST)
    pool1 = dot(grad, squeeze_w[HALF:, :], ((1,), (1,)), precision=HIGHEST)
    pool_terms[...] = jnp.where(is_low, pool1, pool0)
    pool_swap = swap(pool_terms, pool_in, small_s.at[1], small_r.at[1])
    pool_swap.start()
    pool_swap.wait()
    pool = jnp.where(is_low, pool0, pool1) + pool_in[...]
    for j in range(TILES):
        part = pool[:, j * 128 : min(HALF, j * 128 + 128)]
        pool_tiles[j, :, 0 : part.shape[1]] = part * inverse[:, 0 : part.shape[1]]

    def grads(j):
        average, scale = row_of(consts, 0, j), row_of(consts, 1, j)
        gain, shift = row_of(consts, 2, j), row_of(consts, 3, j)
        gate, pooled = excited[j], pool_tiles[j]
        total = jnp.zeros((IMGS, 128), F32)
        total_normed = jnp.zeros((IMGS, 128), F32)
        for tile in range(ROWS_IMG):
            rows = slice(tile * 8, tile * 8 + 8)
            normed = (group[j, rows, :] - average) * scale
            pre = normed * gain + shift
            lead = pooled if tile < BIG_ROWS else pooled * mask10[(tile - BIG_ROWS) % 10]
            act = scaled_grad[j, pl.ds(natural_row(tile), IMGS, stride=ROWS_IMG), :] * gate + lead
            grad = act * slope_of(pre, sigmoid(pre))
            pre_grad[j, rows, :] = grad
            total = total + grad
            total_normed = total_normed + grad * normed
        local[0, pl.ds(j, 1), :] = jnp.sum(total, axis=0, keepdims=True)
        local[1, pl.ds(j, 1), :] = jnp.sum(total_normed, axis=0, keepdims=True)

    pool_tiles[7, :, LAST:128] = jnp.zeros((IMGS, 128 - LAST), F32)
    for_tiles(grads)
    gather = Gather(n, local, sums2, send, recv)
    gather.start()
    gather.wait()


def group_grad_kernel(
    n,
    pre_grad,
    group,
    stats2,
    live,
    norm2,
    sums2,
    mask10,
    kernel,
    padded,
    first,
    stats1,
    norm1,
    kernel_grad,
    first_pre_grad,
    sums1,
    vectors,
    consts,
    consts1,
    local,
    padded_grad,
    band0,
    band1,
    band2,
    band3,
    full,
    send,
    recv,
):
    wait_all = greet(n, partner=False)
    norm_constants(n, stats2, live, norm2, consts)
    back_constants(n, sums2, consts, vectors)
    norm_constants(n, stats1, live, norm1, consts1)
    bands = (band0, band1, band2, band3)
    build_bands(kernel, bands)

    def step(j):
        average, scale = row_of(consts, 0, j), row_of(consts, 1, j)
        less, slope, front = row_of(consts, 5, j), row_of(consts, 6, j), row_of(consts, 7, j)
        zero_pads(padded_grad, j)
        for tile in range(0, ROWS_IMG, 2):
            both = []
            for half in range(2):
                rows = slice(tile * 8 + half * 8, tile * 8 + half * 8 + 8)
                normed = (group[j, rows, :] - average) * scale
                grad = front * (pre_grad[j, rows, :] - less - normed * slope)
                if tile >= BIG_ROWS:
                    grad = grad * mask10[(tile + half - BIG_ROWS) % 10]
                both.append(grad)
            row = padded_row(tile)
            padded_grad[j, row : row + 16, :] = jnp.concatenate(both, axis=0).astype(BF16)

    for_tiles(step)
    started = 0
    for span, (start, end) in enumerate(WINDOWS):
        tiles = (2 * span, 2 * span + 1)
        shifted = [
            jnp.concatenate([window(padded_grad, tiles, -dy, -dx, big) for dy, dx in TAPS], axis=1)
            for big in (True, False)
        ]
        for rows, left in ((slice(0, 784), shifted[0]), (slice(784, ROWS), shifted[1])):
            value = dot(left, bands[span][...], ((1,), (1,)))
            for t in range(start, end):
                part = value[:, (t - start) * 128 : (t - start) * 128 + 128]
                if t < started:
                    first_pre_grad[t, rows, :] += part
                else:
                    first_pre_grad[t, rows, :] = part
        started = end
        right = jnp.concatenate(shifted, axis=0)
        for t in range(start, end, 2):
            pair = range(t, min(t + 2, end))
            left = jnp.concatenate([window(padded, pair, 0, 0, big) for big in (True, False)], axis=0)
            base = (t - start) * 128
            full[base : base + 128 * len(pair), :] = dot(left, right, ((0,), (0,)))
        lane = lax.broadcasted_iota(jnp.int32, (GROUP_WIDTH, 256), 1) + span * 256
        pieces = []
        for tap in range(9):
            piece = jnp.zeros((GROUP_WIDTH, 256), F32)
            for g in range(span * 256 // GROUP_WIDTH, min(18, (span * 256 + 255) // GROUP_WIDTH + 1)):
                row = g * GROUP_WIDTH - start * 128
                inside = (lane >= g * GROUP_WIDTH) & (lane < (g + 1) * GROUP_WIDTH)
                block = full[row : row + GROUP_WIDTH, tap * 256 : tap * 256 + 256]
                piece = jnp.where(inside, block, piece)
            pieces.append(piece)
        pieces.append(jnp.zeros((8, 256), F32))
        value = jnp.concatenate(pieces, axis=0).astype(BF16)
        kernel_grad[2 * span] = value[:, :128]
        kernel_grad[2 * span + 1] = value[:, 128:]

    def slopes(j):
        average, scale = row_of(consts1, 0, j), row_of(consts1, 1, j)
        gain, shift = row_of(consts1, 2, j), row_of(consts1, 3, j)
        total = jnp.zeros((IMGS, 128), F32)
        total_normed = jnp.zeros((IMGS, 128), F32)
        for tile in range(ROWS_IMG):
            rows = slice(tile * 8, tile * 8 + 8)
            x = first[j, pl.ds(natural_row(tile), IMGS, stride=ROWS_IMG), :]
            normed = (x - average) * scale
            pre = normed * gain + shift
            grad = first_pre_grad[j, rows, :] * slope_of(pre, sigmoid(pre))
            if tile >= BIG_ROWS:
                grad = grad * mask10[(tile - BIG_ROWS) % 10]
            first_pre_grad[j, rows, :] = grad
            total = total + grad
            total_normed = total_normed + grad * normed
        local[0, pl.ds(j, 1), :] = jnp.sum(total, axis=0, keepdims=True)
        local[1, pl.ds(j, 1), :] = jnp.sum(total_normed, axis=0, keepdims=True)

    for_tiles(slopes)
    wait_all()
    gather = Gather(n, local, sums1, send, recv)
    gather.start()
    gather.wait()


def first_grad_kernel(
    n,
    pre_grad,
    first,
    stats1,
    live,
    norm1,
    sums1,
    mask10,
    pixels,
    pixels_far,
    weight,
    weight_far,
    merged_grad,
    grad_own,
    grad_far,
    pixels_grad,
    vectors,
    consts,
    low,
    low_far,
    turned,
    swap_s,
    swap_r,
):
    ch = lax.axis_index("ch")
    wait_partner = greet(n, all_images=False)
    norm_constants(n, stats1, live, norm1, consts)
    back_constants(n, sums1, consts, vectors)
    wait_partner()

    def step(j):
        average, scale = row_of(consts, 0, j), row_of(consts, 1, j)
        less, slope, front = row_of(consts, 5, j), row_of(consts, 6, j), row_of(consts, 7, j)
        for tile in range(ROWS_IMG):
            there = pl.ds(natural_row(tile), IMGS, stride=ROWS_IMG)
            normed = (first[j, there, :] - average) * scale
            grad = front * (pre_grad[j, tile * 8 : tile * 8 + 8, :] - less - normed * slope)
            if tile >= BIG_ROWS:
                grad = grad * mask10[(tile - BIG_ROWS) % 10]
            turned[there, :] = grad
        low[j] = turned[...].astype(BF16)
        swap(low.at[j], low_far.at[j], swap_s.at[j], swap_r.at[j]).start()

    for_tiles(step)
    weight_grad(lambda t: pixels[:, t * 128 : min(HALF, t * 128 + 128)], lambda t: low[t], grad_own)
    weight_grad(
        lambda t: pixels_far[:, t * 128 : min(HALF, t * 128 + 128)], lambda t: low[t], grad_far
    )
    own = pl.multiple_of(ch * HALF, 16)
    for t, (a, b) in enumerate(SPANS):
        left = jnp.concatenate([low[j] for j in range(TILES)], axis=1)[:, :HALF]
        value = dot(left, weight[pl.ds(own + a, b - a), :], ((1,), (1,)))
        more = jnp.concatenate([merged_grad[2 * t], merged_grad[2 * t + 1]], axis=1)[:, : b - a]
        pixels_grad[:, a:b] = value + more
    for_tiles(lambda j: swap(low.at[j], low_far.at[j], swap_s.at[j], swap_r.at[j]).wait())
    for t, (a, b) in enumerate(SPANS):
        left = jnp.concatenate([low_far[j] for j in range(TILES)], axis=1)[:, :HALF]
        pixels_grad[:, a:b] += dot(left, weight_far[a:b, :], ((1,), (1,)))


def image_axes(n):
    return {16: (2, 2, 4), 128: (8, 4, 4)}.get(n, (n, 1, 1))


class Part:
    def __init__(self, n, order, source, result, room, sems):
        sizes = image_axes(n)
        strides = (1, sizes[0], sizes[0] * sizes[1])
        self.n, self.me = n, lax.axis_index("img")
        self.sizes = [sizes[a] for a in order]
        self.strides = [strides[a] for a in order]
        self.place = [lax.rem(self.me // s, e) for s, e in zip(self.strides, self.sizes)]
        self.source, self.result, self.room, self.sems = source, result, room, sems
        self.reduces = source is not None
        self.live = []

    def send(self, axis, stage, source, target):
        for d in range(1, self.sizes[axis]):
            q = lax.rem(self.place[axis] + d, self.sizes[axis])
            peer = self.me + (q - self.place[axis]) * self.strides[axis]
            copy = pltpu.make_async_remote_copy(
                src_ref=source(q),
                dst_ref=target(d),
                send_sem=self.sems[0].at[stage, d],
                recv_sem=self.sems[1].at[stage, d],
                device_id={"img": peer},
                device_id_type=MESH,
            )
            copy.start()
            self.live.append(copy)

    def settle(self):
        for copy in self.live:
            copy.wait()
        self.live = []

    def add(self, target, own, arrived, count):
        total = own[...].astype(F32)
        for d in range(1, count):
            total = total + arrived[d - 1][...].astype(F32)
        target[...] = total.astype(BF16)

    def step(self, stage):
        r0, r1, r2, a0, a1 = self.room if self.reduces else (None,) * 5
        p0, p1, p2 = self.place
        if stage == 0 and self.reduces:
            self.send(0, 0, lambda q: self.source.at[q], lambda d: r0.at[d - 1])
        elif stage == 1 and self.reduces:
            self.settle()
            for k in range(self.sizes[1]):
                self.add(
                    a0.at[k], self.source.at[p0, k], [r0.at[d, k] for d in range(self.sizes[0] - 1)], self.sizes[0]
                )
            self.send(1, 1, lambda q: a0.at[q], lambda d: r1.at[d - 1])
        elif stage == 2 and self.reduces:
            self.settle()
            self.add(a1, a0.at[p1], [r1.at[d] for d in range(self.sizes[1] - 1)], self.sizes[1])
            self.send(2, 2, lambda q: a1.at[q], lambda d: r2.at[d - 1])
        elif stage == 3:
            if self.reduces:
                self.settle()
                self.add(
                    self.result.at[p0, p1, p2], a1.at[p2], [r2.at[d] for d in range(self.sizes[2] - 1)], self.sizes[2]
                )
            block = self.result.at[p0, p1, p2]
            self.send(2, 3, lambda q: block, lambda d: block)
        elif stage == 4:
            self.settle()
            block = self.result.at[p0, p1]
            self.send(1, 4, lambda q: block, lambda d: block)
        elif stage == 5:
            self.settle()
            block = self.result.at[p0]
            self.send(0, 5, lambda q: block, lambda d: block)
        elif stage == 6:
            self.settle()

    @staticmethod
    def scratch(n, order, shape, reduces):
        sizes = [image_axes(n)[a] for a in order]
        most = max(sizes)
        sems = [DMA((6, most)), DMA((6, most))]
        if not reduces:
            return sems
        e0, e1, e2, rows, lanes = shape
        room = [
            (max(e0 - 1, 1), e1, e2, rows, lanes),
            (max(e1 - 1, 1), e2, rows, lanes),
            (max(e2 - 1, 1), rows, lanes),
            (e1, e2, rows, lanes),
            (e2, rows, lanes),
        ]
        return [pltpu.VMEM(s, BF16) for s in room] + sems


def settle_kernel(n, orders, reduces, *refs):
    count = len(orders)
    sources, refs = refs[:count], refs[count:]
    results, refs = refs[:count], refs[count:]
    wait_all = greet(n, partner=False)
    parts = []
    for order, reduce, source, result in zip(orders, reduces, sources, results):
        size = 7 if reduce else 2
        own, refs = refs[:size], refs[size:]
        part = Part(n, order, source if reduce else None, result, own[:5], own[-2:])
        if not reduce:
            p0, p1, p2 = part.place
            result[p0, p1, p2] = source[...]
        parts.append(part)
    wait_all()
    ticks = 7 + (count + 1) // 2
    for tick in range(ticks):
        for k, part in enumerate(parts):
            stage = tick - k // 2
            if 0 <= stage <= 6:
                part.step(stage)


def spread_kernel(own, far, out):
    ch = lax.axis_index("ch")
    for source, place in ((own, ch), (far, 1 - ch)):
        rows = pl.ds(pl.multiple_of(place * HALF, 8), HALF)
        for j in range(TILES):
            width = 128 if j < 7 else LAST
            out[rows, j * 128 : j * 128 + width] = source[j, 0:HALF, 0:width].astype(F32)


def finish_kernel(low_half, high_half, factors, group_out, squeeze_w, squeeze_b, excite_w, excite_b):
    ch = lax.axis_index("ch")
    se = squeeze_w.shape[1]
    split = low_half.shape[1]
    for j in range(TILES):
        width = 128 if j < 7 else LAST
        lanes = slice(j * 128, j * 128 + width)
        group_out[0:split, lanes] = low_half[j, :, 0:width].astype(F32)
        rest = 9 * GROUP_WIDTH - split
        group_out[split:, lanes] = high_half[j, :, 0:width].astype(F32)[:rest]
    n = factors.shape[0]
    whole = factors[...].astype(F32).reshape(n, -1, IMGS, 128)

    def columns(start, tiles, width):
        parts = [whole[:, t].reshape(n * IMGS, 128) for t in range(start, start + tiles)]
        return jnp.concatenate(parts, axis=1)[:, :width]

    excite_all, squeeze_all = columns(16, 8, HALF), columns(28, 2, se)
    squeeze_b[...] = jnp.sum(squeeze_all, axis=0, keepdims=True)
    excite_b[...] = jnp.sum(excite_all, axis=0, keepdims=True)
    excite_all, squeeze_all = excite_all.astype(BF16), squeeze_all.astype(BF16)
    for start, place in ((0, ch), (8, 1 - ch)):
        rows = pl.ds(pl.multiple_of(place * HALF, 8), HALF)
        squeeze_w[rows, :] = dot(columns(start, 8, HALF).astype(BF16), squeeze_all, ((0,), (0,)))
    own, far = columns(24, 2, se), columns(26, 2, se)
    for k, left in enumerate((jnp.where(ch == 0, own, far), jnp.where(ch == 0, far, own))):
        excite_w[k * se : (k + 1) * se, :] = dot(left.astype(BF16), excite_all, ((0,), (0,)))


def call(kernel, ins, outs, scratch, ident=None, in_specs=None, out_specs=None):
    params = {"vmem_limit_bytes": VMEM_LIMIT}
    if ident is not None:
        params.update(collective_id=ident, has_side_effects=True)
    return pl.pallas_call(
        kernel,
        out_shape=[jax.ShapeDtypeStruct(shape, dtype) for shape, dtype in outs],
        in_specs=in_specs or [VMEM] * len(ins),
        out_specs=out_specs or [VMEM] * len(outs),
        scratch_shapes=scratch,
        compiler_params=pltpu.CompilerParams(**params),
    )(*ins)


def lane_tiles(vector):
    return jnp.pad(vector, (0, 1024 - HALF)).reshape(TILES, 128)


def body(
    n,
    pixels,
    crop_counts,
    first_weight,
    first_gain,
    first_shift,
    group_weight,
    group_gain,
    group_shift,
    squeeze_weight,
    squeeze_bias,
    excite_weight,
    excite_bias,
    last_weight,
    last_gain,
    last_shift,
    output_grad,
):
    me = lax.axis_index("img")
    assert pixels.shape == (ROWS, HALF)
    se = squeeze_weight.shape[1]
    wide = (TILES, ROWS, 128)
    stat = (n, 2, TILES, 128)
    sem = DMA((n - 1,))

    local_counts = lax.dynamic_slice_in_dim(crop_counts, me * IMGS, IMGS)
    places = jnp.arange(ROWS_IMG, dtype=jnp.int32)
    living = (places[None, :] < BIG_ROWS) | (
        (places[None, :] - BIG_ROWS) // 9 < local_counts[:, None]
    )
    mask = jnp.broadcast_to(living.reshape(ROWS, 1).astype(F32), (ROWS, 128))
    slots = jnp.arange(10, dtype=jnp.int32)[:, None] < local_counts[None, :]
    mask10 = jnp.broadcast_to(slots[:, :, None].astype(F32), (10, IMGS, 128))
    per_image = (BIG_ROWS + 9 * crop_counts).astype(F32)
    live = jnp.sum(per_image.reshape(n, IMGS), axis=1)
    count = lax.dynamic_slice_in_dim(live, me, 1).reshape(1, 1)
    live = jnp.broadcast_to(live[:, None, None], (n, TILES, 128))
    inverse = 1.0 / (BIG_ROWS + 9 * local_counts).astype(F32)
    inverse = jnp.broadcast_to(inverse[:, None], (IMGS, 128))
    norm1, norm2, norm3 = (
        jnp.stack([lane_tiles(gain), lane_tiles(shift)])
        for gain, shift in (
            (first_gain, first_shift),
            (group_gain, group_shift),
            (last_gain, last_shift),
        )
    )
    kernel = jnp.pad(
        group_weight.reshape(9 * GROUP_WIDTH, HALF).astype(F32), ((0, 0), (0, 1024 - HALF))
    )
    local = pltpu.VMEM((2, TILES, 128), F32)
    consts = pltpu.VMEM((8, TILES, 128), F32)
    vectors = ((2, TILES, 128), F32)
    bands = [pltpu.VMEM(((e - s) * 128, 9 * 256), BF16) for s, e in WINDOWS]
    smem = pl.BlockSpec(memory_space=pltpu.SMEM)

    first, pixels_far, stats1 = call(
        functools.partial(first_kernel, n),
        (count, pixels, first_weight, mask),
        [(wide, F32), ((ROWS, HALF), BF16), (stat, F32)],
        [local, DMA((4,)), DMA((4,)), sem, sem],
        0,
        in_specs=[smem, VMEM, VMEM, VMEM],
    )
    padded, group, stats2, first_far, last_far = call(
        functools.partial(group_kernel, n),
        (count, first, stats1, live, norm1, mask10, kernel, first_weight, last_weight),
        [
            ((TILES, PAD_ROWS, 128), BF16),
            (wide, F32),
            (stat, F32),
            ((HALF, HALF), BF16),
            ((HALF, HALF), BF16),
        ],
        [consts, local, *bands, DMA((2,)), DMA((2,)), sem, sem],
        1,
        in_specs=[smem] + [VMEM] * 6 + [ANY] * 2,
        out_specs=[VMEM] * 3 + [ANY] * 2,
    )
    small = (TILES, IMGS, 128)
    (
        scaled,
        scaled_far,
        last,
        stats3,
        pooled,
        pooled_far,
        squeezed,
        squeezed_far,
        squeeze_pre,
        excited,
    ) = call(
        functools.partial(gate_kernel, n),
        (
            count,
            group,
            stats2,
            live,
            norm2,
            mask10,
            inverse,
            squeeze_weight,
            squeeze_bias[None],
            excite_weight,
            excite_bias[None],
            mask,
            last_weight,
        ),
        [
            (wide, BF16),
            (wide, BF16),
            (wide, F32),
            (stat, F32),
            (small, F32),
            (small, F32),
            ((IMGS, se), F32),
            ((IMGS, se), F32),
            ((IMGS, se), F32),
            (small, F32),
        ],
        [
            consts,
            local,
            pltpu.VMEM(wide, F32),
            pltpu.VMEM((ROWS, 128), F32),
            DMA((TILES,)),
            DMA((TILES,)),
            DMA((2,)),
            DMA((2,)),
            sem,
            sem,
        ],
        2,
        in_specs=[smem] + [VMEM] * 12,
    )
    block_out, merged_grad, sums3 = call(
        functools.partial(merge_kernel, n),
        (last, stats3, live, norm3, mask, pixels, output_grad),
        [((ROWS, HALF), BF16), (wide, F32), (stat, F32)],
        [consts, local, sem, sem],
        3,
    )
    half_grad = ((TILES, 1024, 128), BF16)
    last_grad_own, last_grad_far, scaled_grad, vectors3 = call(
        functools.partial(last_grad_kernel, n),
        (
            last,
            stats3,
            live,
            norm3,
            sums3,
            mask,
            merged_grad,
            scaled,
            scaled_far,
            last_weight,
            last_far,
        ),
        [half_grad, half_grad, (wide, F32), vectors],
        [
            consts,
            pltpu.VMEM(wide, BF16),
            pltpu.VMEM(wide, BF16),
            DMA((TILES,)),
            DMA((TILES,)),
        ],
        4,
    )
    pre_grad, sums2, excite_grad, squeeze_grad = call(
        functools.partial(gate_grad_kernel, n),
        (
            scaled_grad,
            group,
            stats2,
            live,
            norm2,
            mask10,
            inverse,
            excited,
            squeeze_pre,
            squeeze_weight,
            excite_weight,
        ),
        [(wide, F32), (stat, F32), (small, F32), ((IMGS, se), F32)],
        [
            consts,
            local,
            pltpu.VMEM((IMGS, se), F32),
            pltpu.VMEM((IMGS, se), F32),
            pltpu.VMEM((IMGS, HALF), F32),
            pltpu.VMEM((IMGS, HALF), F32),
            pltpu.VMEM(small, F32),
            DMA((2,)),
            DMA((2,)),
            sem,
            sem,
        ],
        5,
    )
    kernel_grad, first_pre_grad, sums1, vectors2 = call(
        functools.partial(group_grad_kernel, n),
        (
            pre_grad,
            group,
            stats2,
            live,
            norm2,
            sums2,
            mask10,
            kernel,
            padded,
            first,
            stats1,
            norm1,
        ),
        [((TILES, 512, 128), BF16), (wide, F32), (stat, F32), vectors],
        [
            consts,
            consts,
            local,
            pltpu.VMEM((TILES, PAD_ROWS, 128), BF16),
            *bands,
            pltpu.VMEM((512, 9 * 256), F32),
            sem,
            sem,
        ],
        6,
    )
    first_grad_own, first_grad_far, pixels_grad, vectors1 = call(
        functools.partial(first_grad_kernel, n),
        (
            first_pre_grad,
            first,
            stats1,
            live,
            norm1,
            sums1,
            mask10,
            pixels,
            pixels_far,
            first_weight,
            first_far,
            merged_grad,
        ),
        [half_grad, half_grad, ((ROWS, HALF), F32), vectors],
        [
            consts,
            pltpu.VMEM(wide, BF16),
            pltpu.VMEM(wide, BF16),
            pltpu.VMEM((ROWS, 128), F32),
            DMA((TILES,)),
            DMA((TILES,)),
        ],
        7,
    )

    def tiles_of(value):
        return jnp.pad(value, ((0, 0), (0, 256 - se))).reshape(IMGS, 2, 128).swapaxes(0, 1)

    factors = jnp.concatenate(
        [
            pooled,
            pooled_far,
            excite_grad,
            tiles_of(squeezed),
            tiles_of(squeezed_far),
            tiles_of(squeeze_grad),
        ]
    )
    count_tiles = factors.shape[0]
    factors = factors.reshape(count_tiles * IMGS, 128).astype(BF16)

    sizes = image_axes(n)
    forth, back = (0, 1, 2), (1, 0, 2)

    def split(array, order):
        rows = array.shape[0] * array.shape[1]
        return array.reshape(*(sizes[a] for a in order), rows // n, 128)

    half = kernel_grad.shape[1] // 2
    sources = [
        split(last_grad_own, forth),
        split(last_grad_far, back),
        split(first_grad_own, forth),
        split(first_grad_far, back),
        split(kernel_grad[:, :half], forth),
        split(kernel_grad[:, half:], back),
        factors,
    ]
    orders = (forth, back, forth, back, forth, back, forth)
    reduces = (True,) * 6 + (False,)
    shapes = [s.shape for s in sources[:-1]] + [sizes + factors.shape]
    scratch = []
    for order, shape, reduce in zip(orders, shapes, reduces):
        scratch.extend(Part.scratch(n, order, shape, reduce))
    results = call(
        functools.partial(settle_kernel, n, orders, reduces),
        sources,
        [(shape, BF16) for shape in shapes],
        scratch,
        8,
    )
    grads = [r.reshape(TILES, -1, 128) for r in results[:-1]]

    def spread(own, far):
        return call(spread_kernel, (own, far), [((2 * HALF, HALF), F32)], [])[0]

    last_weight_grad = spread(grads[0], grads[1])
    first_weight_grad = spread(grads[2], grads[3])
    group_weight_grad, squeeze_weight_grad, squeeze_bias_grad, excite_weight_grad, excite_bias_grad = call(
        finish_kernel,
        (grads[4], grads[5], results[-1].reshape(n, count_tiles * IMGS, 128)),
        [
            ((9 * GROUP_WIDTH, HALF), F32),
            ((2 * HALF, se), F32),
            ((1, se), F32),
            ((2 * se, HALF), F32),
            ((1, HALF), F32),
        ],
        [],
    )
    group_weight_grad = group_weight_grad.reshape(3, 3, GROUP_WIDTH, HALF)
    squeeze_bias_grad, excite_bias_grad = squeeze_bias_grad[0], excite_bias_grad[0]

    def pair(vector):
        flat = vector.reshape(2, 1024)[:, :HALF]
        return flat[0], flat[1]

    first_gain_grad, first_shift_grad = pair(vectors1)
    group_gain_grad, group_shift_grad = pair(vectors2)
    last_gain_grad, last_shift_grad = pair(vectors3)
    return (
        block_out,
        pixels_grad,
        first_weight_grad,
        first_gain_grad,
        first_shift_grad,
        group_weight_grad,
        group_gain_grad,
        group_shift_grad,
        squeeze_weight_grad,
        squeeze_bias_grad,
        excite_weight_grad,
        excite_bias_grad,
        last_weight_grad,
        last_gain_grad,
        last_shift_grad,
    )


def solution(mesh):
    wide = P("img", "ch")
    matrix, vector = P(None, "ch"), P("ch")
    cube = P(None, None, None, "ch")
    weights = (matrix, vector, vector, cube, vector, vector, matrix, vector, matrix, vector, matrix, vector, vector)
    return jax.shard_map(
        functools.partial(body, mesh.shape["img"]),
        mesh=mesh,
        in_specs=(wide, P(), *weights, wide),
        out_specs=(wide, wide, *weights),
        check_vma=False,
    )
```

```python
import functools

import jax
import jax.numpy as jnp
from jax import lax
from jax.experimental import pallas as pl
from jax.experimental.pallas import tpu as pltpu
from jax.sharding import PartitionSpec as P


GROUP_WIDTH = 56
ROWS_IMG = 188
BIG_ROWS = 98
IMGS = 8
ROWS = IMGS * ROWS_IMG
HALF = 1008
TILES = 8
LAST = HALF - 7 * 128
EPSILON = 1e-05
F32 = jnp.float32
BF16 = jnp.bfloat16
HIGHEST = lax.Precision.HIGHEST
MESH = pl.DeviceIdType.MESH
VMEM = pl.BlockSpec(memory_space=pltpu.VMEM)
ANY = pl.BlockSpec(memory_space=pl.ANY)
VMEM_LIMIT = 60 * 1024 * 1024
SPANS = ((0, 256), (256, 512), (512, 768), (768, 1008))
WINDOWS = ((0, 3), (1, 5), (3, 7), (5, 8))
BIG_PAD = 73 * 16
PAD_ROWS = BIG_PAD + 21 * 80
TAPS = tuple((dy, dx) for dy in (-1, 0, 1) for dx in (-1, 0, 1))
DMA = pltpu.SemaphoreType.DMA


def big_place(y, x):
    return (1 + (y + 1) * 8 + x) * 16


def small_place(y, x):
    return BIG_PAD + (1 + (y + 1) * 4 + x) * 80


def natural_row(tile):
    if tile < BIG_ROWS:
        return (tile % 2) * 49 + tile // 2
    tile = tile - BIG_ROWS
    return BIG_ROWS + (tile % 10) * 9 + tile // 10


def padded_row(tile):
    if tile < BIG_ROWS:
        pixel = tile // 2
        return big_place(pixel // 7, pixel % 7) + (tile % 2) * 8
    tile = tile - BIG_ROWS
    pixel = tile // 10
    return small_place(pixel // 3, pixel % 3) + (tile % 10) * 8


REAL_ROWS = frozenset(padded_row(tile) for tile in range(0, ROWS_IMG, 2))
ZERO_ROWS = tuple(row for row in range(0, PAD_ROWS, 16) if row not in REAL_ROWS)


def sigmoid(v):
    return 0.5 + 0.5 * jnp.tanh(0.5 * v)


def slope_of(v, s):
    return s * (1.0 + v * (1.0 - s))


def dot(a, b, dims=((1,), (0,)), **kw):
    return lax.dot_general(a, b, (dims, ((), ())), preferred_element_type=F32, **kw)


def for_each(count, step):
    if count <= 16:
        for index in range(count):
            step(index)
    else:
        lax.fori_loop(0, count, lambda index, _: (step(index), 0)[1], 0)


def for_tiles(step):
    lax.fori_loop(0, TILES, lambda j, _: (step(j), 0)[1], 0)


def for_ragged_tiles(step):
    def full(j, _):
        step(j, pl.ds(pl.multiple_of(j * 128, 128), 128), 128)
        return 0

    lax.fori_loop(0, TILES - 1, full, 0)
    step(TILES - 1, pl.ds(7 * 128, LAST), LAST)


def greet(n, all_images=True, partner=True):
    barrier = pltpu.get_barrier_semaphore()
    me = lax.axis_index("img")
    count = 0
    if all_images:
        for_each(
            n - 1,
            lambda d: pl.semaphore_signal(
                barrier, 1, device_id={"img": lax.rem(me + d + 1, n)}, device_id_type=MESH
            ),
        )
        count += n - 1
    if partner:
        pl.semaphore_signal(
            barrier, 1, device_id={"ch": 1 - lax.axis_index("ch")}, device_id_type=MESH
        )
        count += 1
    return lambda: pl.semaphore_wait(barrier, count)


class Gather:
    def __init__(self, n, source, target, send, recv):
        self.n, self.source, self.target, self.send, self.recv = n, source, target, send, recv
        self.me = lax.axis_index("img")

    def copy(self, d):
        return pltpu.make_async_remote_copy(
            src_ref=self.source,
            dst_ref=self.target.at[self.me],
            send_sem=self.send.at[d],
            recv_sem=self.recv.at[d],
            device_id={"img": lax.rem(self.me + d + 1, self.n)},
            device_id_type=MESH,
        )

    def start(self):
        for_each(self.n - 1, lambda d: self.copy(d).start())
        self.target[self.me] = self.source[...]

    def wait(self):
        for_each(self.n - 1, lambda d: self.copy(d).wait())


def swap(source, target, send, recv):
    return pltpu.make_async_remote_copy(
        src_ref=source,
        dst_ref=target,
        send_sem=send,
        recv_sem=recv,
        device_id={"ch": 1 - lax.axis_index("ch")},
        device_id_type=MESH,
    )


def put_span(ref, span, rows, value, add=False):
    left, right = value[:, :128], value[:, 128:]
    width = right.shape[1]
    if add:
        ref[2 * span, rows, :] += left
        ref[2 * span + 1, rows, 0:width] += right
    else:
        ref[2 * span, rows, :] = left
        ref[2 * span + 1, rows, 0:width] = right


def norm_constants(n, stats, live, gain_shift, consts):
    def total(step):
        return lax.fori_loop(0, n, lambda i, acc: acc + step(i), jnp.zeros((TILES, 128), F32))

    number = total(lambda i: live[i])
    average = total(lambda i: live[i] * stats[i, 0]) / number

    def centred(i):
        off = stats[i, 0] - average
        return stats[i, 1] + live[i] * off * off

    variance = total(centred) / number
    consts[0] = average
    consts[1] = lax.rsqrt(variance + EPSILON)
    consts[2] = gain_shift[0]
    consts[3] = gain_shift[1]
    consts[4] = number


def back_constants(n, sums, consts, grads):
    shift_grad = lax.fori_loop(
        0, n, lambda i, acc: acc + sums[i, 0], jnp.zeros((TILES, 128), F32)
    )
    gain_grad = lax.fori_loop(
        0, n, lambda i, acc: acc + sums[i, 1], jnp.zeros((TILES, 128), F32)
    )
    grads[0] = gain_grad
    grads[1] = shift_grad
    consts[5] = shift_grad / consts[4]
    consts[6] = gain_grad / consts[4]
    consts[7] = consts[1] * consts[2]


def row_of(consts, k, j):
    return consts[k, pl.ds(j, 1), :]


def natural_stats(ref, mask, count, local):
    def step(j):
        x = ref[j]
        m = mask[...]
        average = jnp.sum(x * m, axis=0, keepdims=True) / count
        off = x - average
        local[0, pl.ds(j, 1), :] = average
        local[1, pl.ds(j, 1), :] = jnp.sum(m * off * off, axis=0, keepdims=True)

    for_tiles(step)


def crop_sum(value, mask10):
    big = jnp.sum(value[:BIG_ROWS], axis=0)
    small = jnp.sum(value[BIG_ROWS:].reshape(9, 10, IMGS, 128), axis=0)
    return big + jnp.sum(small * mask10[...], axis=0)


def crop_stats(ref, mask10, count, local):
    def step(j):
        x = ref[j].reshape(ROWS_IMG, IMGS, 128)
        average = jnp.sum(crop_sum(x, mask10), axis=0, keepdims=True) / count
        off = x - average[None]
        local[0, pl.ds(j, 1), :] = average
        local[1, pl.ds(j, 1), :] = jnp.sum(crop_sum(off * off, mask10), axis=0, keepdims=True)

    for_tiles(step)


def window(ref, tiles, dy, dx, big):
    pieces = []
    for y in range(7 if big else 3):
        start = big_place(y + dy, dx) if big else small_place(y + dy, dx)
        rows = slice(start, start + (112 if big else 240))
        pieces.append(jnp.concatenate([ref[t, rows, :] for t in tiles], axis=1))
    return jnp.concatenate(pieces, axis=0)


def build_bands(kernel, bands):
    for span, (first, end) in enumerate(WINDOWS):
        base = first * 128
        depth = (end - first) * 128
        lane = lax.broadcasted_iota(jnp.int32, (GROUP_WIDTH, 256), 1) + span * 256
        groups = range(span * 256 // GROUP_WIDTH, min(18, (span * 256 + 255) // GROUP_WIDTH + 1))
        masks = [
            (lane >= g * GROUP_WIDTH) & (lane < (g + 1) * GROUP_WIDTH) for g in groups
        ]
        head = groups[0] * GROUP_WIDTH - base
        tail = depth - head - len(groups) * GROUP_WIDTH
        for tap in range(9):
            piece = kernel[
                tap * GROUP_WIDTH : (tap + 1) * GROUP_WIDTH, span * 256 : span * 256 + 256
            ]
            parts = [jnp.where(m, piece, 0.0) for m in masks]
            if head:
                parts.insert(0, jnp.zeros((head, 256), F32))
            if tail:
                parts.append(jnp.zeros((tail, 256), F32))
            bands[span][:, tap * 256 : tap * 256 + 256] = jnp.concatenate(parts, axis=0).astype(
                BF16
            )


def zero_pads(ref, j):
    for row in ZERO_ROWS:
        ref[j, row : row + 16, :] = jnp.zeros((16, 128), BF16)


def first_kernel(
    n, count, pixels, weight, mask, first, other, stats, local, swap_s, swap_r, send, recv
):
    ch = lax.axis_index("ch")
    wait_all = greet(n)
    own = pl.multiple_of(ch * HALF, 16)
    far = pl.multiple_of((1 - ch) * HALF, 16)
    wait_all()
    chunks = ((0, 384), (384, 384), (768, 384), (1152, 352))
    swaps = []
    for k, (start, size) in enumerate(chunks):
        rows = pl.ds(start, size)
        swaps.append(swap(pixels.at[rows], other.at[rows], swap_s.at[k], swap_r.at[k]))
        swaps[-1].start()
    first[7, :, LAST:128] = jnp.zeros((ROWS, 128 - LAST), F32)
    for t, (a, b) in enumerate(SPANS):
        put_span(first, t, slice(0, ROWS), dot(pixels[...], weight[pl.ds(own, HALF), a:b]))
    for k, (start, size) in enumerate(chunks):
        swaps[k].wait()
        rows = slice(start, start + size)
        for t, (a, b) in enumerate(SPANS):
            put_span(first, t, rows, dot(other[rows, :], weight[pl.ds(far, HALF), a:b]), add=True)
    natural_stats(first, mask, count[0, 0], local)
    gather = Gather(n, local, stats, send, recv)
    gather.start()
    gather.wait()


def group_kernel(
    n,
    count,
    first,
    stats1,
    live,
    norm1,
    mask10,
    kernel,
    weight1,
    weight3,
    padded,
    group,
    stats2,
    far1,
    far3,
    consts,
    local,
    band0,
    band1,
    band2,
    band3,
    swap_s,
    swap_r,
    send,
    recv,
):
    wait_all = greet(n)
    norm_constants(n, stats1, live, norm1, consts)
    wait_all()
    far = pl.multiple_of((1 - lax.axis_index("ch")) * HALF, 16)
    swaps = [
        swap(w.at[pl.ds(far, HALF)], f, swap_s.at[k], swap_r.at[k])
        for k, (w, f) in enumerate(((weight1, far1), (weight3, far3)))
    ]
    for s in swaps:
        s.start()
    bands = (band0, band1, band2, band3)
    build_bands(kernel, bands)

    def step(j):
        average = row_of(consts, 0, j)
        scale = row_of(consts, 1, j) * row_of(consts, 2, j)
        shift = row_of(consts, 3, j)
        zero_pads(padded, j)
        for tile in range(0, ROWS_IMG, 2):
            both = []
            for half in range(2):
                x = first[j, pl.ds(natural_row(tile + half), IMGS, stride=ROWS_IMG), :]
                pre = (x - average) * scale + shift
                both.append(pre * sigmoid(pre))
            row = padded_row(tile)
            padded[j, row : row + 16, :] = jnp.concatenate(both, axis=0).astype(BF16)

    for_tiles(step)
    for span, (start, end) in enumerate(WINDOWS):
        tiles = range(start, end)
        right = jnp.concatenate(
            [bands[span][:, tap * 256 : tap * 256 + 256] for tap in range(9)], axis=0
        )
        for big in (True, False):
            left = jnp.concatenate([window(padded, tiles, dy, dx, big) for dy, dx in TAPS], axis=1)
            rows = slice(0, 784) if big else slice(784, ROWS)
            put_span(group, span, rows, dot(left, right))
    crop_stats(group, mask10, count[0, 0], local)
    gather = Gather(n, local, stats2, send, recv)
    gather.start()
    for s in swaps:
        s.wait()
    gather.wait()


def gate_kernel(
    n,
    count,
    group,
    stats2,
    live,
    norm2,
    mask10,
    inverse,
    squeeze_w,
    squeeze_b,
    excite_w,
    excite_b,
    mask,
    weight,
    scaled,
    scaled_far,
    last,
    stats3,
    pooled,
    pooled_far,
    squeezed,
    squeezed_far,
    squeeze_pre,
    excited,
    consts,
    local,
    act,
    turned,
    swap_s,
    swap_r,
    small_s,
    small_r,
    send,
    recv,
):
    ch = lax.axis_index("ch")
    wait_all = greet(n)
    norm_constants(n, stats2, live, norm2, consts)

    def activate(j):
        average = row_of(consts, 0, j)
        scale = row_of(consts, 1, j) * row_of(consts, 2, j)
        pre = (group[j] - average) * scale + row_of(consts, 3, j)
        value = pre * sigmoid(pre)
        act[j] = value
        pooled[j] = crop_sum(value.reshape(ROWS_IMG, IMGS, 128), mask10) * inverse[...]

    for_tiles(activate)
    wait_all()
    pool_swap = swap(pooled, pooled_far, small_s.at[0], small_r.at[0])
    pool_swap.start()
    pool_swap.wait()
    mine = jnp.concatenate([pooled[j] for j in range(TILES)], axis=1)[:, :HALF]
    theirs = jnp.concatenate([pooled_far[j] for j in range(TILES)], axis=1)[:, :HALF]
    is_low = ch == 0
    pre = (
        dot(jnp.where(is_low, mine, theirs), squeeze_w[0:HALF, :], precision=HIGHEST)
        + dot(jnp.where(is_low, theirs, mine), squeeze_w[HALF:, :], precision=HIGHEST)
        + squeeze_b[...]
    )
    squeeze_pre[...] = pre
    squeezed[...] = pre * sigmoid(pre)
    squeeze_swap = swap(squeezed, squeezed_far, small_s.at[1], small_r.at[1])
    squeeze_swap.start()
    squeeze_swap.wait()
    mine, theirs = squeezed[...], squeezed_far[...]
    width = mine.shape[1]
    gate = sigmoid(
        dot(jnp.where(is_low, mine, theirs), excite_w[0:width, :], precision=HIGHEST)
        + dot(jnp.where(is_low, theirs, mine), excite_w[width:, :], precision=HIGHEST)
        + excite_b[...]
    )
    excited[7] = jnp.zeros((IMGS, 128), F32)
    for j in range(TILES - 1):
        excited[j] = gate[:, j * 128 : j * 128 + 128]
    excited[7, :, 0:LAST] = gate[:, 7 * 128 :]

    def apply(j):
        gate_j = excited[j]
        for tile in range(ROWS_IMG):
            turned[pl.ds(natural_row(tile), IMGS, stride=ROWS_IMG), :] = (
                act[j, tile * 8 : tile * 8 + 8, :] * gate_j
            )
        scaled[j] = turned[...].astype(BF16)
        swap(scaled.at[j], scaled_far.at[j], swap_s.at[j], swap_r.at[j]).start()

    for_tiles(apply)
    own = pl.multiple_of(ch * HALF, 16)
    far = pl.multiple_of((1 - ch) * HALF, 16)
    last[7, :, LAST:128] = jnp.zeros((ROWS, 128 - LAST), F32)
    for t, (a, b) in enumerate(SPANS):
        left = jnp.concatenate([scaled[j] for j in range(TILES)], axis=1)[:, :HALF]
        put_span(last, t, slice(0, ROWS), dot(left, weight[pl.ds(own, HALF), a:b]))
    for_tiles(lambda j: swap(scaled.at[j], scaled_far.at[j], swap_s.at[j], swap_r.at[j]).wait())
    for t, (a, b) in enumerate(SPANS):
        left = jnp.concatenate([scaled_far[j] for j in range(TILES)], axis=1)[:, :HALF]
        put_span(last, t, slice(0, ROWS), dot(left, weight[pl.ds(far, HALF), a:b]), add=True)
    natural_stats(last, mask, count[0, 0], local)
    gather = Gather(n, local, stats3, send, recv)
    gather.start()
    gather.wait()


def merge_kernel(
    n, last, stats3, live, norm3, mask, pixels, output_grad, block, merged_grad, sums3, consts, local, send, recv
):
    wait_all = greet(n, partner=False)
    norm_constants(n, stats3, live, norm3, consts)
    merged_grad[7, :, LAST:128] = jnp.zeros((ROWS, 128 - LAST), F32)
    local[...] = jnp.zeros_like(local)

    def step(j, lanes, width):
        def vec(k):
            return consts[k, pl.ds(j, 1), 0:width]

        m = mask[:, 0:width]
        normed = (last[j, :, 0:width] - vec(0)) * vec(1)
        merged = pixels[:, lanes].astype(F32) + normed * vec(2) + vec(3)
        s = sigmoid(merged)
        block[:, lanes] = (merged * s * m).astype(BF16)
        grad = output_grad[:, lanes].astype(F32) * m * slope_of(merged, s)
        merged_grad[j, :, 0:width] = grad
        local[0, pl.ds(j, 1), 0:width] = jnp.sum(grad, axis=0, keepdims=True)
        local[1, pl.ds(j, 1), 0:width] = jnp.sum(grad * normed, axis=0, keepdims=True)

    for_ragged_tiles(step)
    wait_all()
    gather = Gather(n, local, sums3, send, recv)
    gather.start()
    gather.wait()


def part_extents(n, order):
    sizes = image_axes(n)
    return tuple(sizes[a] for a in order)


def part_shape(n, order, rows):
    return part_extents(n, order) + (rows // n, 128)


def put_blocks(target, tile, tile_rows, start, value):
    _, e1, e2, rows, _ = target.shape
    size = value.shape[0]
    first = start
    while first < start + size:
        block = tile * (tile_rows // rows) + first // rows
        inside = first % rows
        take = min(rows - inside, start + size - first)
        place = (block // (e1 * e2), block // e2 % e1, block % e2)
        target[place[0], place[1], place[2], inside : inside + take, :] = value[
            first - start : first - start + take
        ]
        first += take


def weight_grad(left_span, right_tiles, target, spans):
    for a, b in SPANS:
        left = left_span(a, b)
        for k, span in enumerate(spans):
            right = jnp.concatenate([right_tiles(2 * span), right_tiles(2 * span + 1)], axis=1)
            value = dot(left, right, ((0,), (0,))).astype(BF16)
            put_blocks(target, 2 * k, 1024, a, value[:, :128])
            put_blocks(target, 2 * k + 1, 1024, a, value[:, 128:])


def tile_span(ref):
    def span(a, b):
        tiles = range(a // 128, (b + 127) // 128)
        return jnp.concatenate([ref[t] for t in tiles], axis=1)[:, : b - a]

    return span


def image_axes(n):
    return {16: (2, 2, 4), 128: (8, 4, 4)}.get(n, (n, 1, 1))


class Part:
    def __init__(self, n, order, sems):
        sizes = image_axes(n)
        strides = (1, sizes[0], sizes[0] * sizes[1])
        self.me = lax.axis_index("img")
        self.sizes = [sizes[a] for a in order]
        self.strides = [strides[a] for a in order]
        self.place = [lax.rem(self.me // s, e) for s, e in zip(self.strides, self.sizes)]
        self.sems = sems
        self.live = []

    def send(self, axis, stage, source, target):
        for d in range(1, self.sizes[axis]):
            q = lax.rem(self.place[axis] + d, self.sizes[axis])
            peer = self.me + (q - self.place[axis]) * self.strides[axis]
            copy = pltpu.make_async_remote_copy(
                src_ref=source(q),
                dst_ref=target(d),
                send_sem=self.sems[0].at[stage, d],
                recv_sem=self.sems[1].at[stage, d],
                device_id={"img": peer},
                device_id_type=MESH,
            )
            copy.start()
            self.live.append(copy)

    def keep(self, source, target, stage):
        copy = pltpu.make_async_copy(source, target, self.sems[0].at[stage, 0])
        copy.start()
        self.live.append(copy)

    def settle(self):
        for copy in self.live:
            copy.wait()
        self.live = []

    def add(self, target, own, arrived):
        total = own[...].astype(F32)
        for block in arrived:
            total = total + block[...].astype(F32)
        target[...] = total.astype(BF16)

    def send0(self, source, r0):
        self.send(0, 0, lambda q: source.at[q], lambda d: r0.at[d - 1])

    def sum0(self, source, r0, a0):
        self.settle()
        for k in range(self.sizes[1]):
            self.add(
                a0.at[k],
                source.at[self.place[0], k],
                [r0.at[d, k] for d in range(self.sizes[0] - 1)],
            )

    def send1(self, a0, r1):
        self.send(1, 1, lambda q: a0.at[q], lambda d: r1.at[d - 1])

    def sum1(self, a0, r1, a1):
        self.settle()
        self.add(a1, a0.at[self.place[1]], [r1.at[d] for d in range(self.sizes[1] - 1)])

    def send2(self, a1, r2):
        self.send(2, 2, lambda q: a1.at[q], lambda d: r2.at[d - 1])

    def sum2(self, a1, r2, column):
        self.settle()
        p2 = self.place[2]
        self.add(column.at[p2], a1.at[p2], [r2.at[d] for d in range(self.sizes[2] - 1)])

    def spread2(self, column):
        block = column.at[self.place[2]]
        self.send(2, 3, lambda q: block, lambda d: block)

    def spread1(self, column, result):
        self.settle()
        block = result.at[self.place[0], self.place[1]]
        self.send(1, 4, lambda q: column, lambda d: block)
        self.keep(column, block, 4)

    def spread0(self, result):
        self.settle()
        block = result.at[self.place[0]]
        self.send(0, 5, lambda q: block, lambda d: block)

    @staticmethod
    def room(n, order, shape):
        e0, e1, e2, rows, lanes = shape
        return (
            (max(e0 - 1, 1), e1, e2, rows, lanes),
            (e1, e2, rows, lanes),
            (max(e1 - 1, 1), e2, rows, lanes),
            (e2, rows, lanes),
            (max(e2 - 1, 1), rows, lanes),
            (e2, rows, lanes),
        )


def part_sems(n, count):
    most = max(image_axes(n))
    return [DMA((6, most)) for _ in range(2 * count)]


def fetch(source, target, sem):
    copy = pltpu.make_async_copy(source, target, sem)
    copy.start()
    return copy


class Refs:
    def __init__(self, refs):
        self.refs = list(refs)

    def take(self, count=None):
        if count is None:
            return self.refs.pop(0)
        head, self.refs = self.refs[:count], self.refs[count:]
        return head


ORDERS = ((0, 1, 2), (1, 0, 2), (0, 1, 2), (1, 0, 2))


def last_grad_kernel(n, *refs):
    r = Refs(refs)
    last_any, merged_any, group_any, scaled_any, scaled_far_any, weight_any, weight_far_any = r.take(7)
    stats3, live, norm3, sums3, mask = r.take(5)
    stats2, norm2, mask10, inverse, excited, squeeze_pre, squeeze_any, excite_any = r.take(8)
    pre_grad, sums2, excite_grad, squeeze_grad, vectors = r.take(5)
    mid1, mid3 = r.take(2), r.take(2)
    arrive1 = r.take(2)
    consts, consts2, local, buf_a, buf_b, low, low_far, scaled, scaled_far = r.take(9)
    weight, weight_far, squeeze_w, excite_w = r.take(4)
    terms, terms_in, pool_terms, pool_in, pool_tiles = r.take(5)
    grads, rooms = r.take(4), r.take(4)
    load, swap_s, swap_r, small_s, small_r, send, recv = r.take(7)
    sems = r.take(8)
    ch = lax.axis_index("ch")
    own = pl.multiple_of(ch * HALF, 16)
    wait_all = greet(n)
    loads = [
        fetch(source, target, load.at[k])
        for k, (source, target) in enumerate(
            (
                (last_any, buf_a),
                (merged_any, buf_b),
                (scaled_any, scaled),
                (scaled_far_any, scaled_far),
                (weight_any.at[pl.ds(own, HALF)], weight),
                (weight_far_any, weight_far),
                (squeeze_any, squeeze_w),
                (excite_any, excite_w),
            )
        )
    ]
    norm_constants(n, stats3, live, norm3, consts)
    back_constants(n, sums3, consts, vectors)
    norm_constants(n, stats2, live, norm2, consts2)
    parts = [Part(n, order, sems[2 * k : 2 * k + 2]) for k, order in enumerate(ORDERS)]
    wait_all()
    loads[0].wait()
    loads[1].wait()

    def step(j):
        normed = (buf_a[j] - row_of(consts, 0, j)) * row_of(consts, 1, j)
        inner = buf_b[j] - row_of(consts, 5, j) - normed * row_of(consts, 6, j)
        low[j] = (mask[...] * row_of(consts, 7, j) * inner).astype(BF16)
        swap(low.at[j], low_far.at[j], swap_s.at[j], swap_r.at[j]).start()

    for_tiles(step)
    load_group = fetch(group_any, buf_a, load.at[0])
    for part in range(4):
        if part < 2:
            loads[2 + part].wait()
        left = tile_span((scaled, scaled_far)[part % 2])
        weight_grad(left, lambda t: low[t], grads[part], (0, 1) if part < 2 else (2, 3))
        if part < 2:
            parts[part].send0(grads[part], rooms[part])
    loads[4].wait()
    for t, (a, b) in enumerate(SPANS):
        left = jnp.concatenate([low[j] for j in range(TILES)], axis=1)[:, :HALF]
        put_span(buf_b, t, slice(0, ROWS), dot(left, weight[a:b, :], ((1,), (1,))))
    buf_b[7, :, LAST:128] = jnp.zeros((ROWS, 128 - LAST), F32)
    for_tiles(lambda j: swap(low.at[j], low_far.at[j], swap_s.at[j], swap_r.at[j]).wait())
    loads[5].wait()
    for t, (a, b) in enumerate(SPANS):
        left = jnp.concatenate([low_far[j] for j in range(TILES)], axis=1)[:, :HALF]
        put_span(
            buf_b, t, slice(0, ROWS), dot(left, weight_far[a:b, :], ((1,), (1,))), add=True
        )
    load_group.wait()

    def gate_sum(j):
        average = row_of(consts2, 0, j)
        scale = row_of(consts2, 1, j) * row_of(consts2, 2, j)
        shift = row_of(consts2, 3, j)
        total = jnp.zeros((IMGS, 128), F32)
        for tile in range(ROWS_IMG):
            pre = (buf_a[j, tile * 8 : tile * 8 + 8, :] - average) * scale + shift
            act = pre * sigmoid(pre)
            total = total + act * buf_b[j, pl.ds(natural_row(tile), IMGS, stride=ROWS_IMG), :]
        gate = excited[j]
        excite_grad[j] = total * gate * (1.0 - gate)

    for_tiles(gate_sum)
    for k in range(2):
        parts[k].sum0(grads[k], rooms[k], mid1[k])
        parts[k].send1(mid1[k], arrive1[k])
        parts[k + 2].send0(grads[k + 2], rooms[k + 2])
    wide = jnp.concatenate([excite_grad[j] for j in range(TILES)], axis=1)[:, :HALF]
    width = squeeze_w.shape[1]
    is_low = ch == 0
    loads[6].wait()
    loads[7].wait()
    part0 = dot(wide, excite_w[0:width, :], ((1,), (1,)), precision=HIGHEST)
    part1 = dot(wide, excite_w[width:, :], ((1,), (1,)), precision=HIGHEST)
    terms[...] = jnp.where(is_low, part1, part0)
    term_swap = swap(terms, terms_in, small_s.at[0], small_r.at[0])
    term_swap.start()
    term_swap.wait()
    pre = squeeze_pre[...]
    grad = (jnp.where(is_low, part0, part1) + terms_in[...]) * slope_of(pre, sigmoid(pre))
    squeeze_grad[...] = grad
    pool0 = dot(grad, squeeze_w[0:HALF, :], ((1,), (1,)), precision=HIGHEST)
    pool1 = dot(grad, squeeze_w[HALF:, :], ((1,), (1,)), precision=HIGHEST)
    pool_terms[...] = jnp.where(is_low, pool1, pool0)
    pool_swap = swap(pool_terms, pool_in, small_s.at[1], small_r.at[1])
    pool_swap.start()
    pool_swap.wait()
    pool = jnp.where(is_low, pool0, pool1) + pool_in[...]
    pool_tiles[7, :, LAST:128] = jnp.zeros((IMGS, 128 - LAST), F32)
    for j in range(TILES):
        part = pool[:, j * 128 : min(HALF, j * 128 + 128)]
        pool_tiles[j, :, 0 : part.shape[1]] = part * inverse[:, 0 : part.shape[1]]

    def slopes(j):
        average, scale = row_of(consts2, 0, j), row_of(consts2, 1, j)
        gain, shift = row_of(consts2, 2, j), row_of(consts2, 3, j)
        gate, pooled = excited[j], pool_tiles[j]
        total = jnp.zeros((IMGS, 128), F32)
        total_normed = jnp.zeros((IMGS, 128), F32)
        for tile in range(ROWS_IMG):
            rows = slice(tile * 8, tile * 8 + 8)
            normed = (buf_a[j, rows, :] - average) * scale
            pre = normed * gain + shift
            lead = pooled if tile < BIG_ROWS else pooled * mask10[(tile - BIG_ROWS) % 10]
            act = buf_b[j, pl.ds(natural_row(tile), IMGS, stride=ROWS_IMG), :] * gate + lead
            grad = act * slope_of(pre, sigmoid(pre))
            buf_a[j, rows, :] = grad
            total = total + grad
            total_normed = total_normed + grad * normed
        local[0, pl.ds(j, 1), :] = jnp.sum(total, axis=0, keepdims=True)
        local[1, pl.ds(j, 1), :] = jnp.sum(total_normed, axis=0, keepdims=True)

    for_tiles(slopes)
    gather = Gather(n, local, sums2, send, recv)
    gather.start()
    store = fetch(buf_a, pre_grad, load.at[0])
    gather.wait()
    for k in range(2):
        parts[k].settle()
        parts[k + 2].sum0(grads[k + 2], rooms[k + 2], mid3[k])
    store.wait()


def group_grad_kernel(n, *refs):
    r = Refs(refs)
    pre_any, group_any, padded_any, first_any = r.take(4)
    stats2, live, norm2, sums2, mask10, kernel, stats1, norm1 = r.take(8)
    mid1, mid3, arrive1 = r.take(2), r.take(2), r.take(2)
    first_pre_grad, sums1, vectors = r.take(3)
    kernel_grads = r.take(2)
    columns = r.take(4)
    consts, consts1, local, buf_a, buf_b, padded_grad, padded, full = r.take(8)
    bands = r.take(4)
    arrive3, a1, r2 = r.take(2), r.take(4), r.take(4)
    load, send, recv = r.take(3)
    sems = r.take(8)
    wait_all = greet(n, partner=False)
    loads = [
        fetch(source, target, load.at[k])
        for k, (source, target) in enumerate(
            ((pre_any, buf_a), (group_any, buf_b), (padded_any, padded))
        )
    ]
    parts = [Part(n, order, sems[2 * k : 2 * k + 2]) for k, order in enumerate(ORDERS)]
    norm_constants(n, stats2, live, norm2, consts)
    back_constants(n, sums2, consts, vectors)
    norm_constants(n, stats1, live, norm1, consts1)
    wait_all()
    for k in range(2):
        parts[k].sum1(mid1[k], arrive1[k], a1[k])
        parts[k].send2(a1[k], r2[k])
        parts[k + 2].send1(mid3[k], arrive3[k])
    build_bands(kernel, bands)
    loads[0].wait()
    loads[1].wait()

    def step(j):
        average, scale = row_of(consts, 0, j), row_of(consts, 1, j)
        less, slope, front = row_of(consts, 5, j), row_of(consts, 6, j), row_of(consts, 7, j)
        zero_pads(padded_grad, j)
        for tile in range(0, ROWS_IMG, 2):
            both = []
            for half in range(2):
                rows = slice(tile * 8 + half * 8, tile * 8 + half * 8 + 8)
                normed = (buf_b[j, rows, :] - average) * scale
                grad = front * (buf_a[j, rows, :] - less - normed * slope)
                if tile >= BIG_ROWS:
                    grad = grad * mask10[(tile + half - BIG_ROWS) % 10]
                both.append(grad)
            row = padded_row(tile)
            padded_grad[j, row : row + 16, :] = jnp.concatenate(both, axis=0).astype(BF16)

    for_tiles(step)
    load_first = fetch(first_any, buf_b, load.at[0])
    loads[2].wait()

    def advance(span):
        if span == 0:
            for k in range(2, 4):
                parts[k].sum1(mid3[k - 2], arrive3[k - 2], a1[k])
                parts[k].send2(a1[k], r2[k])
        elif span == 1:
            for k in range(2):
                parts[k].sum2(a1[k], r2[k], columns[k])
                parts[k].spread2(columns[k])
        elif span == 2:
            for k in range(2, 4):
                parts[k].sum2(a1[k], r2[k], columns[k])
                parts[k].spread2(columns[k])

    started = 0
    for span, (start, end) in enumerate(WINDOWS):
        tiles = (2 * span, 2 * span + 1)
        shifted = [
            jnp.concatenate([window(padded_grad, tiles, -dy, -dx, big) for dy, dx in TAPS], axis=1)
            for big in (True, False)
        ]
        for rows, left in ((slice(0, 784), shifted[0]), (slice(784, ROWS), shifted[1])):
            value = dot(left, bands[span][...], ((1,), (1,)))
            for t in range(start, end):
                part = value[:, (t - start) * 128 : (t - start) * 128 + 128]
                if t < started:
                    buf_a[t, rows, :] += part
                else:
                    buf_a[t, rows, :] = part
        started = end
        right = jnp.concatenate(shifted, axis=0)
        for t in range(start, end, 2):
            pair = range(t, min(t + 2, end))
            left = jnp.concatenate([window(padded, pair, 0, 0, big) for big in (True, False)], axis=0)
            base = (t - start) * 128
            full[base : base + 128 * len(pair), :] = dot(left, right, ((0,), (0,)))
        lane = lax.broadcasted_iota(jnp.int32, (GROUP_WIDTH, 256), 1) + span * 256
        pieces = []
        for tap in range(9):
            piece = jnp.zeros((GROUP_WIDTH, 256), F32)
            for g in range(span * 256 // GROUP_WIDTH, min(18, (span * 256 + 255) // GROUP_WIDTH + 1)):
                row = g * GROUP_WIDTH - start * 128
                inside = (lane >= g * GROUP_WIDTH) & (lane < (g + 1) * GROUP_WIDTH)
                block = full[row : row + GROUP_WIDTH, tap * 256 : tap * 256 + 256]
                piece = jnp.where(inside, block, piece)
            pieces.append(piece)
        pieces.append(jnp.zeros((8, 256), F32))
        value = jnp.concatenate(pieces, axis=0).astype(BF16)
        for half in range(2):
            rows = slice(half * 256, half * 256 + 256)
            put_blocks(kernel_grads[half], 2 * span, 256, 0, value[rows, :128])
            put_blocks(kernel_grads[half], 2 * span + 1, 256, 0, value[rows, 128:])
        advance(span)
    load_first.wait()

    def slopes(j):
        average, scale = row_of(consts1, 0, j), row_of(consts1, 1, j)
        gain, shift = row_of(consts1, 2, j), row_of(consts1, 3, j)
        total = jnp.zeros((IMGS, 128), F32)
        total_normed = jnp.zeros((IMGS, 128), F32)
        for tile in range(ROWS_IMG):
            rows = slice(tile * 8, tile * 8 + 8)
            x = buf_b[j, pl.ds(natural_row(tile), IMGS, stride=ROWS_IMG), :]
            normed = (x - average) * scale
            pre = normed * gain + shift
            grad = buf_a[j, rows, :] * slope_of(pre, sigmoid(pre))
            if tile >= BIG_ROWS:
                grad = grad * mask10[(tile - BIG_ROWS) % 10]
            buf_a[j, rows, :] = grad
            total = total + grad
            total_normed = total_normed + grad * normed
        local[0, pl.ds(j, 1), :] = jnp.sum(total, axis=0, keepdims=True)
        local[1, pl.ds(j, 1), :] = jnp.sum(total_normed, axis=0, keepdims=True)

    for_tiles(slopes)
    gather = Gather(n, local, sums1, send, recv)
    gather.start()
    store = fetch(buf_a, first_pre_grad, load.at[0])
    gather.wait()
    for part in parts:
        part.settle()
    store.wait()


def first_grad_kernel(n, *refs):
    r = Refs(refs)
    pre_any, first_any, pixels_any, pixels_far_any, weight_any, weight_far_any, merged_any = r.take(7)
    stats1, live, norm1, sums1, mask10, factors = r.take(6)
    kernel_grads, columns = r.take(2), r.take(4)
    pixels_grad, vectors = r.take(2)
    last_sums, first_sums, kernel_sums = r.take(4), r.take(4), r.take(2)
    factor_sums = r.take()
    consts, buf_a, buf_b, low, low_far, pixels, pixels_far, weight, weight_far, turned = r.take(10)
    grads = r.take(4)
    first_rooms = [r.take(6) for _ in range(4)]
    kernel_rooms = [r.take(6) for _ in range(2)]
    factor_column = r.take()
    load, swap_s, swap_r = r.take(3)
    sems = [r.take(2) for _ in range(11)]
    own = pl.multiple_of(lax.axis_index("ch") * HALF, 16)
    wait_all = greet(n)
    loads = [
        fetch(source, target, load.at[k])
        for k, (source, target) in enumerate(
            (
                (pre_any, buf_a),
                (first_any, buf_b),
                (pixels_any, pixels),
                (pixels_far_any, pixels_far),
                (weight_any.at[pl.ds(own, HALF)], weight),
                (weight_far_any, weight_far),
            )
        )
    ]
    firsts = [Part(n, order, sems[k]) for k, order in enumerate(ORDERS)]
    lasts = [Part(n, order, sems[4 + k]) for k, order in enumerate(ORDERS)]
    kernels = [Part(n, ORDERS[k], sems[8 + k]) for k in range(2)]
    factor = Part(n, ORDERS[0], sems[10])
    norm_constants(n, stats1, live, norm1, consts)
    back_constants(n, sums1, consts, vectors)
    wait_all()
    for k in range(4):
        lasts[k].spread1(columns[k], last_sums[k])
    for k in range(2):
        kernels[k].send0(kernel_grads[k], kernel_rooms[k][0])
    factor_column[factor.place[2]] = factors[...]
    factor.spread2(factor_column)
    loads[0].wait()
    loads[1].wait()

    def step(j):
        average, scale = row_of(consts, 0, j), row_of(consts, 1, j)
        less, slope, front = row_of(consts, 5, j), row_of(consts, 6, j), row_of(consts, 7, j)
        for tile in range(ROWS_IMG):
            there = pl.ds(natural_row(tile), IMGS, stride=ROWS_IMG)
            normed = (buf_b[j, there, :] - average) * scale
            grad = front * (buf_a[j, tile * 8 : tile * 8 + 8, :] - less - normed * slope)
            if tile >= BIG_ROWS:
                grad = grad * mask10[(tile - BIG_ROWS) % 10]
            turned[there, :] = grad
        low[j] = turned[...].astype(BF16)
        swap(low.at[j], low_far.at[j], swap_s.at[j], swap_r.at[j]).start()

    for_tiles(step)
    load_merged = fetch(merged_any, buf_a, load.at[0])
    for part in range(4):
        if part < 2:
            loads[2 + part].wait()
        rows = (pixels, pixels_far)[part % 2]
        weight_grad(
            lambda a, b: rows[:, a:b], lambda t: low[t], grads[part], (0, 1) if part < 2 else (2, 3)
        )
        if part < 2:
            firsts[part].send0(grads[part], first_rooms[part][0])
    load_merged.wait()
    loads[4].wait()
    for t, (a, b) in enumerate(SPANS):
        left = jnp.concatenate([low[j] for j in range(TILES)], axis=1)[:, :HALF]
        put_span(buf_a, t, slice(0, ROWS), dot(left, weight[a:b, :], ((1,), (1,))), add=True)
    for_tiles(lambda j: swap(low.at[j], low_far.at[j], swap_s.at[j], swap_r.at[j]).wait())
    loads[5].wait()
    for t, (a, b) in enumerate(SPANS):
        left = jnp.concatenate([low_far[j] for j in range(TILES)], axis=1)[:, :HALF]
        put_span(buf_a, t, slice(0, ROWS), dot(left, weight_far[a:b, :], ((1,), (1,))), add=True)
    store = fetch(buf_a, pixels_grad, load.at[0])

    def advance(part, stage, source, room, result):
        r0, a0, r1, a1, r2, column = room
        if stage == 0:
            part.send0(source, r0)
        elif stage == 1:
            part.sum0(source, r0, a0)
            part.send1(a0, r1)
        elif stage == 2:
            part.sum1(a0, r1, a1)
            part.send2(a1, r2)
        elif stage == 3:
            part.sum2(a1, r2, column)
            part.spread2(column)
        elif stage == 4:
            part.spread1(column, result)
        elif stage == 5:
            part.spread0(result)
        else:
            part.settle()

    def first_to(k, stage):
        advance(firsts[k], stage, grads[k], first_rooms[k], first_sums[k])

    def kernel_to(stage):
        for k in range(2):
            advance(kernels[k], stage, kernel_grads[k], kernel_rooms[k], kernel_sums[k])

    for tick in range(1, 8):
        for k in range(4):
            stage = tick - (1 if k >= 2 else 0)
            if 0 <= stage <= 6 and not (k < 2 and stage == 0):
                first_to(k, stage)
        if tick <= 6:
            kernel_to(tick)
        if tick == 1:
            for k in range(4):
                lasts[k].spread0(last_sums[k])
            factor.spread1(factor_column, factor_sums)
        if tick == 2:
            factor.spread0(factor_sums)
    for k in range(4):
        lasts[k].settle()
    factor.settle()
    store.wait()


def spread_kernel(*refs):
    lasts, firsts, pixels_wide = refs[0:4], refs[4:8], refs[8]
    last_out, first_out, pixels_out = refs[9:12]
    ch = lax.axis_index("ch")
    j = pl.program_id(0)
    for sums, out in ((lasts, last_out), (firsts, first_out)):
        for late in range(2):

            @pl.when((j >= 4) == bool(late))
            def _():
                for k, place in ((0, ch), (1, 1 - ch)):
                    rows = pl.ds(pl.multiple_of(place * HALF, 8), HALF)
                    out[rows, :] = sums[2 * late + k][0, 0:HALF, :].astype(F32)

    pixels_out[...] = pixels_wide[0]


def finish_kernel(low_half, high_half, factors, group_out, squeeze_w, squeeze_b, excite_w, excite_b):
    ch = lax.axis_index("ch")
    se = squeeze_w.shape[1]
    split = low_half.shape[1]
    for j in range(TILES):
        width = 128 if j < 7 else LAST
        lanes = slice(j * 128, j * 128 + width)
        group_out[0:split, lanes] = low_half[j, :, 0:width].astype(F32)
        rest = 9 * GROUP_WIDTH - split
        group_out[split:, lanes] = high_half[j, :, 0:width].astype(F32)[:rest]
    n = factors.shape[0]
    whole = factors[...].astype(F32).reshape(n, -1, IMGS, 128)

    def columns(start, tiles, width):
        parts = [whole[:, t].reshape(n * IMGS, 128) for t in range(start, start + tiles)]
        return jnp.concatenate(parts, axis=1)[:, :width]

    excite_all, squeeze_all = columns(16, 8, HALF), columns(28, 2, se)
    squeeze_b[...] = jnp.sum(squeeze_all, axis=0, keepdims=True)
    excite_b[...] = jnp.sum(excite_all, axis=0, keepdims=True)
    excite_all, squeeze_all = excite_all.astype(BF16), squeeze_all.astype(BF16)
    for start, place in ((0, ch), (8, 1 - ch)):
        rows = pl.ds(pl.multiple_of(place * HALF, 8), HALF)
        squeeze_w[rows, :] = dot(columns(start, 8, HALF).astype(BF16), squeeze_all, ((0,), (0,)))
    own, far = columns(24, 2, se), columns(26, 2, se)
    for k, left in enumerate((jnp.where(ch == 0, own, far), jnp.where(ch == 0, far, own))):
        excite_w[k * se : (k + 1) * se, :] = dot(left.astype(BF16), excite_all, ((0,), (0,)))


def call(kernel, ins, outs, scratch, ident=None, in_specs=None, out_specs=None, grid=()):
    params = {"vmem_limit_bytes": VMEM_LIMIT}
    if ident is not None:
        params.update(collective_id=ident, has_side_effects=True)
    return pl.pallas_call(
        kernel,
        grid=grid,
        out_shape=[jax.ShapeDtypeStruct(shape, dtype) for shape, dtype in outs],
        in_specs=in_specs or [VMEM] * len(ins),
        out_specs=out_specs or [VMEM] * len(outs),
        scratch_shapes=scratch,
        compiler_params=pltpu.CompilerParams(**params),
    )(*ins)


def lane_tiles(vector):
    return jnp.pad(vector, (0, 1024 - HALF)).reshape(TILES, 128)


def body(
    n,
    pixels,
    crop_counts,
    first_weight,
    first_gain,
    first_shift,
    group_weight,
    group_gain,
    group_shift,
    squeeze_weight,
    squeeze_bias,
    excite_weight,
    excite_bias,
    last_weight,
    last_gain,
    last_shift,
    output_grad,
):
    me = lax.axis_index("img")
    assert pixels.shape == (ROWS, HALF)
    se = squeeze_weight.shape[1]
    wide = (TILES, ROWS, 128)
    stat = (n, 2, TILES, 128)
    sem = DMA((n - 1,))

    local_counts = lax.dynamic_slice_in_dim(crop_counts, me * IMGS, IMGS)
    places = jnp.arange(ROWS_IMG, dtype=jnp.int32)
    living = (places[None, :] < BIG_ROWS) | (
        (places[None, :] - BIG_ROWS) // 9 < local_counts[:, None]
    )
    mask = jnp.broadcast_to(living.reshape(ROWS, 1).astype(F32), (ROWS, 128))
    slots = jnp.arange(10, dtype=jnp.int32)[:, None] < local_counts[None, :]
    mask10 = jnp.broadcast_to(slots[:, :, None].astype(F32), (10, IMGS, 128))
    per_image = (BIG_ROWS + 9 * crop_counts).astype(F32)
    live = jnp.sum(per_image.reshape(n, IMGS), axis=1)
    count = lax.dynamic_slice_in_dim(live, me, 1).reshape(1, 1)
    live = jnp.broadcast_to(live[:, None, None], (n, TILES, 128))
    inverse = 1.0 / (BIG_ROWS + 9 * local_counts).astype(F32)
    inverse = jnp.broadcast_to(inverse[:, None], (IMGS, 128))
    norm1, norm2, norm3 = (
        jnp.stack([lane_tiles(gain), lane_tiles(shift)])
        for gain, shift in (
            (first_gain, first_shift),
            (group_gain, group_shift),
            (last_gain, last_shift),
        )
    )
    kernel = jnp.pad(
        group_weight.reshape(9 * GROUP_WIDTH, HALF).astype(F32), ((0, 0), (0, 1024 - HALF))
    )
    local = pltpu.VMEM((2, TILES, 128), F32)
    consts = pltpu.VMEM((8, TILES, 128), F32)
    vectors = ((2, TILES, 128), F32)
    bands = [pltpu.VMEM(((e - s) * 128, 9 * 256), BF16) for s, e in WINDOWS]
    smem = pl.BlockSpec(memory_space=pltpu.SMEM)

    first, pixels_far, stats1 = call(
        functools.partial(first_kernel, n),
        (count, pixels, first_weight, mask),
        [(wide, F32), ((ROWS, HALF), BF16), (stat, F32)],
        [local, DMA((4,)), DMA((4,)), sem, sem],
        0,
        in_specs=[smem, VMEM, VMEM, VMEM],
    )
    padded, group, stats2, first_far, last_far = call(
        functools.partial(group_kernel, n),
        (count, first, stats1, live, norm1, mask10, kernel, first_weight, last_weight),
        [
            ((TILES, PAD_ROWS, 128), BF16),
            (wide, F32),
            (stat, F32),
            ((HALF, HALF), BF16),
            ((HALF, HALF), BF16),
        ],
        [consts, local, *bands, DMA((2,)), DMA((2,)), sem, sem],
        1,
        in_specs=[smem] + [VMEM] * 6 + [ANY] * 2,
        out_specs=[VMEM] * 3 + [ANY] * 2,
    )
    small = (TILES, IMGS, 128)
    (
        scaled,
        scaled_far,
        last,
        stats3,
        pooled,
        pooled_far,
        squeezed,
        squeezed_far,
        squeeze_pre,
        excited,
    ) = call(
        functools.partial(gate_kernel, n),
        (
            count,
            group,
            stats2,
            live,
            norm2,
            mask10,
            inverse,
            squeeze_weight,
            squeeze_bias[None],
            excite_weight,
            excite_bias[None],
            mask,
            last_weight,
        ),
        [
            (wide, BF16),
            (wide, BF16),
            (wide, F32),
            (stat, F32),
            (small, F32),
            (small, F32),
            ((IMGS, se), F32),
            ((IMGS, se), F32),
            ((IMGS, se), F32),
            (small, F32),
        ],
        [
            consts,
            local,
            pltpu.VMEM(wide, F32),
            pltpu.VMEM((ROWS, 128), F32),
            DMA((TILES,)),
            DMA((TILES,)),
            DMA((2,)),
            DMA((2,)),
            sem,
            sem,
        ],
        2,
        in_specs=[smem] + [VMEM] * 12,
    )
    block_out, merged_grad, sums3 = call(
        functools.partial(merge_kernel, n),
        (last, stats3, live, norm3, mask, pixels, output_grad),
        [((ROWS, HALF), BF16), (wide, F32), (stat, F32)],
        [consts, local, sem, sem],
        3,
    )
    def vmem(shape, dtype=BF16):
        return pltpu.VMEM(shape, dtype)

    shapes = [part_shape(n, order, 4 * 1024) for order in ORDERS]
    rooms = [Part.room(n, order, shape) for order, shape in zip(ORDERS, shapes)]
    wide_buf = vmem(wide, F32)
    low_buf = vmem(wide)
    weight_buf = vmem((HALF, HALF))
    pre_grad, sums2, excite_grad, squeeze_grad, vectors3, *carry = call(
        functools.partial(last_grad_kernel, n),
        (
            last,
            merged_grad,
            group,
            scaled,
            scaled_far,
            last_weight,
            last_far,
            stats3,
            live,
            norm3,
            sums3,
            mask,
            stats2,
            norm2,
            mask10,
            inverse,
            excited,
            squeeze_pre,
            squeeze_weight,
            excite_weight,
        ),
        [(wide, F32), (stat, F32), (small, F32), ((IMGS, se), F32), vectors]
        + [(rooms[k][1], BF16) for k in range(4)]
        + [(rooms[k][2], BF16) for k in range(2)],
        [
            consts,
            consts,
            local,
            wide_buf,
            wide_buf,
            low_buf,
            low_buf,
            low_buf,
            low_buf,
            weight_buf,
            weight_buf,
            vmem((2 * HALF, se), F32),
            vmem((2 * se, HALF), F32),
            vmem((IMGS, se), F32),
            vmem((IMGS, se), F32),
            vmem((IMGS, HALF), F32),
            vmem((IMGS, HALF), F32),
            vmem(small, F32),
            *(vmem(shape) for shape in shapes),
            *(vmem(room[0]) for room in rooms),
            DMA((8,)),
            DMA((TILES,)),
            DMA((TILES,)),
            DMA((2,)),
            DMA((2,)),
            sem,
            sem,
            *part_sems(n, 4),
        ],
        4,
        in_specs=[ANY] * 7 + [VMEM] * 11 + [ANY] * 2,
        out_specs=[ANY] + [VMEM] * 10,
    )
    mid1, mid3, arrive1 = carry[0:2], carry[2:4], carry[4:6]
    kernel_shapes = [part_shape(n, ORDERS[k], TILES * 256) for k in range(2)]
    first_pre_grad, sums1, vectors2, *carry = call(
        functools.partial(group_grad_kernel, n),
        (
            pre_grad,
            group,
            padded,
            first,
            stats2,
            live,
            norm2,
            sums2,
            mask10,
            kernel,
            stats1,
            norm1,
            *mid1,
            *mid3,
            *arrive1,
        ),
        [(wide, F32), (stat, F32), vectors]
        + [(shape, BF16) for shape in kernel_shapes]
        + [(room[5], BF16) for room in rooms],
        [
            consts,
            consts,
            local,
            wide_buf,
            wide_buf,
            vmem((TILES, PAD_ROWS, 128)),
            vmem((TILES, PAD_ROWS, 128)),
            vmem((512, 9 * 256), F32),
            *bands,
            *(vmem(rooms[k][2]) for k in (2, 3)),
            *(vmem(room[3]) for room in rooms),
            *(vmem(room[4]) for room in rooms),
            DMA((3,)),
            sem,
            sem,
            *part_sems(n, 4),
        ],
        5,
        in_specs=[ANY] * 4 + [VMEM] * 14,
        out_specs=[ANY] + [VMEM] * 8,
    )
    kernel_grads, columns = carry[0:2], carry[2:6]

    def tiles_of(value):
        return jnp.pad(value, ((0, 0), (0, 256 - se))).reshape(IMGS, 2, 128).swapaxes(0, 1)

    factors = jnp.concatenate(
        [
            pooled,
            pooled_far,
            excite_grad,
            tiles_of(squeezed),
            tiles_of(squeezed_far),
            tiles_of(squeeze_grad),
        ]
    )
    count_tiles = factors.shape[0]
    factors = factors.reshape(count_tiles * IMGS, 128).astype(BF16)
    factor_shape = part_extents(n, ORDERS[0]) + factors.shape
    kernel_rooms = [Part.room(n, ORDERS[k], kernel_shapes[k]) for k in range(2)]
    pixels_wide, vectors1, *carry = call(
        functools.partial(first_grad_kernel, n),
        (
            first_pre_grad,
            first,
            pixels,
            pixels_far,
            first_weight,
            first_far,
            merged_grad,
            stats1,
            live,
            norm1,
            sums1,
            mask10,
            factors,
            *kernel_grads,
            *columns,
        ),
        [(wide, F32), vectors]
        + [(shape, BF16) for shape in shapes * 2 + kernel_shapes]
        + [(factor_shape, BF16)],
        [
            consts,
            wide_buf,
            wide_buf,
            low_buf,
            low_buf,
            vmem((ROWS, HALF)),
            vmem((ROWS, HALF)),
            weight_buf,
            weight_buf,
            vmem((ROWS, 128), F32),
            *(vmem(shape) for shape in shapes),
            *(vmem(shape) for room in rooms for shape in room),
            *(vmem(shape) for room in kernel_rooms for shape in room),
            vmem(factor_shape[2:]),
            DMA((6,)),
            DMA((TILES,)),
            DMA((TILES,)),
            *part_sems(n, 11),
        ],
        6,
        in_specs=[ANY] * 7 + [VMEM] * 12,
        out_specs=[ANY, VMEM] + [ANY] * 11,
    )
    sums = [s.reshape(4, 1024, 128) for s in carry[0:8]]
    kernel_sums = [s.reshape(TILES, 256, 128) for s in carry[8:10]]
    late = pl.BlockSpec((1, 1024, 128), lambda j: (jnp.maximum(j - 4, 0), 0, 0))
    early = pl.BlockSpec((1, 1024, 128), lambda j: (jnp.minimum(j, 3), 0, 0))
    last_weight_grad, first_weight_grad, pixels_grad = call(
        spread_kernel,
        (*sums, pixels_wide),
        [((2 * HALF, HALF), F32), ((2 * HALF, HALF), F32), ((ROWS, HALF), F32)],
        [],
        in_specs=[early, early, late, late] * 2 + [pl.BlockSpec((1, ROWS, 128), lambda j: (j, 0, 0))],
        out_specs=[
            pl.BlockSpec((2 * HALF, 128), lambda j: (0, j)),
            pl.BlockSpec((2 * HALF, 128), lambda j: (0, j)),
            pl.BlockSpec((ROWS, 128), lambda j: (0, j)),
        ],
        grid=(TILES,),
    )
    group_weight_grad, squeeze_weight_grad, squeeze_bias_grad, excite_weight_grad, excite_bias_grad = call(
        finish_kernel,
        (*kernel_sums, carry[10].reshape(n, count_tiles * IMGS, 128)),
        [
            ((9 * GROUP_WIDTH, HALF), F32),
            ((2 * HALF, se), F32),
            ((1, se), F32),
            ((2 * se, HALF), F32),
            ((1, HALF), F32),
        ],
        [],
    )
    group_weight_grad = group_weight_grad.reshape(3, 3, GROUP_WIDTH, HALF)
    squeeze_bias_grad, excite_bias_grad = squeeze_bias_grad[0], excite_bias_grad[0]

    def pair(vector):
        flat = vector.reshape(2, 1024)[:, :HALF]
        return flat[0], flat[1]

    first_gain_grad, first_shift_grad = pair(vectors1)
    group_gain_grad, group_shift_grad = pair(vectors2)
    last_gain_grad, last_shift_grad = pair(vectors3)
    return (
        block_out,
        pixels_grad,
        first_weight_grad,
        first_gain_grad,
        first_shift_grad,
        group_weight_grad,
        group_gain_grad,
        group_shift_grad,
        squeeze_weight_grad,
        squeeze_bias_grad,
        excite_weight_grad,
        excite_bias_grad,
        last_weight_grad,
        last_gain_grad,
        last_shift_grad,
    )


def solution(mesh):
    wide = P("img", "ch")
    matrix, vector = P(None, "ch"), P("ch")
    cube = P(None, None, None, "ch")
    weights = (matrix, vector, vector, cube, vector, vector, matrix, vector, matrix, vector, matrix, vector, vector)
    return jax.shard_map(
        functools.partial(body, mesh.shape["img"]),
        mesh=mesh,
        in_specs=(wide, P(), *weights, wide),
        out_specs=(wide, wide, *weights),
        check_vma=False,
    )
```

```python
import functools

import jax
import jax.numpy as jnp
from jax import lax
from jax.experimental import pallas as pl
from jax.experimental.pallas import tpu as pltpu
from jax.sharding import PartitionSpec as P


GROUP_WIDTH = 56
ROWS_IMG = 188
BIG_ROWS = 98
IMGS = 8
ROWS = IMGS * ROWS_IMG
HALF = 1008
TILES = 8
LAST = HALF - 7 * 128
EPSILON = 1e-05
F32 = jnp.float32
BF16 = jnp.bfloat16
MESH = pl.DeviceIdType.MESH
VMEM = pl.BlockSpec(memory_space=pltpu.VMEM)
ANY = pl.BlockSpec(memory_space=pl.ANY)
VMEM_LIMIT = 60 * 1024 * 1024
SPANS = ((0, 256), (256, 512), (512, 768), (768, 1008))
WINDOWS = ((0, 3), (1, 5), (3, 7), (5, 8))
BIG_PAD = 73 * 16
PAD_ROWS = BIG_PAD + 21 * 80
TAPS = tuple((dy, dx) for dy in (-1, 0, 1) for dx in (-1, 0, 1))
DMA = pltpu.SemaphoreType.DMA


def big_place(y, x):
    return (1 + (y + 1) * 8 + x) * 16


def small_place(y, x):
    return BIG_PAD + (1 + (y + 1) * 4 + x) * 80


def natural_row(tile):
    if tile < BIG_ROWS:
        return (tile % 2) * 49 + tile // 2
    tile = tile - BIG_ROWS
    return BIG_ROWS + (tile % 10) * 9 + tile // 10


def padded_row(tile):
    if tile < BIG_ROWS:
        pixel = tile // 2
        return big_place(pixel // 7, pixel % 7) + (tile % 2) * 8
    tile = tile - BIG_ROWS
    pixel = tile // 10
    return small_place(pixel // 3, pixel % 3) + (tile % 10) * 8


REAL_ROWS = frozenset(padded_row(tile) for tile in range(0, ROWS_IMG, 2))
ZERO_ROWS = tuple(row for row in range(0, PAD_ROWS, 16) if row not in REAL_ROWS)


def sigmoid(v):
    return 0.5 + 0.5 * jnp.tanh(0.5 * v)


def slope_of(v, s):
    return s * (1.0 + v * (1.0 - s))


def dot(a, b, dims=((1,), (0,)), **kw):
    return lax.dot_general(a, b, (dims, ((), ())), preferred_element_type=F32, **kw)


def for_each(count, step):
    if count <= 16:
        for index in range(count):
            step(index)
    else:
        lax.fori_loop(0, count, lambda index, _: (step(index), 0)[1], 0)


def for_tiles(step):
    lax.fori_loop(0, TILES, lambda j, _: (step(j), 0)[1], 0)


def for_ragged_tiles(step):
    def full(j, _):
        step(j, pl.ds(pl.multiple_of(j * 128, 128), 128), 128)
        return 0

    lax.fori_loop(0, TILES - 1, full, 0)
    step(TILES - 1, pl.ds(7 * 128, LAST), LAST)


def greet(n, all_images=True, partner=True):
    barrier = pltpu.get_barrier_semaphore()
    me = lax.axis_index("img")
    count = 0
    if all_images:
        for_each(
            n - 1,
            lambda d: pl.semaphore_signal(
                barrier, 1, device_id={"img": lax.rem(me + d + 1, n)}, device_id_type=MESH
            ),
        )
        count += n - 1
    if partner:
        pl.semaphore_signal(
            barrier, 1, device_id={"ch": 1 - lax.axis_index("ch")}, device_id_type=MESH
        )
        count += 1
    return lambda: pl.semaphore_wait(barrier, count)


class Gather:
    def __init__(self, n, source, target, send, recv):
        self.n, self.source, self.target, self.send, self.recv = n, source, target, send, recv
        self.me = lax.axis_index("img")

    def copy(self, d):
        return pltpu.make_async_remote_copy(
            src_ref=self.source,
            dst_ref=self.target.at[self.me],
            send_sem=self.send.at[d],
            recv_sem=self.recv.at[d],
            device_id={"img": lax.rem(self.me + d + 1, self.n)},
            device_id_type=MESH,
        )

    def start(self):
        for_each(self.n - 1, lambda d: self.copy(d).start())
        self.target[self.me] = self.source[...]

    def wait(self):
        for_each(self.n - 1, lambda d: self.copy(d).wait())


def swap(source, target, send, recv):
    return pltpu.make_async_remote_copy(
        src_ref=source,
        dst_ref=target,
        send_sem=send,
        recv_sem=recv,
        device_id={"ch": 1 - lax.axis_index("ch")},
        device_id_type=MESH,
    )


def put_span(ref, span, rows, value, add=False):
    left, right = value[:, :128], value[:, 128:]
    width = right.shape[1]
    if add:
        ref[2 * span, rows, :] += left
        ref[2 * span + 1, rows, 0:width] += right
    else:
        ref[2 * span, rows, :] = left
        ref[2 * span + 1, rows, 0:width] = right


def norm_constants(n, stats, live, gain_shift, consts):
    def total(step):
        return lax.fori_loop(0, n, lambda i, acc: acc + step(i), jnp.zeros((TILES, 128), F32))

    number = total(lambda i: live[i])
    average = total(lambda i: live[i] * stats[i, 0]) / number

    def centred(i):
        off = stats[i, 0] - average
        return stats[i, 1] + live[i] * off * off

    variance = total(centred) / number
    consts[0] = average
    consts[1] = lax.rsqrt(variance + EPSILON)
    consts[2] = gain_shift[0]
    consts[3] = gain_shift[1]
    consts[4] = number


def back_constants(n, sums, consts, grads):
    shift_grad = lax.fori_loop(
        0, n, lambda i, acc: acc + sums[i, 0], jnp.zeros((TILES, 128), F32)
    )
    gain_grad = lax.fori_loop(
        0, n, lambda i, acc: acc + sums[i, 1], jnp.zeros((TILES, 128), F32)
    )
    grads[0] = gain_grad
    grads[1] = shift_grad
    consts[5] = shift_grad / consts[4]
    consts[6] = gain_grad / consts[4]
    consts[7] = consts[1] * consts[2]


def row_of(consts, k, j):
    return consts[k, pl.ds(j, 1), :]


def natural_stats(ref, mask, count, local):
    def step(j):
        x = ref[j]
        m = mask[...]
        average = jnp.sum(x * m, axis=0, keepdims=True) / count
        off = x - average
        local[0, pl.ds(j, 1), :] = average
        local[1, pl.ds(j, 1), :] = jnp.sum(m * off * off, axis=0, keepdims=True)

    for_tiles(step)


def crop_sum(value, mask10):
    big = jnp.sum(value[:BIG_ROWS], axis=0)
    small = jnp.sum(value[BIG_ROWS:].reshape(9, 10, IMGS, 128), axis=0)
    return big + jnp.sum(small * mask10[...], axis=0)


def crop_stats(ref, mask10, count, local):
    def step(j):
        x = ref[j].reshape(ROWS_IMG, IMGS, 128)
        average = jnp.sum(crop_sum(x, mask10), axis=0, keepdims=True) / count
        off = x - average[None]
        local[0, pl.ds(j, 1), :] = average
        local[1, pl.ds(j, 1), :] = jnp.sum(crop_sum(off * off, mask10), axis=0, keepdims=True)

    for_tiles(step)


def window(ref, tiles, dy, dx, big):
    pieces = []
    for y in range(7 if big else 3):
        start = big_place(y + dy, dx) if big else small_place(y + dy, dx)
        rows = slice(start, start + (112 if big else 240))
        pieces.append(jnp.concatenate([ref[t, rows, :] for t in tiles], axis=1))
    return jnp.concatenate(pieces, axis=0)


def build_bands(kernel, bands):
    for span, (first, end) in enumerate(WINDOWS):
        base = first * 128
        depth = (end - first) * 128
        lane = lax.broadcasted_iota(jnp.int32, (GROUP_WIDTH, 256), 1) + span * 256
        groups = range(span * 256 // GROUP_WIDTH, min(18, (span * 256 + 255) // GROUP_WIDTH + 1))
        masks = [
            (lane >= g * GROUP_WIDTH) & (lane < (g + 1) * GROUP_WIDTH) for g in groups
        ]
        head = groups[0] * GROUP_WIDTH - base
        tail = depth - head - len(groups) * GROUP_WIDTH
        for tap in range(9):
            piece = kernel[
                tap * GROUP_WIDTH : (tap + 1) * GROUP_WIDTH, span * 256 : span * 256 + 256
            ]
            parts = [jnp.where(m, piece, 0.0) for m in masks]
            if head:
                parts.insert(0, jnp.zeros((head, 256), F32))
            if tail:
                parts.append(jnp.zeros((tail, 256), F32))
            bands[span][:, tap * 256 : tap * 256 + 256] = jnp.concatenate(parts, axis=0).astype(
                BF16
            )


def zero_pads(ref, j):
    for row in ZERO_ROWS:
        ref[j, row : row + 16, :] = jnp.zeros((16, 128), BF16)


def halves(value):
    high = value.astype(BF16)
    return high, (value - high.astype(F32)).astype(BF16)


def fine_dot(left, right_high, right_low, dims=((1,), (0,))):
    high, low = halves(left)
    both = jnp.concatenate([high.astype(F32), low.astype(F32)], axis=0).astype(BF16)
    value = dot(both, right_high, dims)
    return value[:IMGS] + value[IMGS:] + dot(both, right_low, dims)[:IMGS]


def load_vectors(vectors, first, norm):
    norm[...] = jnp.zeros_like(norm)
    for k in range(2):
        for j in range(TILES):
            width = 128 if j < 7 else LAST
            norm[k, j : j + 1, 0:width] = vectors[
                first + k : first + k + 1, j * 128 : j * 128 + width
            ]


def live_slots(counts, mask10):
    for slot in range(10):
        mask10[slot] = (counts[...] > slot).astype(F32)


def natural_mask(mask10, mask):
    for tile in range(ROWS_IMG):
        there = pl.ds(natural_row(tile), IMGS, stride=ROWS_IMG)
        if tile < BIG_ROWS:
            mask[there, :] = jnp.ones((IMGS, 128), F32)
        else:
            mask[there, :] = mask10[(tile - BIG_ROWS) % 10]


def forward_kernel(n, *refs):
    r = Refs(refs)
    pixels_any, weight1_any, weight3_any, kernel_any, squeeze_any, excite_any, output_any = r.take(7)
    counts, live, vectors, squeeze_b, excite_b = r.take(5)
    first_out, far_out, padded_out, group_out, scaled_out, scaled_far_out = r.take(6)
    last_out, merged_out, block_out = r.take(3)
    far1, far3 = r.take(2)
    split_outs = r.take(4)
    stats1, stats2, stats3, sums3 = r.take(4)
    pooled, pooled_far, squeezed, squeezed_far, squeeze_pre, excited = r.take(6)
    consts, norm, local, buf_a, buf_b, pixels, far, weight, zone = r.take(9)
    kernel_low, kernel, squeeze_w, excite_w = r.take(4)
    splits = r.take(4)
    turned, mask, mask10 = r.take(3)
    bands = r.take(4)
    load, store, swap_s, swap_r, tile_s, tile_r, small_s, small_r = r.take(8)
    gathers = [r.take(2) for _ in range(4)]
    ch = lax.axis_index("ch")
    wait_all = greet(n)
    loads = [
        fetch(source, target, load.at[k])
        for k, (source, target) in enumerate(
            (
                (pixels_any, pixels),
                (weight1_any, weight),
                (kernel_any, kernel_low),
                (squeeze_any, squeeze_w),
                (excite_any, excite_w),
            )
        )
    ]
    own = pl.multiple_of(ch * HALF, 16)
    away = pl.multiple_of((1 - ch) * HALF, 16)
    live_slots(counts, mask10)
    natural_mask(mask10, mask)
    count = live[lax.axis_index("img")][0:1, :]
    wait_all()
    chunks = ((0, 384), (384, 384), (768, 384), (1152, 352))
    swaps = []
    for k, (start, size) in enumerate(chunks):
        rows = pl.ds(start, size)
        swaps.append(swap(pixels_any.at[rows], far.at[rows], swap_s.at[k], swap_r.at[k]))
        swaps[-1].start()
    loads[0].wait()
    loads[1].wait()
    for t, (a, b) in enumerate(SPANS):
        put_span(buf_a, t, slice(0, ROWS), dot(pixels[...], weight[pl.ds(own, HALF), a:b]))
    buf_a[7, :, LAST:128] = jnp.zeros((ROWS, 128 - LAST), F32)
    for k, (start, size) in enumerate(chunks):
        swaps[k].wait()
        rows = slice(start, start + size)
        for t, (a, b) in enumerate(SPANS):
            put_span(buf_a, t, rows, dot(far[rows, :], weight[pl.ds(away, HALF), a:b]), add=True)
    natural_stats(buf_a, mask, count, local)
    gather = Gather(n, local, stats1, *gathers[0])
    gather.start()
    weight_swaps = [
        swap(w.at[pl.ds(away, HALF)], f, swap_s.at[4 + k], swap_r.at[4 + k])
        for k, (w, f) in enumerate(((weight1_any, far1), (weight3_any, far3)))
    ]
    for s in weight_swaps:
        s.start()
    load_weight = fetch(weight3_any, weight, load.at[0])
    store_far = fetch(far, far_out, store.at[0])
    stores = []
    store_first = fetch(buf_a, first_out, store.at[1])
    loads[2].wait()
    kernel[:, 0:HALF] = kernel_low[...].astype(F32)
    kernel[:, HALF:1024] = jnp.zeros((9 * GROUP_WIDTH, 1024 - HALF), F32)
    build_bands(kernel, bands)
    loads[3].wait()
    loads[4].wait()
    for k, w in enumerate((squeeze_w, excite_w)):
        splits[2 * k][...], splits[2 * k + 1][...] = halves(w[...])
    stores += [fetch(splits[k], split_outs[k], store.at[2 + k]) for k in range(4)]
    load_vectors(vectors, 0, norm)
    gather.wait()
    norm_constants(n, stats1, live, norm, consts)

    def activate_first(j):
        average = row_of(consts, 0, j)
        scale = row_of(consts, 1, j) * row_of(consts, 2, j)
        shift = row_of(consts, 3, j)
        zero_pads(zone, j)
        for tile in range(0, ROWS_IMG, 2):
            both = []
            for half in range(2):
                x = buf_a[j, pl.ds(natural_row(tile + half), IMGS, stride=ROWS_IMG), :]
                pre = (x - average) * scale + shift
                both.append(pre * sigmoid(pre))
            row = padded_row(tile)
            zone[j, row : row + 16, :] = jnp.concatenate(both, axis=0).astype(BF16)

    for_tiles(activate_first)
    store_padded = fetch(zone.at[:, pl.ds(0, PAD_ROWS)], padded_out, store.at[6])
    for span, (start, end) in enumerate(WINDOWS):
        tiles = range(start, end)
        right = jnp.concatenate(
            [bands[span][:, tap * 256 : tap * 256 + 256] for tap in range(9)], axis=0
        )
        for big in (True, False):
            left = jnp.concatenate([window(zone, tiles, dy, dx, big) for dy, dx in TAPS], axis=1)
            rows = slice(0, 784) if big else slice(784, ROWS)
            put_span(buf_b, span, rows, dot(left, right))
    crop_stats(buf_b, mask10, count, local)
    gather = Gather(n, local, stats2, *gathers[1])
    gather.start()
    store_group = fetch(buf_b, group_out, store.at[7])
    load_vectors(vectors, 2, norm)
    store_first.wait()
    store_padded.wait()
    store_far.wait()
    load_output = fetch(output_any, far, load.at[1])
    gather.wait()
    norm_constants(n, stats2, live, norm, consts)
    inverse = 1.0 / (BIG_ROWS + 9.0 * counts[...].astype(F32))

    def activate_group(j):
        average = row_of(consts, 0, j)
        scale = row_of(consts, 1, j) * row_of(consts, 2, j)
        pre = (buf_b[j] - average) * scale + row_of(consts, 3, j)
        value = pre * sigmoid(pre)
        buf_a[j] = value
        pooled[j] = crop_sum(value.reshape(ROWS_IMG, IMGS, 128), mask10) * inverse

    for_tiles(activate_group)
    pool_swap = swap(pooled, pooled_far, small_s.at[0], small_r.at[0])
    pool_swap.start()
    pool_swap.wait()
    mine = jnp.concatenate([pooled[j] for j in range(TILES)], axis=1)[:, :HALF]
    theirs = jnp.concatenate([pooled_far[j] for j in range(TILES)], axis=1)[:, :HALF]
    is_low = ch == 0
    high, low = splits[0], splits[1]
    pre = (
        fine_dot(jnp.where(is_low, mine, theirs), high[0:HALF, :], low[0:HALF, :])
        + fine_dot(jnp.where(is_low, theirs, mine), high[HALF:, :], low[HALF:, :])
        + squeeze_b[...]
    )
    squeeze_pre[...] = pre
    squeezed[...] = pre * sigmoid(pre)
    squeeze_swap = swap(squeezed, squeezed_far, small_s.at[1], small_r.at[1])
    squeeze_swap.start()
    squeeze_swap.wait()
    mine, theirs = squeezed[...], squeezed_far[...]
    width = mine.shape[1]
    high, low = splits[2], splits[3]
    gate = sigmoid(
        fine_dot(jnp.where(is_low, mine, theirs), high[0:width, :], low[0:width, :])
        + fine_dot(jnp.where(is_low, theirs, mine), high[width:, :], low[width:, :])
        + excite_b[...]
    )
    excited[7] = jnp.zeros((IMGS, 128), F32)
    for j in range(TILES - 1):
        excited[j] = gate[:, j * 128 : j * 128 + 128]
    excited[7, :, 0:LAST] = gate[:, 7 * 128 :]
    mine_rows, far_rows = pl.ds(0, ROWS), pl.ds(ROWS, ROWS)

    def tile_swap(j):
        return swap(zone.at[j, mine_rows], zone.at[j, far_rows], tile_s.at[j], tile_r.at[j])

    def apply(j):
        gate_j = excited[j]
        for tile in range(ROWS_IMG):
            turned[pl.ds(natural_row(tile), IMGS, stride=ROWS_IMG), :] = (
                buf_a[j, tile * 8 : tile * 8 + 8, :] * gate_j
            )
        zone[j, 0:ROWS, :] = turned[...].astype(BF16)
        tile_swap(j).start()

    for_tiles(apply)
    stores.append(fetch(zone.at[:, mine_rows], scaled_out, store.at[8]))
    load_weight.wait()
    store_group.wait()
    for t, (a, b) in enumerate(SPANS):
        left = jnp.concatenate([zone[j, 0:ROWS, :] for j in range(TILES)], axis=1)[:, :HALF]
        put_span(buf_b, t, slice(0, ROWS), dot(left, weight[pl.ds(own, HALF), a:b]))
    buf_b[7, :, LAST:128] = jnp.zeros((ROWS, 128 - LAST), F32)
    for_tiles(lambda j: tile_swap(j).wait())
    stores.append(fetch(zone.at[:, far_rows], scaled_far_out, store.at[9]))
    for t, (a, b) in enumerate(SPANS):
        left = jnp.concatenate([zone[j, ROWS : 2 * ROWS, :] for j in range(TILES)], axis=1)[:, :HALF]
        put_span(buf_b, t, slice(0, ROWS), dot(left, weight[pl.ds(away, HALF), a:b]), add=True)
    natural_stats(buf_b, mask, count, local)
    gather = Gather(n, local, stats3, *gathers[2])
    gather.start()
    stores.append(fetch(buf_b, last_out, store.at[10]))
    load_vectors(vectors, 4, norm)
    buf_a[7, :, LAST:128] = jnp.zeros((ROWS, 128 - LAST), F32)
    load_output.wait()
    gather.wait()
    norm_constants(n, stats3, live, norm, consts)
    local[...] = jnp.zeros_like(local)

    def merge(j, lanes, width):
        def vec(k):
            return consts[k, pl.ds(j, 1), 0:width]

        m = mask[:, 0:width]
        normed = (buf_b[j, :, 0:width] - vec(0)) * vec(1)
        merged = pixels[:, lanes].astype(F32) + normed * vec(2) + vec(3)
        s = sigmoid(merged)
        grad = far[:, lanes].astype(F32) * m * slope_of(merged, s)
        far[:, lanes] = (merged * s * m).astype(BF16)
        buf_a[j, :, 0:width] = grad
        local[0, pl.ds(j, 1), 0:width] = jnp.sum(grad, axis=0, keepdims=True)
        local[1, pl.ds(j, 1), 0:width] = jnp.sum(grad * normed, axis=0, keepdims=True)

    for_ragged_tiles(merge)
    gather = Gather(n, local, sums3, *gathers[3])
    gather.start()
    stores.append(fetch(buf_a, merged_out, store.at[11]))
    stores.append(fetch(far, block_out, store.at[12]))
    for s in weight_swaps + stores:
        s.wait()
    gather.wait()


def part_extents(n, order):
    sizes = image_axes(n)
    return tuple(sizes[a] for a in order)


def part_shape(n, order, rows):
    return part_extents(n, order) + (rows // n, 128)


def put_blocks(target, tile, tile_rows, start, value):
    _, e1, e2, rows, _ = target.shape
    size = value.shape[0]
    first = start
    while first < start + size:
        block = tile * (tile_rows // rows) + first // rows
        inside = first % rows
        take = min(rows - inside, start + size - first)
        place = (block // (e1 * e2), block // e2 % e1, block % e2)
        target[place[0], place[1], place[2], inside : inside + take, :] = value[
            first - start : first - start + take
        ]
        first += take


def weight_grad(left_span, right_tiles, target, spans):
    for a, b in SPANS:
        left = left_span(a, b)
        for k, span in enumerate(spans):
            right = jnp.concatenate([right_tiles(2 * span), right_tiles(2 * span + 1)], axis=1)
            value = dot(left, right, ((0,), (0,))).astype(BF16)
            put_blocks(target, 2 * k, 1024, a, value[:, :128])
            put_blocks(target, 2 * k + 1, 1024, a, value[:, 128:])


def tile_span(ref):
    def span(a, b):
        tiles = range(a // 128, (b + 127) // 128)
        return jnp.concatenate([ref[t] for t in tiles], axis=1)[:, : b - a]

    return span


def image_axes(n):
    return {16: (2, 2, 4), 128: (8, 4, 4)}.get(n, (n, 1, 1))


class Part:
    def __init__(self, n, order, sems):
        sizes = image_axes(n)
        strides = (1, sizes[0], sizes[0] * sizes[1])
        self.me = lax.axis_index("img")
        self.sizes = [sizes[a] for a in order]
        self.strides = [strides[a] for a in order]
        self.place = [lax.rem(self.me // s, e) for s, e in zip(self.strides, self.sizes)]
        self.sems = sems
        self.live = []

    def send(self, axis, stage, source, target):
        for d in range(1, self.sizes[axis]):
            q = lax.rem(self.place[axis] + d, self.sizes[axis])
            peer = self.me + (q - self.place[axis]) * self.strides[axis]
            copy = pltpu.make_async_remote_copy(
                src_ref=source(q),
                dst_ref=target(d),
                send_sem=self.sems[0].at[stage, d],
                recv_sem=self.sems[1].at[stage, d],
                device_id={"img": peer},
                device_id_type=MESH,
            )
            copy.start()
            self.live.append(copy)

    def keep(self, source, target, stage):
        copy = pltpu.make_async_copy(source, target, self.sems[0].at[stage, 0])
        copy.start()
        self.live.append(copy)

    def settle(self):
        for copy in self.live:
            copy.wait()
        self.live = []

    def add(self, target, own, arrived):
        total = own[...].astype(F32)
        for block in arrived:
            total = total + block[...].astype(F32)
        target[...] = total.astype(BF16)

    def send0(self, source, r0):
        self.send(0, 0, lambda q: source.at[q], lambda d: r0.at[d - 1])

    def sum0(self, source, r0, a0):
        self.settle()
        for k in range(self.sizes[1]):
            self.add(
                a0.at[k],
                source.at[self.place[0], k],
                [r0.at[d, k] for d in range(self.sizes[0] - 1)],
            )

    def send1(self, a0, r1):
        self.send(1, 1, lambda q: a0.at[q], lambda d: r1.at[d - 1])

    def sum1(self, a0, r1, a1):
        self.settle()
        self.add(a1, a0.at[self.place[1]], [r1.at[d] for d in range(self.sizes[1] - 1)])

    def send2(self, a1, r2):
        self.send(2, 2, lambda q: a1.at[q], lambda d: r2.at[d - 1])

    def sum2(self, a1, r2, column):
        self.settle()
        p2 = self.place[2]
        self.add(column.at[p2], a1.at[p2], [r2.at[d] for d in range(self.sizes[2] - 1)])

    def spread2(self, column):
        block = column.at[self.place[2]]
        self.send(2, 3, lambda q: block, lambda d: block)

    def spread1(self, column, result):
        self.settle()
        block = result.at[self.place[0], self.place[1]]
        self.send(1, 4, lambda q: column, lambda d: block)
        self.keep(column, block, 4)

    def spread0(self, result):
        self.settle()
        block = result.at[self.place[0]]
        self.send(0, 5, lambda q: block, lambda d: block)

    @staticmethod
    def room(n, order, shape):
        e0, e1, e2, rows, lanes = shape
        return (
            (max(e0 - 1, 1), e1, e2, rows, lanes),
            (e1, e2, rows, lanes),
            (max(e1 - 1, 1), e2, rows, lanes),
            (e2, rows, lanes),
            (max(e2 - 1, 1), rows, lanes),
            (e2, rows, lanes),
        )


def part_sems(n, count):
    most = max(image_axes(n))
    return [DMA((6, most)) for _ in range(2 * count)]


def fetch(source, target, sem):
    copy = pltpu.make_async_copy(source, target, sem)
    copy.start()
    return copy


class Refs:
    def __init__(self, refs):
        self.refs = list(refs)

    def take(self, count=None):
        if count is None:
            return self.refs.pop(0)
        head, self.refs = self.refs[:count], self.refs[count:]
        return head


ORDERS = ((0, 1, 2), (1, 0, 2), (0, 1, 2), (1, 0, 2))


def last_grad_kernel(n, *refs):
    r = Refs(refs)
    last_any, merged_any, group_any, scaled_any, scaled_far_any, weight_any, weight_far_any = r.take(7)
    stats3, live, sums3 = r.take(3)
    stats2, counts, vectors_in, excited, squeeze_pre = r.take(5)
    split_anys = r.take(4)
    pre_grad, sums2, excite_grad, squeeze_grad, vectors = r.take(5)
    mid1, mid3 = r.take(2), r.take(2)
    arrive1 = r.take(2)
    consts, consts2, local, buf_a, buf_b, low, low_far, scaled, scaled_far = r.take(9)
    weight, weight_far, norm, mask, mask10 = r.take(5)
    splits = r.take(4)
    terms, terms_in, pool_terms, pool_in, pool_tiles = r.take(5)
    grads, rooms = r.take(4), r.take(4)
    load, swap_s, swap_r, small_s, small_r, send, recv = r.take(7)
    sems = r.take(8)
    ch = lax.axis_index("ch")
    own = pl.multiple_of(ch * HALF, 16)
    wait_all = greet(n)
    loads = [
        fetch(source, target, load.at[k])
        for k, (source, target) in enumerate(
            (
                (last_any, buf_a),
                (merged_any, buf_b),
                (scaled_any, scaled),
                (scaled_far_any, scaled_far),
                (weight_any.at[pl.ds(own, HALF)], weight),
                (weight_far_any, weight_far),
                *zip(split_anys, splits),
            )
        )
    ]
    live_slots(counts, mask10)
    natural_mask(mask10, mask)
    inverse = 1.0 / (BIG_ROWS + 9.0 * counts[...].astype(F32))
    load_vectors(vectors_in, 4, norm)
    norm_constants(n, stats3, live, norm, consts)
    back_constants(n, sums3, consts, vectors)
    load_vectors(vectors_in, 2, norm)
    norm_constants(n, stats2, live, norm, consts2)
    parts = [Part(n, order, sems[2 * k : 2 * k + 2]) for k, order in enumerate(ORDERS)]
    wait_all()
    loads[0].wait()
    loads[1].wait()

    def step(j):
        normed = (buf_a[j] - row_of(consts, 0, j)) * row_of(consts, 1, j)
        inner = buf_b[j] - row_of(consts, 5, j) - normed * row_of(consts, 6, j)
        low[j] = (mask[...] * row_of(consts, 7, j) * inner).astype(BF16)
        swap(low.at[j], low_far.at[j], swap_s.at[j], swap_r.at[j]).start()

    for_tiles(step)
    load_group = fetch(group_any, buf_a, load.at[0])
    for part in range(4):
        if part < 2:
            loads[2 + part].wait()
        left = tile_span((scaled, scaled_far)[part % 2])
        weight_grad(left, lambda t: low[t], grads[part], (0, 1) if part < 2 else (2, 3))
        if part < 2:
            parts[part].send0(grads[part], rooms[part])
    loads[4].wait()
    for t, (a, b) in enumerate(SPANS):
        left = jnp.concatenate([low[j] for j in range(TILES)], axis=1)[:, :HALF]
        put_span(buf_b, t, slice(0, ROWS), dot(left, weight[a:b, :], ((1,), (1,))))
    buf_b[7, :, LAST:128] = jnp.zeros((ROWS, 128 - LAST), F32)
    for_tiles(lambda j: swap(low.at[j], low_far.at[j], swap_s.at[j], swap_r.at[j]).wait())
    loads[5].wait()
    for t, (a, b) in enumerate(SPANS):
        left = jnp.concatenate([low_far[j] for j in range(TILES)], axis=1)[:, :HALF]
        put_span(
            buf_b, t, slice(0, ROWS), dot(left, weight_far[a:b, :], ((1,), (1,))), add=True
        )
    load_group.wait()

    def gate_sum(j):
        average = row_of(consts2, 0, j)
        scale = row_of(consts2, 1, j) * row_of(consts2, 2, j)
        shift = row_of(consts2, 3, j)
        total = jnp.zeros((IMGS, 128), F32)
        for tile in range(ROWS_IMG):
            pre = (buf_a[j, tile * 8 : tile * 8 + 8, :] - average) * scale + shift
            act = pre * sigmoid(pre)
            total = total + act * buf_b[j, pl.ds(natural_row(tile), IMGS, stride=ROWS_IMG), :]
        gate = excited[j]
        excite_grad[j] = total * gate * (1.0 - gate)

    for_tiles(gate_sum)
    for k in range(2):
        parts[k].sum0(grads[k], rooms[k], mid1[k])
        parts[k].send1(mid1[k], arrive1[k])
        parts[k + 2].send0(grads[k + 2], rooms[k + 2])
    wide = jnp.concatenate([excite_grad[j] for j in range(TILES)], axis=1)[:, :HALF]
    width = squeeze_pre.shape[1]
    is_low = ch == 0
    for k in range(6, 10):
        loads[k].wait()
    across = ((1,), (1,))
    high, low_part = splits[2], splits[3]
    part0 = fine_dot(wide, high[0:width, :], low_part[0:width, :], across)
    part1 = fine_dot(wide, high[width:, :], low_part[width:, :], across)
    terms[...] = jnp.where(is_low, part1, part0)
    term_swap = swap(terms, terms_in, small_s.at[0], small_r.at[0])
    term_swap.start()
    term_swap.wait()
    pre = squeeze_pre[...]
    grad = (jnp.where(is_low, part0, part1) + terms_in[...]) * slope_of(pre, sigmoid(pre))
    squeeze_grad[...] = grad
    high, low_part = splits[0], splits[1]
    pool0 = fine_dot(grad, high[0:HALF, :], low_part[0:HALF, :], across)
    pool1 = fine_dot(grad, high[HALF:, :], low_part[HALF:, :], across)
    pool_terms[...] = jnp.where(is_low, pool1, pool0)
    pool_swap = swap(pool_terms, pool_in, small_s.at[1], small_r.at[1])
    pool_swap.start()
    pool_swap.wait()
    pool = jnp.where(is_low, pool0, pool1) + pool_in[...]
    pool_tiles[7, :, LAST:128] = jnp.zeros((IMGS, 128 - LAST), F32)
    for j in range(TILES):
        part = pool[:, j * 128 : min(HALF, j * 128 + 128)]
        pool_tiles[j, :, 0 : part.shape[1]] = part * inverse[:, 0 : part.shape[1]]

    def slopes(j):
        average, scale = row_of(consts2, 0, j), row_of(consts2, 1, j)
        gain, shift = row_of(consts2, 2, j), row_of(consts2, 3, j)
        gate, pooled = excited[j], pool_tiles[j]
        total = jnp.zeros((IMGS, 128), F32)
        total_normed = jnp.zeros((IMGS, 128), F32)
        for tile in range(ROWS_IMG):
            rows = slice(tile * 8, tile * 8 + 8)
            normed = (buf_a[j, rows, :] - average) * scale
            pre = normed * gain + shift
            lead = pooled if tile < BIG_ROWS else pooled * mask10[(tile - BIG_ROWS) % 10]
            act = buf_b[j, pl.ds(natural_row(tile), IMGS, stride=ROWS_IMG), :] * gate + lead
            grad = act * slope_of(pre, sigmoid(pre))
            buf_a[j, rows, :] = grad
            total = total + grad
            total_normed = total_normed + grad * normed
        local[0, pl.ds(j, 1), :] = jnp.sum(total, axis=0, keepdims=True)
        local[1, pl.ds(j, 1), :] = jnp.sum(total_normed, axis=0, keepdims=True)

    for_tiles(slopes)
    gather = Gather(n, local, sums2, send, recv)
    gather.start()
    store = fetch(buf_a, pre_grad, load.at[0])
    gather.wait()
    for k in range(2):
        parts[k].settle()
        parts[k + 2].sum0(grads[k + 2], rooms[k + 2], mid3[k])
    store.wait()


def group_grad_kernel(n, *refs):
    r = Refs(refs)
    pre_any, group_any, padded_any, first_any = r.take(4)
    stats2, live, sums2, counts, vectors_in, kernel_low, stats1 = r.take(7)
    mid1, mid3, arrive1 = r.take(2), r.take(2), r.take(2)
    first_pre_grad, sums1, vectors = r.take(3)
    kernel_grads, kernel_arrive = r.take(2), r.take(2)
    columns = r.take(2)
    last_sums = r.take(2)
    early_columns = r.take(2)
    consts, consts1, norm, mask10, kernel = r.take(5)
    local, buf_a, buf_b, padded_grad, padded, full = r.take(6)
    bands = r.take(4)
    arrive3, a1, r2 = r.take(2), r.take(4), r.take(4)
    load, send, recv = r.take(3)
    sems = r.take(12)
    wait_all = greet(n, partner=False)
    columns = early_columns + columns
    loads = [
        fetch(source, target, load.at[k])
        for k, (source, target) in enumerate(
            ((pre_any, buf_a), (group_any, buf_b), (padded_any, padded))
        )
    ]
    parts = [Part(n, order, sems[2 * k : 2 * k + 2]) for k, order in enumerate(ORDERS)]
    kernels = [Part(n, ORDERS[k], sems[8 + 2 * k : 10 + 2 * k]) for k in range(2)]
    live_slots(counts, mask10)
    load_vectors(vectors_in, 2, norm)
    norm_constants(n, stats2, live, norm, consts)
    back_constants(n, sums2, consts, vectors)
    load_vectors(vectors_in, 0, norm)
    norm_constants(n, stats1, live, norm, consts1)
    wait_all()
    for k in range(2):
        parts[k].sum1(mid1[k], arrive1[k], a1[k])
        parts[k].send2(a1[k], r2[k])
        parts[k + 2].send1(mid3[k], arrive3[k])
    kernel[:, 0:HALF] = kernel_low[...].astype(F32)
    kernel[:, HALF:1024] = jnp.zeros((9 * GROUP_WIDTH, 1024 - HALF), F32)
    build_bands(kernel, bands)
    loads[0].wait()
    loads[1].wait()

    def step(j):
        average, scale = row_of(consts, 0, j), row_of(consts, 1, j)
        less, slope, front = row_of(consts, 5, j), row_of(consts, 6, j), row_of(consts, 7, j)
        zero_pads(padded_grad, j)
        for tile in range(0, ROWS_IMG, 2):
            both = []
            for half in range(2):
                rows = slice(tile * 8 + half * 8, tile * 8 + half * 8 + 8)
                normed = (buf_b[j, rows, :] - average) * scale
                grad = front * (buf_a[j, rows, :] - less - normed * slope)
                if tile >= BIG_ROWS:
                    grad = grad * mask10[(tile + half - BIG_ROWS) % 10]
                both.append(grad)
            row = padded_row(tile)
            padded_grad[j, row : row + 16, :] = jnp.concatenate(both, axis=0).astype(BF16)

    for_tiles(step)
    load_first = fetch(first_any, buf_b, load.at[0])
    loads[2].wait()

    for k in range(2):
        parts[k].sum2(a1[k], r2[k], columns[k])
        parts[k].spread2(columns[k])

    def advance(span):
        if span == 0:
            for k in range(2, 4):
                parts[k].sum1(mid3[k - 2], arrive3[k - 2], a1[k])
                parts[k].send2(a1[k], r2[k])
        elif span == 1:
            for k in range(2):
                parts[k].spread1(columns[k], last_sums[k])
        elif span == 2:
            for k in range(2):
                parts[k].spread0(last_sums[k])
            for k in range(2, 4):
                parts[k].sum2(a1[k], r2[k], columns[k])
                parts[k].spread2(columns[k])
        else:
            for k in range(2):
                kernels[k].send0(kernel_grads[k], kernel_arrive[k])

    started = 0
    for span, (start, end) in enumerate(WINDOWS):
        tiles = (2 * span, 2 * span + 1)
        shifted = [
            jnp.concatenate([window(padded_grad, tiles, -dy, -dx, big) for dy, dx in TAPS], axis=1)
            for big in (True, False)
        ]
        for rows, left in ((slice(0, 784), shifted[0]), (slice(784, ROWS), shifted[1])):
            value = dot(left, bands[span][...], ((1,), (1,)))
            for t in range(start, end):
                part = value[:, (t - start) * 128 : (t - start) * 128 + 128]
                if t < started:
                    buf_a[t, rows, :] += part
                else:
                    buf_a[t, rows, :] = part
        started = end
        right = jnp.concatenate(shifted, axis=0)
        for t in range(start, end, 2):
            pair = range(t, min(t + 2, end))
            left = jnp.concatenate([window(padded, pair, 0, 0, big) for big in (True, False)], axis=0)
            base = (t - start) * 128
            full[base : base + 128 * len(pair), :] = dot(left, right, ((0,), (0,)))
        lane = lax.broadcasted_iota(jnp.int32, (GROUP_WIDTH, 256), 1) + span * 256
        pieces = []
        for tap in range(9):
            piece = jnp.zeros((GROUP_WIDTH, 256), F32)
            for g in range(span * 256 // GROUP_WIDTH, min(18, (span * 256 + 255) // GROUP_WIDTH + 1)):
                row = g * GROUP_WIDTH - start * 128
                inside = (lane >= g * GROUP_WIDTH) & (lane < (g + 1) * GROUP_WIDTH)
                block = full[row : row + GROUP_WIDTH, tap * 256 : tap * 256 + 256]
                piece = jnp.where(inside, block, piece)
            pieces.append(piece)
        pieces.append(jnp.zeros((8, 256), F32))
        value = jnp.concatenate(pieces, axis=0).astype(BF16)
        for half in range(2):
            rows = slice(half * 256, half * 256 + 256)
            put_blocks(kernel_grads[half], 2 * span, 256, 0, value[rows, :128])
            put_blocks(kernel_grads[half], 2 * span + 1, 256, 0, value[rows, 128:])
        advance(span)
    load_first.wait()

    def slopes(j):
        average, scale = row_of(consts1, 0, j), row_of(consts1, 1, j)
        gain, shift = row_of(consts1, 2, j), row_of(consts1, 3, j)
        total = jnp.zeros((IMGS, 128), F32)
        total_normed = jnp.zeros((IMGS, 128), F32)
        for tile in range(ROWS_IMG):
            rows = slice(tile * 8, tile * 8 + 8)
            x = buf_b[j, pl.ds(natural_row(tile), IMGS, stride=ROWS_IMG), :]
            normed = (x - average) * scale
            pre = normed * gain + shift
            grad = buf_a[j, rows, :] * slope_of(pre, sigmoid(pre))
            if tile >= BIG_ROWS:
                grad = grad * mask10[(tile - BIG_ROWS) % 10]
            buf_a[j, rows, :] = grad
            total = total + grad
            total_normed = total_normed + grad * normed
        local[0, pl.ds(j, 1), :] = jnp.sum(total, axis=0, keepdims=True)
        local[1, pl.ds(j, 1), :] = jnp.sum(total_normed, axis=0, keepdims=True)

    for_tiles(slopes)
    gather = Gather(n, local, sums1, send, recv)
    gather.start()
    store = fetch(buf_a, first_pre_grad, load.at[0])
    gather.wait()
    for part in parts + kernels:
        part.settle()
    store.wait()


def first_grad_kernel(n, *refs):
    r = Refs(refs)
    pre_any, first_any, pixels_any, pixels_far_any, weight_any, weight_far_any, merged_any = r.take(7)
    stats1, live, sums1, counts, vectors_in, factors = r.take(6)
    kernel_grads, kernel_arrive, columns = r.take(2), r.take(2), r.take(2)
    pixels_grad, vectors = r.take(2)
    last_sums, first_sums, kernel_sums = r.take(2), r.take(4), r.take(2)
    factor_sums = r.take()
    consts, norm, mask10 = r.take(3)
    buf_a, buf_b, low, low_far, pixels, pixels_far, weight, weight_far, turned = r.take(9)
    grads = r.take(4)
    first_rooms = [r.take(6) for _ in range(4)]
    kernel_rooms = [r.take(5) for _ in range(2)]
    factor_column = r.take()
    load, swap_s, swap_r = r.take(3)
    sems = [r.take(2) for _ in range(9)]
    own = pl.multiple_of(lax.axis_index("ch") * HALF, 16)
    wait_all = greet(n)
    loads = [
        fetch(source, target, load.at[k])
        for k, (source, target) in enumerate(
            (
                (pre_any, buf_a),
                (first_any, buf_b),
                (pixels_any, pixels),
                (pixels_far_any, pixels_far),
                (weight_any.at[pl.ds(own, HALF)], weight),
                (weight_far_any, weight_far),
            )
        )
    ]
    firsts = [Part(n, order, sems[k]) for k, order in enumerate(ORDERS)]
    lasts = [Part(n, ORDERS[2 + k], sems[4 + k]) for k in range(2)]
    kernels = [Part(n, ORDERS[k], sems[6 + k]) for k in range(2)]
    factor = Part(n, ORDERS[0], sems[8])
    live_slots(counts, mask10)
    load_vectors(vectors_in, 0, norm)
    norm_constants(n, stats1, live, norm, consts)
    back_constants(n, sums1, consts, vectors)
    wait_all()
    for k in range(2):
        lasts[k].spread1(columns[k], last_sums[k])
        a0, r1, a1, r2, column = kernel_rooms[k]
        kernels[k].sum0(kernel_grads[k], kernel_arrive[k], a0)
        kernels[k].send1(a0, r1)
    factor_column[factor.place[2]] = factors[...]
    factor.spread2(factor_column)
    loads[0].wait()
    loads[1].wait()

    def step(j):
        average, scale = row_of(consts, 0, j), row_of(consts, 1, j)
        less, slope, front = row_of(consts, 5, j), row_of(consts, 6, j), row_of(consts, 7, j)
        for tile in range(ROWS_IMG):
            there = pl.ds(natural_row(tile), IMGS, stride=ROWS_IMG)
            normed = (buf_b[j, there, :] - average) * scale
            grad = front * (buf_a[j, tile * 8 : tile * 8 + 8, :] - less - normed * slope)
            if tile >= BIG_ROWS:
                grad = grad * mask10[(tile - BIG_ROWS) % 10]
            turned[there, :] = grad
        low[j] = turned[...].astype(BF16)
        swap(low.at[j], low_far.at[j], swap_s.at[j], swap_r.at[j]).start()

    for_tiles(step)
    load_merged = fetch(merged_any, buf_a, load.at[0])
    for part in range(4):
        if part < 2:
            loads[2 + part].wait()
        rows = (pixels, pixels_far)[part % 2]
        weight_grad(
            lambda a, b: rows[:, a:b], lambda t: low[t], grads[part], (0, 1) if part < 2 else (2, 3)
        )
        if part < 2:
            firsts[part].send0(grads[part], first_rooms[part][0])
    load_merged.wait()
    loads[4].wait()
    for t, (a, b) in enumerate(SPANS):
        left = jnp.concatenate([low[j] for j in range(TILES)], axis=1)[:, :HALF]
        put_span(buf_a, t, slice(0, ROWS), dot(left, weight[a:b, :], ((1,), (1,))), add=True)
    for k in range(2):
        a0, r1, a1, r2, column = kernel_rooms[k]
        kernels[k].sum1(a0, r1, a1)
        kernels[k].send2(a1, r2)
    for_tiles(lambda j: swap(low.at[j], low_far.at[j], swap_s.at[j], swap_r.at[j]).wait())
    loads[5].wait()
    for t, (a, b) in enumerate(SPANS):
        left = jnp.concatenate([low_far[j] for j in range(TILES)], axis=1)[:, :HALF]
        put_span(buf_a, t, slice(0, ROWS), dot(left, weight_far[a:b, :], ((1,), (1,))), add=True)
    store = fetch(buf_a, pixels_grad, load.at[0])

    def reduce0(k):
        r0, a0, r1, a1, r2, column = first_rooms[k]
        firsts[k].sum0(grads[k], r0, a0)
        firsts[k].send1(a0, r1)

    def reduce1(k):
        r0, a0, r1, a1, r2, column = first_rooms[k]
        firsts[k].sum1(a0, r1, a1)
        firsts[k].send2(a1, r2)

    def reduce2(k):
        r0, a0, r1, a1, r2, column = first_rooms[k]
        firsts[k].sum2(a1, r2, column)
        firsts[k].spread2(column)

    def each(step, ks):
        for k in ks:
            step(k)

    head, tail, two = (0, 1), (2, 3), range(2)
    each(reduce0, head)
    each(lambda k: firsts[k].send0(grads[k], first_rooms[k][0]), tail)
    factor.spread1(factor_column, factor_sums)
    for k in two:
        a0, r1, a1, r2, column = kernel_rooms[k]
        kernels[k].sum2(a1, r2, column)
        kernels[k].spread2(column)
    each(reduce1, head)
    each(reduce0, tail)
    each(lambda k: lasts[k].spread0(last_sums[k]), two)
    factor.spread0(factor_sums)
    each(lambda k: kernels[k].spread1(kernel_rooms[k][4], kernel_sums[k]), two)
    each(reduce2, head)
    each(reduce1, tail)
    each(lambda k: kernels[k].spread0(kernel_sums[k]), two)
    each(lambda k: firsts[k].spread1(first_rooms[k][5], first_sums[k]), head)
    each(reduce2, tail)
    each(lambda k: firsts[k].spread0(first_sums[k]), head)
    each(lambda k: firsts[k].spread1(first_rooms[k][5], first_sums[k]), tail)
    each(lambda k: firsts[k].spread0(first_sums[k]), tail)
    for part in (*firsts, *lasts, *kernels, factor):
        part.settle()
    store.wait()


def spread_kernel(*refs):
    lasts, firsts, pixels_wide = refs[0:4], refs[4:8], refs[8]
    last_out, first_out, pixels_out = refs[9:12]
    ch = lax.axis_index("ch")
    j = pl.program_id(0)
    for sums, out in ((lasts, last_out), (firsts, first_out)):
        for late in range(2):

            @pl.when((j >= 4) == bool(late))
            def _():
                for k, place in ((0, ch), (1, 1 - ch)):
                    rows = pl.ds(pl.multiple_of(place * HALF, 8), HALF)
                    out[rows, :] = sums[2 * late + k][0, 0:HALF, :].astype(F32)

    pixels_out[...] = pixels_wide[0]


def finish_kernel(low_half, high_half, factors, group_out, squeeze_w, squeeze_b, excite_w, excite_b):
    ch = lax.axis_index("ch")
    se = squeeze_w.shape[1]
    split = low_half.shape[1]
    for j in range(TILES):
        width = 128 if j < 7 else LAST
        lanes = slice(j * 128, j * 128 + width)
        group_out[0:split, lanes] = low_half[j, :, 0:width].astype(F32)
        rest = 9 * GROUP_WIDTH - split
        group_out[split:, lanes] = high_half[j, :, 0:width].astype(F32)[:rest]
    n = factors.shape[0]
    whole = factors[...].astype(F32).reshape(n, -1, IMGS, 128)

    def columns(start, tiles, width):
        parts = [whole[:, t].reshape(n * IMGS, 128) for t in range(start, start + tiles)]
        return jnp.concatenate(parts, axis=1)[:, :width]

    excite_all, squeeze_all = columns(16, 8, HALF), columns(28, 2, se)
    squeeze_b[...] = jnp.sum(squeeze_all, axis=0, keepdims=True)
    excite_b[...] = jnp.sum(excite_all, axis=0, keepdims=True)
    excite_all, squeeze_all = excite_all.astype(BF16), squeeze_all.astype(BF16)
    for start, place in ((0, ch), (8, 1 - ch)):
        rows = pl.ds(pl.multiple_of(place * HALF, 8), HALF)
        squeeze_w[rows, :] = dot(columns(start, 8, HALF).astype(BF16), squeeze_all, ((0,), (0,)))
    own, far = columns(24, 2, se), columns(26, 2, se)
    for k, left in enumerate((jnp.where(ch == 0, own, far), jnp.where(ch == 0, far, own))):
        excite_w[k * se : (k + 1) * se, :] = dot(left.astype(BF16), excite_all, ((0,), (0,)))


def call(kernel, ins, outs, scratch, ident=None, in_specs=None, out_specs=None, grid=()):
    params = {"vmem_limit_bytes": VMEM_LIMIT}
    if ident is not None:
        params.update(collective_id=ident, has_side_effects=True)
    return pl.pallas_call(
        kernel,
        grid=grid,
        out_shape=[jax.ShapeDtypeStruct(shape, dtype) for shape, dtype in outs],
        in_specs=in_specs or [VMEM] * len(ins),
        out_specs=out_specs or [VMEM] * len(outs),
        scratch_shapes=scratch,
        compiler_params=pltpu.CompilerParams(**params),
    )(*ins)


def body(
    n,
    pixels,
    crop_counts,
    first_weight,
    first_gain,
    first_shift,
    group_weight,
    group_gain,
    group_shift,
    squeeze_weight,
    squeeze_bias,
    excite_weight,
    excite_bias,
    last_weight,
    last_gain,
    last_shift,
    output_grad,
):
    me = lax.axis_index("img")
    assert pixels.shape == (ROWS, HALF)
    se = squeeze_weight.shape[1]
    wide = (TILES, ROWS, 128)
    stat = (n, 2, TILES, 128)
    sem = DMA((n - 1,))

    local_counts = lax.dynamic_slice_in_dim(crop_counts, me * IMGS, IMGS)
    counts = jnp.broadcast_to(local_counts[:, None], (IMGS, 128))
    live = jnp.sum((BIG_ROWS + 9 * crop_counts).reshape(n, IMGS), axis=1).astype(F32)
    live = jnp.broadcast_to(live[:, None, None], (n, TILES, 128))
    gains = jnp.stack(
        [first_gain, first_shift, group_gain, group_shift, last_gain, last_shift]
    )
    kernel = group_weight.reshape(9 * GROUP_WIDTH, HALF)
    local = pltpu.VMEM((2, TILES, 128), F32)
    consts = pltpu.VMEM((8, TILES, 128), F32)
    vectors = ((2, TILES, 128), F32)
    bands = [pltpu.VMEM(((e - s) * 128, 9 * 256), BF16) for s, e in WINDOWS]
    mask10 = pltpu.VMEM((10, IMGS, 128), F32)
    mask = pltpu.VMEM((ROWS, 128), F32)
    kernel_buf = pltpu.VMEM((9 * GROUP_WIDTH, 1024), F32)
    small = (TILES, IMGS, 128)
    wide_buf = pltpu.VMEM(wide, F32)
    tall = (ROWS, HALF)
    split_shapes = [(2 * HALF, se)] * 2 + [(2 * se, HALF)] * 2
    (
        first,
        pixels_far,
        padded,
        group,
        scaled,
        scaled_far,
        last,
        merged_grad,
        block_out,
        first_far,
        last_far,
        *rest,
    ) = call(
        functools.partial(forward_kernel, n),
        (
            pixels,
            first_weight,
            last_weight,
            kernel,
            squeeze_weight,
            excite_weight,
            output_grad,
            counts,
            live,
            gains,
            squeeze_bias[None],
            excite_bias[None],
        ),
        [
            (wide, F32),
            (tall, BF16),
            ((TILES, PAD_ROWS, 128), BF16),
            (wide, F32),
            (wide, BF16),
            (wide, BF16),
            (wide, F32),
            (wide, F32),
            (tall, BF16),
            ((HALF, HALF), BF16),
            ((HALF, HALF), BF16),
        ]
        + [(shape, BF16) for shape in split_shapes]
        + [(stat, F32)] * 4
        + [(small, F32)] * 2
        + [((IMGS, se), F32)] * 3
        + [(small, F32)],
        [
            consts,
            local,
            local,
            wide_buf,
            wide_buf,
            pltpu.VMEM(tall, BF16),
            pltpu.VMEM(tall, BF16),
            pltpu.VMEM((2 * HALF, HALF), BF16),
            pltpu.VMEM((TILES, 2 * ROWS, 128), BF16),
            pltpu.VMEM((9 * GROUP_WIDTH, HALF), BF16),
            kernel_buf,
            pltpu.VMEM((2 * HALF, se), F32),
            pltpu.VMEM((2 * se, HALF), F32),
            *(pltpu.VMEM(shape, BF16) for shape in split_shapes),
            mask,
            mask,
            mask10,
            *bands,
            DMA((6,)),
            DMA((13,)),
            DMA((6,)),
            DMA((6,)),
            DMA((TILES,)),
            DMA((TILES,)),
            DMA((2,)),
            DMA((2,)),
            *[sem] * 8,
        ],
        0,
        in_specs=[ANY] * 7 + [VMEM] * 5,
        out_specs=[ANY] * 15 + [VMEM] * 10,
    )
    splits, rest = rest[:4], rest[4:]
    stats1, stats2, stats3, sums3, pooled, pooled_far = rest[:6]
    squeezed, squeezed_far, squeeze_pre, excited = rest[6:]

    def vmem(shape, dtype=BF16):
        return pltpu.VMEM(shape, dtype)

    shapes = [part_shape(n, order, 4 * 1024) for order in ORDERS]
    rooms = [Part.room(n, order, shape) for order, shape in zip(ORDERS, shapes)]
    low_buf = vmem(wide)
    weight_buf = vmem((HALF, HALF))
    pre_grad, sums2, excite_grad, squeeze_grad, vectors3, *carry = call(
        functools.partial(last_grad_kernel, n),
        (
            last,
            merged_grad,
            group,
            scaled,
            scaled_far,
            last_weight,
            last_far,
            stats3,
            live,
            sums3,
            stats2,
            counts,
            gains,
            excited,
            squeeze_pre,
            *splits,
        ),
        [(wide, F32), (stat, F32), (small, F32), ((IMGS, se), F32), vectors]
        + [(rooms[k][1], BF16) for k in range(4)]
        + [(rooms[k][2], BF16) for k in range(2)],
        [
            consts,
            consts,
            local,
            wide_buf,
            wide_buf,
            low_buf,
            low_buf,
            low_buf,
            low_buf,
            weight_buf,
            weight_buf,
            local,
            mask,
            mask10,
            *(vmem(shape) for shape in split_shapes),
            vmem((IMGS, se), F32),
            vmem((IMGS, se), F32),
            vmem((IMGS, HALF), F32),
            vmem((IMGS, HALF), F32),
            vmem(small, F32),
            *(vmem(shape) for shape in shapes),
            *(vmem(room[0]) for room in rooms),
            DMA((10,)),
            DMA((TILES,)),
            DMA((TILES,)),
            DMA((2,)),
            DMA((2,)),
            sem,
            sem,
            *part_sems(n, 4),
        ],
        4,
        in_specs=[ANY] * 7 + [VMEM] * 8 + [ANY] * 4,
        out_specs=[ANY] + [VMEM] * 10,
    )
    mid1, mid3, arrive1 = carry[0:2], carry[2:4], carry[4:6]
    kernel_shapes = [part_shape(n, ORDERS[k], TILES * 256) for k in range(2)]
    kernel_rooms = [Part.room(n, ORDERS[k], kernel_shapes[k]) for k in range(2)]
    first_pre_grad, sums1, vectors2, *carry = call(
        functools.partial(group_grad_kernel, n),
        (
            pre_grad,
            group,
            padded,
            first,
            stats2,
            live,
            sums2,
            counts,
            gains,
            kernel,
            stats1,
            *mid1,
            *mid3,
            *arrive1,
        ),
        [(wide, F32), (stat, F32), vectors]
        + [(shape, BF16) for shape in kernel_shapes]
        + [(room[0], BF16) for room in kernel_rooms]
        + [(room[5], BF16) for room in rooms[2:]]
        + [(shape, BF16) for shape in shapes[:2]],
        [
            *(vmem(room[5]) for room in rooms[:2]),
            consts,
            consts,
            local,
            mask10,
            kernel_buf,
            local,
            wide_buf,
            wide_buf,
            vmem((TILES, PAD_ROWS, 128)),
            vmem((TILES, PAD_ROWS, 128)),
            vmem((512, 9 * 256), F32),
            *bands,
            *(vmem(rooms[k][2]) for k in (2, 3)),
            *(vmem(room[3]) for room in rooms),
            *(vmem(room[4]) for room in rooms),
            DMA((3,)),
            sem,
            sem,
            *part_sems(n, 6),
        ],
        5,
        in_specs=[ANY] * 4 + [VMEM] * 13,
        out_specs=[ANY] + [VMEM] * 8 + [ANY] * 2,
    )
    kernel_grads, kernel_arrive, columns, last_early = carry[0:2], carry[2:4], carry[4:6], carry[6:8]

    def tiles_of(value):
        return jnp.pad(value, ((0, 0), (0, 256 - se))).reshape(IMGS, 2, 128).swapaxes(0, 1)

    factors = jnp.concatenate(
        [
            pooled,
            pooled_far,
            excite_grad,
            tiles_of(squeezed),
            tiles_of(squeezed_far),
            tiles_of(squeeze_grad),
        ]
    )
    count_tiles = factors.shape[0]
    factors = factors.reshape(count_tiles * IMGS, 128).astype(BF16)
    factor_shape = part_extents(n, ORDERS[0]) + factors.shape
    pixels_wide, vectors1, *carry = call(
        functools.partial(first_grad_kernel, n),
        (
            first_pre_grad,
            first,
            pixels,
            pixels_far,
            first_weight,
            first_far,
            merged_grad,
            stats1,
            live,
            sums1,
            counts,
            gains,
            factors,
            *kernel_grads,
            *kernel_arrive,
            *columns,
        ),
        [(wide, F32), vectors]
        + [(shape, BF16) for shape in shapes[2:] + shapes + kernel_shapes]
        + [(factor_shape, BF16)],
        [
            consts,
            local,
            mask10,
            wide_buf,
            wide_buf,
            low_buf,
            low_buf,
            vmem((ROWS, HALF)),
            vmem((ROWS, HALF)),
            weight_buf,
            weight_buf,
            vmem((ROWS, 128), F32),
            *(vmem(shape) for shape in shapes),
            *(vmem(shape) for room in rooms for shape in room),
            *(vmem(shape) for room in kernel_rooms for shape in room[1:]),
            vmem(factor_shape[2:]),
            DMA((6,)),
            DMA((TILES,)),
            DMA((TILES,)),
            *part_sems(n, 9),
        ],
        6,
        in_specs=[ANY] * 7 + [VMEM] * 12,
        out_specs=[ANY, VMEM] + [ANY] * 9,
    )
    sums = [s.reshape(4, 1024, 128) for s in (*last_early, *carry[0:6])]
    kernel_sums = [s.reshape(TILES, 256, 128) for s in carry[6:8]]
    late = pl.BlockSpec((1, 1024, 128), lambda j: (jnp.maximum(j - 4, 0), 0, 0))
    early = pl.BlockSpec((1, 1024, 128), lambda j: (jnp.minimum(j, 3), 0, 0))
    last_weight_grad, first_weight_grad, pixels_grad = call(
        spread_kernel,
        (*sums, pixels_wide),
        [((2 * HALF, HALF), F32), ((2 * HALF, HALF), F32), ((ROWS, HALF), F32)],
        [],
        in_specs=[early, early, late, late] * 2 + [pl.BlockSpec((1, ROWS, 128), lambda j: (j, 0, 0))],
        out_specs=[
            pl.BlockSpec((2 * HALF, 128), lambda j: (0, j)),
            pl.BlockSpec((2 * HALF, 128), lambda j: (0, j)),
            pl.BlockSpec((ROWS, 128), lambda j: (0, j)),
        ],
        grid=(TILES,),
    )
    group_weight_grad, squeeze_weight_grad, squeeze_bias_grad, excite_weight_grad, excite_bias_grad = call(
        finish_kernel,
        (*kernel_sums, carry[8].reshape(n, count_tiles * IMGS, 128)),
        [
            ((9 * GROUP_WIDTH, HALF), F32),
            ((2 * HALF, se), F32),
            ((1, se), F32),
            ((2 * se, HALF), F32),
            ((1, HALF), F32),
        ],
        [],
    )
    group_weight_grad = group_weight_grad.reshape(3, 3, GROUP_WIDTH, HALF)
    squeeze_bias_grad, excite_bias_grad = squeeze_bias_grad[0], excite_bias_grad[0]

    def pair(vector):
        flat = vector.reshape(2, 1024)[:, :HALF]
        return flat[0], flat[1]

    first_gain_grad, first_shift_grad = pair(vectors1)
    group_gain_grad, group_shift_grad = pair(vectors2)
    last_gain_grad, last_shift_grad = pair(vectors3)
    return (
        block_out,
        pixels_grad,
        first_weight_grad,
        first_gain_grad,
        first_shift_grad,
        group_weight_grad,
        group_gain_grad,
        group_shift_grad,
        squeeze_weight_grad,
        squeeze_bias_grad,
        excite_weight_grad,
        excite_bias_grad,
        last_weight_grad,
        last_gain_grad,
        last_shift_grad,
    )


def solution(mesh):
    wide = P("img", "ch")
    matrix, vector = P(None, "ch"), P("ch")
    cube = P(None, None, None, "ch")
    weights = (matrix, vector, vector, cube, vector, vector, matrix, vector, matrix, vector, matrix, vector, vector)
    return jax.shard_map(
        functools.partial(body, mesh.shape["img"]),
        mesh=mesh,
        in_specs=(wide, P(), *weights, wide),
        out_specs=(wide, wide, *weights),
        check_vma=False,
    )
```

```python
import functools

import jax
import jax.numpy as jnp
from jax import lax
from jax.experimental import pallas as pl
from jax.experimental.pallas import tpu as pltpu
from jax.sharding import PartitionSpec as P


GROUP_WIDTH = 56
ROWS_IMG = 188
BIG_ROWS = 98
IMGS = 8
ROWS = IMGS * ROWS_IMG
HALF = 1008
TILES = 8
LAST = HALF - 7 * 128
EPSILON = 1e-05
F32 = jnp.float32
BF16 = jnp.bfloat16
MESH = pl.DeviceIdType.MESH
VMEM = pl.BlockSpec(memory_space=pltpu.VMEM)
ANY = pl.BlockSpec(memory_space=pl.ANY)
VMEM_LIMIT = 60 * 1024 * 1024
SPANS = ((0, 256), (256, 512), (512, 768), (768, 1008))
WINDOWS = ((0, 3), (1, 5), (3, 7), (5, 8))
BIG_PAD = 73 * 16
PAD_ROWS = BIG_PAD + 21 * 80
TAPS = tuple((dy, dx) for dy in (-1, 0, 1) for dx in (-1, 0, 1))
DMA = pltpu.SemaphoreType.DMA


def big_place(y, x):
    return (1 + (y + 1) * 8 + x) * 16


def small_place(y, x):
    return BIG_PAD + (1 + (y + 1) * 4 + x) * 80


def natural_row(tile):
    if tile < BIG_ROWS:
        return (tile % 2) * 49 + tile // 2
    tile = tile - BIG_ROWS
    return BIG_ROWS + (tile % 10) * 9 + tile // 10


def padded_row(tile):
    if tile < BIG_ROWS:
        pixel = tile // 2
        return big_place(pixel // 7, pixel % 7) + (tile % 2) * 8
    tile = tile - BIG_ROWS
    pixel = tile // 10
    return small_place(pixel // 3, pixel % 3) + (tile % 10) * 8


REAL_ROWS = frozenset(padded_row(tile) for tile in range(0, ROWS_IMG, 2))
ZERO_ROWS = tuple(row for row in range(0, PAD_ROWS, 16) if row not in REAL_ROWS)


def sigmoid(v):
    return 0.5 + 0.5 * jnp.tanh(0.5 * v)


def slope_of(v, s):
    return s * (1.0 + v * (1.0 - s))


def dot(a, b, dims=((1,), (0,)), **kw):
    return lax.dot_general(a, b, (dims, ((), ())), preferred_element_type=F32, **kw)


def for_each(count, step):
    if count <= 16:
        for index in range(count):
            step(index)
    else:
        lax.fori_loop(0, count, lambda index, _: (step(index), 0)[1], 0)


def for_tiles(step):
    lax.fori_loop(0, TILES, lambda j, _: (step(j), 0)[1], 0)


def for_ragged_tiles(step):
    def full(j, _):
        step(j, pl.ds(pl.multiple_of(j * 128, 128), 128), 128)
        return 0

    lax.fori_loop(0, TILES - 1, full, 0)
    step(TILES - 1, pl.ds(7 * 128, LAST), LAST)


def greet(n, all_images=True, partner=True):
    barrier = pltpu.get_barrier_semaphore()
    me = lax.axis_index("img")
    count = 0
    if all_images:
        for_each(
            n - 1,
            lambda d: pl.semaphore_signal(
                barrier, 1, device_id={"img": lax.rem(me + d + 1, n)}, device_id_type=MESH
            ),
        )
        count += n - 1
    if partner:
        pl.semaphore_signal(
            barrier, 1, device_id={"ch": 1 - lax.axis_index("ch")}, device_id_type=MESH
        )
        count += 1
    return lambda: pl.semaphore_wait(barrier, count)


class Gather:
    def __init__(self, n, source, target, send, recv):
        self.n, self.source, self.target, self.send, self.recv = n, source, target, send, recv
        self.me = lax.axis_index("img")

    def copy(self, d):
        return pltpu.make_async_remote_copy(
            src_ref=self.source,
            dst_ref=self.target.at[self.me],
            send_sem=self.send.at[d],
            recv_sem=self.recv.at[d],
            device_id={"img": lax.rem(self.me + d + 1, self.n)},
            device_id_type=MESH,
        )

    def start(self):
        for_each(self.n - 1, lambda d: self.copy(d).start())
        self.target[self.me] = self.source[...]

    def wait(self):
        for_each(self.n - 1, lambda d: self.copy(d).wait())


def swap(source, target, send, recv):
    return pltpu.make_async_remote_copy(
        src_ref=source,
        dst_ref=target,
        send_sem=send,
        recv_sem=recv,
        device_id={"ch": 1 - lax.axis_index("ch")},
        device_id_type=MESH,
    )


def put_span(ref, span, rows, value, add=False):
    left, right = value[:, :128], value[:, 128:]
    width = right.shape[1]
    if add:
        ref[2 * span, rows, :] += left
        ref[2 * span + 1, rows, 0:width] += right
    else:
        ref[2 * span, rows, :] = left
        ref[2 * span + 1, rows, 0:width] = right


def norm_constants(n, stats, live, gain_shift, consts):
    def total(step):
        return lax.fori_loop(0, n, lambda i, acc: acc + step(i), jnp.zeros((TILES, 128), F32))

    number = total(lambda i: live[i])
    average = total(lambda i: live[i] * stats[i, 0]) / number

    def centred(i):
        off = stats[i, 0] - average
        return stats[i, 1] + live[i] * off * off

    variance = total(centred) / number
    consts[0] = average
    consts[1] = lax.rsqrt(variance + EPSILON)
    consts[2] = gain_shift[0]
    consts[3] = gain_shift[1]
    consts[4] = number


def back_constants(n, sums, consts, grads):
    shift_grad = lax.fori_loop(
        0, n, lambda i, acc: acc + sums[i, 0], jnp.zeros((TILES, 128), F32)
    )
    gain_grad = lax.fori_loop(
        0, n, lambda i, acc: acc + sums[i, 1], jnp.zeros((TILES, 128), F32)
    )
    grads[0] = gain_grad
    grads[1] = shift_grad
    consts[5] = shift_grad / consts[4]
    consts[6] = gain_grad / consts[4]
    consts[7] = consts[1] * consts[2]


def row_of(consts, k, j):
    return consts[k, pl.ds(j, 1), :]


def natural_stats(ref, mask, count, local):
    def step(j):
        x = ref[j]
        m = mask[...]
        average = jnp.sum(x * m, axis=0, keepdims=True) / count
        off = x - average
        local[0, pl.ds(j, 1), :] = average
        local[1, pl.ds(j, 1), :] = jnp.sum(m * off * off, axis=0, keepdims=True)

    for_tiles(step)


def crop_sum(value, mask10):
    big = jnp.sum(value[:BIG_ROWS], axis=0)
    small = jnp.sum(value[BIG_ROWS:].reshape(9, 10, IMGS, 128), axis=0)
    return big + jnp.sum(small * mask10[...], axis=0)


def crop_stats(ref, mask10, count, local):
    def step(j):
        x = ref[j].reshape(ROWS_IMG, IMGS, 128)
        average = jnp.sum(crop_sum(x, mask10), axis=0, keepdims=True) / count
        off = x - average[None]
        local[0, pl.ds(j, 1), :] = average
        local[1, pl.ds(j, 1), :] = jnp.sum(crop_sum(off * off, mask10), axis=0, keepdims=True)

    for_tiles(step)


def window(ref, tiles, dy, dx, big):
    pieces = []
    for y in range(7 if big else 3):
        start = big_place(y + dy, dx) if big else small_place(y + dy, dx)
        rows = slice(start, start + (112 if big else 240))
        pieces.append(jnp.concatenate([ref[t, rows, :] for t in tiles], axis=1))
    return jnp.concatenate(pieces, axis=0)


def span_groups(span):
    return range(span * 256 // GROUP_WIDTH, min(18, (span * 256 + 255) // GROUP_WIDTH + 1))


def span_masks(span):
    lane = lax.broadcasted_iota(jnp.int32, (GROUP_WIDTH, 256), 1) + span * 256
    return [(lane >= g * GROUP_WIDTH) & (lane < (g + 1) * GROUP_WIDTH) for g in span_groups(span)]


def tap_rows(kernel, tap, span):
    first = tap * GROUP_WIDTH
    start = first // 16 * 16
    end = min(9 * GROUP_WIDTH, (first + GROUP_WIDTH + 15) // 16 * 16)
    a, b = SPANS[span]
    piece = kernel[start:end, a:b].astype(F32)[first - start : first - start + GROUP_WIDTH]
    if b - a < 256:
        piece = jnp.concatenate([piece, jnp.zeros((GROUP_WIDTH, 256 - (b - a)), F32)], axis=1)
    return piece


def build_band(kernel, span, band):
    first, end = WINDOWS[span]
    depth = (end - first) * 128
    groups = span_groups(span)
    masks = span_masks(span)
    head = groups[0] * GROUP_WIDTH - first * 128
    tail = depth - head - len(groups) * GROUP_WIDTH
    for tap in range(9):
        piece = tap_rows(kernel, tap, span)
        parts = [jnp.where(m, piece, 0.0) for m in masks]
        if head:
            parts.insert(0, jnp.zeros((head, 256), F32))
        if tail:
            parts.append(jnp.zeros((tail, 256), F32))
        band[0:depth, tap * 256 : tap * 256 + 256] = jnp.concatenate(parts, axis=0).astype(BF16)


def zero_pads(ref, j):
    for row in ZERO_ROWS:
        ref[j, row : row + 16, :] = jnp.zeros((16, 128), BF16)


def halves(value):
    high = value.astype(BF16)
    return high, (value - high.astype(F32)).astype(BF16)


def fine_dot(left, right_high, right_low, dims=((1,), (0,))):
    high, low = halves(left)
    both = jnp.concatenate([high.astype(F32), low.astype(F32)], axis=0).astype(BF16)
    value = dot(both, right_high, dims)
    return value[:IMGS] + value[IMGS:] + dot(both, right_low, dims)[:IMGS]


def load_vectors(vectors, first, norm):
    norm[...] = jnp.zeros_like(norm)
    for k in range(2):
        for j in range(TILES):
            width = 128 if j < 7 else LAST
            norm[k, j : j + 1, 0:width] = vectors[
                first + k : first + k + 1, j * 128 : j * 128 + width
            ]


def live_slots(counts, mask10):
    for slot in range(10):
        mask10[slot] = (counts[...] > slot).astype(F32)


def natural_mask(mask10, mask):
    for tile in range(ROWS_IMG):
        there = pl.ds(natural_row(tile), IMGS, stride=ROWS_IMG)
        if tile < BIG_ROWS:
            mask[there, :] = jnp.ones((IMGS, 128), F32)
        else:
            mask[there, :] = mask10[(tile - BIG_ROWS) % 10]


def forward_kernel(n, *refs):
    r = Refs(refs)
    pixels_any, weight1_any, weight3_any, kernel_any, squeeze_any, excite_any, output_any = r.take(7)
    counts, live, vectors, squeeze_b, excite_b = r.take(5)
    first_out, pixels_out, far_out, padded_out, group_out, scaled_out, scaled_far_out = r.take(7)
    last_out, merged_out, block_out = r.take(3)
    far1, far3 = r.take(2)
    split_outs = r.take(4)
    stats1, stats2, stats3, sums3 = r.take(4)
    pooled, pooled_far, squeezed, squeezed_far, squeeze_pre, excited = r.take(6)
    factor_sums = r.take()
    consts, norm, local, buf_a, buf_b, pixels, far, weight, zone = r.take(9)
    kernel_low, squeeze_w, excite_w = r.take(3)
    splits = r.take(4)
    turned, mask, mask10 = r.take(3)
    bands = r.take(4)
    load, store, swap_s, swap_r, tile_s, tile_r, small_s, small_r = r.take(8)
    gathers = [r.take(2) for _ in range(4)]
    factor_column, factors = r.take(2)
    factor = Part(n, ORDERS[0], r.take(2))
    ch = lax.axis_index("ch")
    wait_all = greet(n)
    loads = [
        fetch(source, target, load.at[k])
        for k, (source, target) in enumerate(
            (
                (pixels_any, pixels),
                (weight1_any, weight),
                (kernel_any, kernel_low),
                (squeeze_any, squeeze_w),
                (excite_any, excite_w),
            )
        )
    ]
    own = pl.multiple_of(ch * HALF, 16)
    away = pl.multiple_of((1 - ch) * HALF, 16)
    live_slots(counts, mask10)
    natural_mask(mask10, mask)
    count = live[lax.axis_index("img")][0:1, :]
    wait_all()
    chunks = ((0, 384), (384, 384), (768, 384), (1152, 352))
    swaps = []
    for k, (start, size) in enumerate(chunks):
        rows = pl.ds(start, size)
        swaps.append(swap(pixels_any.at[rows], far.at[rows], swap_s.at[k], swap_r.at[k]))
        swaps[-1].start()
    loads[0].wait()
    loads[1].wait()
    for t, (a, b) in enumerate(SPANS):
        put_span(buf_a, t, slice(0, ROWS), dot(pixels[...], weight[pl.ds(own, HALF), a:b]))
    buf_a[7, :, LAST:128] = jnp.zeros((ROWS, 128 - LAST), F32)
    for k, (start, size) in enumerate(chunks):
        swaps[k].wait()
        rows = slice(start, start + size)
        for t, (a, b) in enumerate(SPANS):
            put_span(buf_a, t, rows, dot(far[rows, :], weight[pl.ds(away, HALF), a:b]), add=True)
    natural_stats(buf_a, mask, count, local)
    gather = Gather(n, local, stats1, *gathers[0])
    gather.start()
    weight_swaps = [
        swap(w.at[pl.ds(away, HALF)], f, swap_s.at[4 + k], swap_r.at[4 + k])
        for k, (w, f) in enumerate(((weight1_any, far1), (weight3_any, far3)))
    ]
    for s in weight_swaps:
        s.start()
    load_weight = fetch(weight3_any, weight, load.at[0])
    mine_rows, far_rows = pl.ds(0, ROWS), pl.ds(ROWS, ROWS)
    for source, start in ((pixels, 0), (far, ROWS)):
        for j in range(TILES):
            width = 128 if j < 7 else LAST
            lanes = slice(j * 128, j * 128 + width)
            zone[j, start : start + ROWS, 0:width] = source[:, lanes]
    zone[7, :, LAST:128] = jnp.zeros((2 * ROWS, 128 - LAST), BF16)
    store_pixels = [
        fetch(zone.at[:, mine_rows], pixels_out, store.at[0]),
        fetch(zone.at[:, far_rows], far_out, store.at[12]),
    ]
    stores = []
    store_first = fetch(buf_a, first_out, store.at[1])
    loads[2].wait()
    for span in range(4):
        build_band(kernel_low, span, bands[span])
    loads[3].wait()
    loads[4].wait()
    for k, w in enumerate((squeeze_w, excite_w)):
        splits[2 * k][...], splits[2 * k + 1][...] = halves(w[...])
    stores += [fetch(splits[k], split_outs[k], store.at[2 + k]) for k in range(4)]
    load_vectors(vectors, 0, norm)
    load_output = fetch(output_any, far, load.at[1])
    for s in store_pixels:
        s.wait()
    gather.wait()
    norm_constants(n, stats1, live, norm, consts)

    def activate_first(j):
        average = row_of(consts, 0, j)
        scale = row_of(consts, 1, j) * row_of(consts, 2, j)
        shift = row_of(consts, 3, j)
        zero_pads(zone, j)
        for tile in range(0, ROWS_IMG, 2):
            both = []
            for half in range(2):
                x = buf_a[j, pl.ds(natural_row(tile + half), IMGS, stride=ROWS_IMG), :]
                pre = (x - average) * scale + shift
                both.append(pre * sigmoid(pre))
            row = padded_row(tile)
            zone[j, row : row + 16, :] = jnp.concatenate(both, axis=0).astype(BF16)

    for_tiles(activate_first)
    store_padded = fetch(zone.at[:, pl.ds(0, PAD_ROWS)], padded_out, store.at[6])
    for span, (start, end) in enumerate(WINDOWS):
        tiles = range(start, end)
        right = jnp.concatenate(
            [bands[span][:, tap * 256 : tap * 256 + 256] for tap in range(9)], axis=0
        )
        for big in (True, False):
            left = jnp.concatenate([window(zone, tiles, dy, dx, big) for dy, dx in TAPS], axis=1)
            rows = slice(0, 784) if big else slice(784, ROWS)
            put_span(buf_b, span, rows, dot(left, right))
    crop_stats(buf_b, mask10, count, local)
    gather = Gather(n, local, stats2, *gathers[1])
    gather.start()
    store_group = fetch(buf_b, group_out, store.at[7])
    load_vectors(vectors, 2, norm)
    store_first.wait()
    store_padded.wait()
    gather.wait()
    norm_constants(n, stats2, live, norm, consts)
    inverse = 1.0 / (BIG_ROWS + 9.0 * counts[...].astype(F32))

    def activate_group(j):
        average = row_of(consts, 0, j)
        scale = row_of(consts, 1, j) * row_of(consts, 2, j)
        pre = (buf_b[j] - average) * scale + row_of(consts, 3, j)
        value = pre * sigmoid(pre)
        buf_a[j] = value
        pooled[j] = crop_sum(value.reshape(ROWS_IMG, IMGS, 128), mask10) * inverse

    for_tiles(activate_group)
    pool_swap = swap(pooled, pooled_far, small_s.at[0], small_r.at[0])
    pool_swap.start()
    pool_swap.wait()
    mine = jnp.concatenate([pooled[j] for j in range(TILES)], axis=1)[:, :HALF]
    theirs = jnp.concatenate([pooled_far[j] for j in range(TILES)], axis=1)[:, :HALF]
    is_low = ch == 0
    high, low = splits[0], splits[1]
    pre = (
        fine_dot(jnp.where(is_low, mine, theirs), high[0:HALF, :], low[0:HALF, :])
        + fine_dot(jnp.where(is_low, theirs, mine), high[HALF:, :], low[HALF:, :])
        + squeeze_b[...]
    )
    squeeze_pre[...] = pre
    squeezed[...] = pre * sigmoid(pre)
    squeeze_swap = swap(squeezed, squeezed_far, small_s.at[1], small_r.at[1])
    squeeze_swap.start()
    squeeze_swap.wait()
    mine, theirs = squeezed[...], squeezed_far[...]
    width = mine.shape[1]
    high, low = splits[2], splits[3]
    gate = sigmoid(
        fine_dot(jnp.where(is_low, mine, theirs), high[0:width, :], low[0:width, :])
        + fine_dot(jnp.where(is_low, theirs, mine), high[width:, :], low[width:, :])
        + excite_b[...]
    )
    excited[7] = jnp.zeros((IMGS, 128), F32)
    for j in range(TILES - 1):
        excited[j] = gate[:, j * 128 : j * 128 + 128]
    excited[7, :, 0:LAST] = gate[:, 7 * 128 :]
    pack_factors((pooled, pooled_far), (squeezed, squeezed_far), factors)
    factor_column[factor.place[2]] = factors[...]
    factor.spread2(factor_column)

    def tile_swap(j):
        return swap(zone.at[j, mine_rows], zone.at[j, far_rows], tile_s.at[j], tile_r.at[j])

    def apply(j):
        gate_j = excited[j]
        for tile in range(ROWS_IMG):
            turned[pl.ds(natural_row(tile), IMGS, stride=ROWS_IMG), :] = (
                buf_a[j, tile * 8 : tile * 8 + 8, :] * gate_j
            )
        zone[j, 0:ROWS, :] = turned[...].astype(BF16)
        tile_swap(j).start()

    for_tiles(apply)
    stores.append(fetch(zone.at[:, mine_rows], scaled_out, store.at[8]))
    load_weight.wait()
    store_group.wait()
    for t, (a, b) in enumerate(SPANS):
        left = jnp.concatenate([zone[j, 0:ROWS, :] for j in range(TILES)], axis=1)[:, :HALF]
        put_span(buf_b, t, slice(0, ROWS), dot(left, weight[pl.ds(own, HALF), a:b]))
    buf_b[7, :, LAST:128] = jnp.zeros((ROWS, 128 - LAST), F32)
    factor.spread1(factor_column, factor_sums)
    for_tiles(lambda j: tile_swap(j).wait())
    stores.append(fetch(zone.at[:, far_rows], scaled_far_out, store.at[9]))
    for t, (a, b) in enumerate(SPANS):
        left = jnp.concatenate([zone[j, ROWS : 2 * ROWS, :] for j in range(TILES)], axis=1)[:, :HALF]
        put_span(buf_b, t, slice(0, ROWS), dot(left, weight[pl.ds(away, HALF), a:b]), add=True)
    natural_stats(buf_b, mask, count, local)
    gather = Gather(n, local, stats3, *gathers[2])
    gather.start()
    stores.append(fetch(buf_b, last_out, store.at[10]))
    load_vectors(vectors, 4, norm)
    factor.spread0(factor_sums)
    buf_a[7, :, LAST:128] = jnp.zeros((ROWS, 128 - LAST), F32)
    load_output.wait()
    gather.wait()
    norm_constants(n, stats3, live, norm, consts)
    local[...] = jnp.zeros_like(local)

    def merge(j, lanes, width):
        def vec(k):
            return consts[k, pl.ds(j, 1), 0:width]

        m = mask[:, 0:width]
        normed = (buf_b[j, :, 0:width] - vec(0)) * vec(1)
        merged = pixels[:, lanes].astype(F32) + normed * vec(2) + vec(3)
        s = sigmoid(merged)
        grad = far[:, lanes].astype(F32) * m * slope_of(merged, s)
        far[:, lanes] = (merged * s * m).astype(BF16)
        buf_a[j, :, 0:width] = grad
        local[0, pl.ds(j, 1), 0:width] = jnp.sum(grad, axis=0, keepdims=True)
        local[1, pl.ds(j, 1), 0:width] = jnp.sum(grad * normed, axis=0, keepdims=True)

    for_ragged_tiles(merge)
    gather = Gather(n, local, sums3, *gathers[3])
    gather.start()
    stores.append(fetch(buf_a, merged_out, store.at[11]))
    stores.append(fetch(far, block_out, store.at[13]))
    for s in weight_swaps + stores:
        s.wait()
    factor.settle()
    gather.wait()


def part_extents(n, order):
    sizes = image_axes(n)
    return tuple(sizes[a] for a in order)


def part_shape(n, order, rows):
    return part_extents(n, order) + (rows // n, 128)


def put_blocks(target, tile, tile_rows, start, value):
    _, e1, e2, rows, _ = target.shape
    size = value.shape[0]
    first = start
    while first < start + size:
        block = tile * (tile_rows // rows) + first // rows
        inside = first % rows
        take = min(rows - inside, start + size - first)
        place = (block // (e1 * e2), block // e2 % e1, block % e2)
        target[place[0], place[1], place[2], inside : inside + take, :] = value[
            first - start : first - start + take
        ]
        first += take


def weight_grad(left_span, right_tiles, target, spans):
    for a, b in SPANS:
        left = left_span(a, b)
        for k, span in enumerate(spans):
            right = jnp.concatenate([right_tiles(2 * span), right_tiles(2 * span + 1)], axis=1)
            value = dot(left, right, ((0,), (0,))).astype(BF16)
            put_blocks(target, 2 * k, 1024, a, value[:, :128])
            put_blocks(target, 2 * k + 1, 1024, a, value[:, 128:])


def tile_span(tile):
    def span(a, b):
        tiles = range(a // 128, (b + 127) // 128)
        return jnp.concatenate([tile(t) for t in tiles], axis=1)[:, : b - a]

    return span


def image_axes(n):
    return {16: (2, 2, 4), 128: (4, 4, 8)}.get(n, (n, 1, 1))


class Part:
    def __init__(self, n, order, sems):
        sizes = image_axes(n)
        strides = (1, sizes[0], sizes[0] * sizes[1])
        self.me = lax.axis_index("img")
        self.sizes = [sizes[a] for a in order]
        self.strides = [strides[a] for a in order]
        self.place = [lax.rem(self.me // s, e) for s, e in zip(self.strides, self.sizes)]
        self.sems = sems
        self.live = []

    def send(self, axis, stage, source, target):
        for d in range(1, self.sizes[axis]):
            q = lax.rem(self.place[axis] + d, self.sizes[axis])
            peer = self.me + (q - self.place[axis]) * self.strides[axis]
            copy = pltpu.make_async_remote_copy(
                src_ref=source(q),
                dst_ref=target(d),
                send_sem=self.sems[0].at[stage, d],
                recv_sem=self.sems[1].at[stage, d],
                device_id={"img": peer},
                device_id_type=MESH,
            )
            copy.start()
            self.live.append(copy)

    def keep(self, source, target, stage):
        copy = pltpu.make_async_copy(source, target, self.sems[0].at[stage, 0])
        copy.start()
        self.live.append(copy)

    def settle(self):
        for copy in self.live:
            copy.wait()
        self.live = []

    def add(self, target, own, arrived):
        total = own[...].astype(F32)
        for block in arrived:
            total = total + block[...].astype(F32)
        target[...] = total.astype(BF16)

    def send0(self, source, r0):
        self.send(0, 0, lambda q: source.at[q], lambda d: r0.at[d - 1])

    def sum0(self, source, r0, a0):
        self.settle()
        for k in range(self.sizes[1]):
            self.add(
                a0.at[k],
                source.at[self.place[0], k],
                [r0.at[d, k] for d in range(self.sizes[0] - 1)],
            )

    def send1(self, a0, r1):
        self.send(1, 1, lambda q: a0.at[q], lambda d: r1.at[d - 1])

    def sum1(self, a0, r1, a1):
        self.settle()
        self.add(a1, a0.at[self.place[1]], [r1.at[d] for d in range(self.sizes[1] - 1)])

    def send2(self, a1, r2):
        self.send(2, 2, lambda q: a1.at[q], lambda d: r2.at[d - 1])

    def sum2(self, a1, r2, column):
        self.settle()
        p2 = self.place[2]
        self.add(column.at[p2], a1.at[p2], [r2.at[d] for d in range(self.sizes[2] - 1)])

    def spread2(self, column):
        block = column.at[self.place[2]]
        self.send(2, 3, lambda q: block, lambda d: block)

    def spread1(self, column, result):
        self.settle()
        block = result.at[self.place[0], self.place[1]]
        self.send(1, 4, lambda q: column, lambda d: block)
        self.keep(column, block, 4)

    def spread0(self, result):
        self.settle()
        block = result.at[self.place[0]]
        self.send(0, 5, lambda q: block, lambda d: block)

    @staticmethod
    def room(n, order, shape):
        e0, e1, e2, rows, lanes = shape
        return (
            (max(e0 - 1, 1), e1, e2, rows, lanes),
            (e1, e2, rows, lanes),
            (max(e1 - 1, 1), e2, rows, lanes),
            (e2, rows, lanes),
            (max(e2 - 1, 1), rows, lanes),
            (e2, rows, lanes),
        )


def part_sems(n, count):
    most = max(image_axes(n))
    return [DMA((6, most)) for _ in range(2 * count)]


def fetch(source, target, sem):
    copy = pltpu.make_async_copy(source, target, sem)
    copy.start()
    return copy


class Refs:
    def __init__(self, refs):
        self.refs = list(refs)

    def take(self, count=None):
        if count is None:
            return self.refs.pop(0)
        head, self.refs = self.refs[:count], self.refs[count:]
        return head


ORDERS = ((0, 1, 2), (1, 0, 2), (0, 1, 2), (1, 0, 2))
KERNEL_ORDERS = ORDERS[:2]
AHEAD_TILES = 20
BACK_TILES = 10


def last_grad_kernel(n, *refs):
    r = Refs(refs)
    last_any, merged_any, group_any, scaled_any, scaled_far_any, weight_any, weight_far_any = r.take(7)
    stats3, live, sums3 = r.take(3)
    stats2, counts, vectors_in, excited, squeeze_pre = r.take(5)
    split_anys = r.take(4)
    pre_grad, sums2, excite_grad, squeeze_grad, vectors = r.take(5)
    done1, arrive2, mid3 = r.take(2), r.take(2), r.take(2)
    consts, consts2, local, buf_a, buf_b, low, low_far, scaled, scaled_far = r.take(9)
    weight, weight_far, norm, mask, mask10 = r.take(5)
    splits = r.take(4)
    terms, terms_in, pool_terms, pool_in, pool_tiles = r.take(5)
    grads, rooms, mid1, arrive1 = r.take(4), r.take(4), r.take(2), r.take(2)
    load, swap_s, swap_r, small_s, small_r, send, recv = r.take(7)
    sems = r.take(8)
    ch = lax.axis_index("ch")
    own = pl.multiple_of(ch * HALF, 16)
    wait_all = greet(n)
    loads = [
        fetch(source, target, load.at[k])
        for k, (source, target) in enumerate(
            (
                (last_any, buf_a),
                (merged_any, buf_b),
                (scaled_any, scaled),
                (scaled_far_any, scaled_far),
                (weight_any.at[pl.ds(own, HALF)], weight),
                (weight_far_any, weight_far),
                *zip(split_anys, splits),
            )
        )
    ]
    live_slots(counts, mask10)
    natural_mask(mask10, mask)
    inverse = 1.0 / (BIG_ROWS + 9.0 * counts[...].astype(F32))
    load_vectors(vectors_in, 4, norm)
    norm_constants(n, stats3, live, norm, consts)
    back_constants(n, sums3, consts, vectors)
    load_vectors(vectors_in, 2, norm)
    norm_constants(n, stats2, live, norm, consts2)
    parts = [Part(n, order, sems[2 * k : 2 * k + 2]) for k, order in enumerate(ORDERS)]
    wait_all()
    loads[0].wait()
    loads[1].wait()

    def step(j):
        normed = (buf_a[j] - row_of(consts, 0, j)) * row_of(consts, 1, j)
        inner = buf_b[j] - row_of(consts, 5, j) - normed * row_of(consts, 6, j)
        low[j] = (mask[...] * row_of(consts, 7, j) * inner).astype(BF16)
        swap(low.at[j], low_far.at[j], swap_s.at[j], swap_r.at[j]).start()

    for_tiles(step)
    load_group = fetch(group_any, buf_a, load.at[0])
    for part in range(4):
        if part < 2:
            loads[2 + part].wait()
        rows = (scaled, scaled_far)[part % 2]
        left = tile_span(lambda t: rows[t])
        weight_grad(left, lambda t: low[t], grads[part], (0, 1) if part < 2 else (2, 3))
        if part < 2:
            parts[part].send0(grads[part], rooms[part])
    loads[4].wait()
    for t, (a, b) in enumerate(SPANS):
        left = jnp.concatenate([low[j] for j in range(TILES)], axis=1)[:, :HALF]
        put_span(buf_b, t, slice(0, ROWS), dot(left, weight[a:b, :], ((1,), (1,))))
    buf_b[7, :, LAST:128] = jnp.zeros((ROWS, 128 - LAST), F32)
    for_tiles(lambda j: swap(low.at[j], low_far.at[j], swap_s.at[j], swap_r.at[j]).wait())
    loads[5].wait()
    for t, (a, b) in enumerate(SPANS):
        left = jnp.concatenate([low_far[j] for j in range(TILES)], axis=1)[:, :HALF]
        put_span(
            buf_b, t, slice(0, ROWS), dot(left, weight_far[a:b, :], ((1,), (1,))), add=True
        )
    load_group.wait()

    def gate_sum(j):
        average = row_of(consts2, 0, j)
        scale = row_of(consts2, 1, j) * row_of(consts2, 2, j)
        shift = row_of(consts2, 3, j)
        total = jnp.zeros((IMGS, 128), F32)
        for tile in range(ROWS_IMG):
            pre = (buf_a[j, tile * 8 : tile * 8 + 8, :] - average) * scale + shift
            act = pre * sigmoid(pre)
            total = total + act * buf_b[j, pl.ds(natural_row(tile), IMGS, stride=ROWS_IMG), :]
        gate = excited[j]
        excite_grad[j] = total * gate * (1.0 - gate)

    for_tiles(gate_sum)
    for k in range(2):
        parts[k].sum0(grads[k], rooms[k], mid1[k])
        parts[k].send1(mid1[k], arrive1[k])
    wide = jnp.concatenate([excite_grad[j] for j in range(TILES)], axis=1)[:, :HALF]
    width = squeeze_pre.shape[1]
    is_low = ch == 0
    for k in range(6, 10):
        loads[k].wait()
    across = ((1,), (1,))
    high, low_part = splits[2], splits[3]
    part0 = fine_dot(wide, high[0:width, :], low_part[0:width, :], across)
    part1 = fine_dot(wide, high[width:, :], low_part[width:, :], across)
    terms[...] = jnp.where(is_low, part1, part0)
    term_swap = swap(terms, terms_in, small_s.at[0], small_r.at[0])
    term_swap.start()
    term_swap.wait()
    pre = squeeze_pre[...]
    grad = (jnp.where(is_low, part0, part1) + terms_in[...]) * slope_of(pre, sigmoid(pre))
    squeeze_grad[...] = grad
    high, low_part = splits[0], splits[1]
    pool0 = fine_dot(grad, high[0:HALF, :], low_part[0:HALF, :], across)
    pool1 = fine_dot(grad, high[HALF:, :], low_part[HALF:, :], across)
    pool_terms[...] = jnp.where(is_low, pool1, pool0)
    pool_swap = swap(pool_terms, pool_in, small_s.at[1], small_r.at[1])
    pool_swap.start()
    pool_swap.wait()
    for k in range(2):
        parts[k].sum1(mid1[k], arrive1[k], done1[k])
        parts[k].send2(done1[k], arrive2[k])
        parts[k + 2].send0(grads[k + 2], rooms[k + 2])
    pool = jnp.where(is_low, pool0, pool1) + pool_in[...]
    pool_tiles[7, :, LAST:128] = jnp.zeros((IMGS, 128 - LAST), F32)
    for j in range(TILES):
        part = pool[:, j * 128 : min(HALF, j * 128 + 128)]
        pool_tiles[j, :, 0 : part.shape[1]] = part * inverse[:, 0 : part.shape[1]]

    def slopes(j):
        average, scale = row_of(consts2, 0, j), row_of(consts2, 1, j)
        gain, shift = row_of(consts2, 2, j), row_of(consts2, 3, j)
        gate, pooled = excited[j], pool_tiles[j]
        total = jnp.zeros((IMGS, 128), F32)
        total_normed = jnp.zeros((IMGS, 128), F32)
        for tile in range(ROWS_IMG):
            rows = slice(tile * 8, tile * 8 + 8)
            normed = (buf_a[j, rows, :] - average) * scale
            pre = normed * gain + shift
            lead = pooled if tile < BIG_ROWS else pooled * mask10[(tile - BIG_ROWS) % 10]
            act = buf_b[j, pl.ds(natural_row(tile), IMGS, stride=ROWS_IMG), :] * gate + lead
            grad = act * slope_of(pre, sigmoid(pre))
            buf_a[j, rows, :] = grad
            total = total + grad
            total_normed = total_normed + grad * normed
        local[0, pl.ds(j, 1), :] = jnp.sum(total, axis=0, keepdims=True)
        local[1, pl.ds(j, 1), :] = jnp.sum(total_normed, axis=0, keepdims=True)

    for_tiles(slopes)
    gather = Gather(n, local, sums2, send, recv)
    gather.start()
    store = fetch(buf_a, pre_grad, load.at[0])
    gather.wait()
    for k in range(2):
        parts[k].settle()
        parts[k + 2].sum0(grads[k + 2], rooms[k + 2], mid3[k])
    store.wait()


def pack_factors(wides, narrows, factors):
    tiles = [part[j] for part in wides for j in range(TILES)]
    for part in narrows:
        rest = part[:, 128:]
        blank = jnp.zeros((IMGS, 128 - rest.shape[1]), F32)
        tiles += [part[:, 0:128], jnp.concatenate([rest, blank], axis=1)]
    for k in range(0, len(tiles), 2):
        both = jnp.concatenate(tiles[k : k + 2], axis=0)
        factors[k * IMGS : (k + 2) * IMGS, :] = both.astype(BF16)


def tail_kernel(n, *refs):
    r = Refs(refs)
    pre_any, group_any, padded_any, first_any = r.take(4)
    pixels_any, pixels_far_any, weight_any, weight_far_any, merged_any = r.take(5)
    stats2, live, sums2, counts, vectors_in, kernel, stats1 = r.take(7)
    done1, arrive2, mid3 = r.take(2), r.take(2), r.take(2)
    factor_parts = r.take(2)
    pixels_grad, group_vectors, first_vectors = r.take(3)
    last_sums, first_sums, kernel_sums = r.take(4), r.take(4), r.take(2)
    factor_sums = r.take()
    consts, consts1, norm, mask10, local, sums1 = r.take(6)
    buf_a, buf_b, zone1, zone2, weight, weight_far, turned = r.take(7)
    bands = r.take(2)
    arrive3, done3, arrive4, last_columns = r.take(2), r.take(2), r.take(2), r.take(4)
    grads = r.take(4)
    first_rooms = [r.take(6) for _ in range(4)]
    kernel_grads = r.take(2)
    kernel_rooms = [r.take(6) for _ in range(2)]
    factor_column, factors = r.take(2)
    load, swap_s, swap_r, send, recv, free = r.take(6)
    sems = [r.take(2) for _ in range(11)]
    own = pl.multiple_of(lax.axis_index("ch") * HALF, 16)
    mine_rows, far_rows = pl.ds(0, ROWS), pl.ds(ROWS, ROWS)
    wait_all = greet(n)
    loads = [
        fetch(source, target, load.at[k])
        for k, (source, target) in enumerate(
            (
                (pre_any, buf_a),
                (group_any, buf_b),
                (padded_any, zone1.at[:, pl.ds(0, PAD_ROWS)]),
                (weight_any.at[pl.ds(own, HALF)], weight),
                (weight_far_any, weight_far),
            )
        )
    ]
    firsts = [Part(n, order, sems[k]) for k, order in enumerate(ORDERS)]
    lasts = [Part(n, order, sems[4 + k]) for k, order in enumerate(ORDERS)]
    kernels = [Part(n, KERNEL_ORDERS[k], sems[8 + k]) for k in range(2)]
    factor = Part(n, ORDERS[0], sems[10])
    live_slots(counts, mask10)
    load_vectors(vectors_in, 2, norm)
    norm_constants(n, stats2, live, norm, consts)
    back_constants(n, sums2, consts, group_vectors)
    load_vectors(vectors_in, 0, norm)
    norm_constants(n, stats1, live, norm, consts1)
    wait_all()

    def each(step, ks):
        for k in ks:
            step(k)

    def last1(k):
        lasts[k].sum1(mid3[k - 2], arrive3[k - 2], done3[k - 2])
        lasts[k].send2(done3[k - 2], arrive4[k - 2])

    def last2(k):
        lasts[k].sum2((*done1, *done3)[k], (*arrive2, *arrive4)[k], last_columns[k])
        lasts[k].spread2(last_columns[k])

    def last3(k):
        lasts[k].spread1(last_columns[k], last_sums[k])

    def last4(k):
        lasts[k].spread0(last_sums[k])

    def reducer(part, source, room, result):
        r0, a0, r1, a1, r2, column = room

        def stage0():
            part.send0(source, r0)

        def stage1():
            part.sum0(source, r0, a0)
            part.send1(a0, r1)

        def stage2():
            part.sum1(a0, r1, a1)
            part.send2(a1, r2)

        def stage3():
            part.sum2(a1, r2, column)
            part.spread2(column)

        return (
            stage0,
            stage1,
            stage2,
            stage3,
            lambda: part.spread1(column, result),
            lambda: part.spread0(result),
        )

    first = [reducer(firsts[k], grads[k], first_rooms[k], first_sums[k]) for k in range(4)]
    kernel_sum = [
        reducer(kernels[k], kernel_grads[k], kernel_rooms[k], kernel_sums[k]) for k in range(2)
    ]
    head, back, two = (0, 1), (2, 3), range(2)
    each(last2, head)
    for k in two:
        lasts[k + 2].send1(mid3[k], arrive3[k])
    for span in range(2):
        build_band(kernel, span, bands[span])
    loads[0].wait()
    loads[1].wait()

    def group_step(j):
        average, scale = row_of(consts, 0, j), row_of(consts, 1, j)
        less, slope, front = row_of(consts, 5, j), row_of(consts, 6, j), row_of(consts, 7, j)
        zero_pads(zone2, j)
        for tile in range(0, ROWS_IMG, 2):
            both = []
            for half in range(2):
                rows = slice(tile * 8 + half * 8, tile * 8 + half * 8 + 8)
                normed = (buf_b[j, rows, :] - average) * scale
                grad = front * (buf_a[j, rows, :] - less - normed * slope)
                if tile >= BIG_ROWS:
                    grad = grad * mask10[(tile + half - BIG_ROWS) % 10]
                both.append(grad)
            row = padded_row(tile)
            zone2[j, row : row + 16, :] = jnp.concatenate(both, axis=0).astype(BF16)

    for_tiles(group_step)
    load_first = fetch(first_any, buf_b, load.at[0])
    each(last1, back)
    pack_factors(factor_parts[:1], factor_parts[1:], factors)
    factor_column[factor.place[2]] = factors[...]
    factor.spread2(factor_column)
    loads[2].wait()
    started = 0
    for span, (start, end) in enumerate(WINDOWS):
        tiles = (2 * span, 2 * span + 1)
        depth = (end - start) * 128
        band = bands[span % 2]
        if span >= 2:
            build_band(kernel, span, band)
        shifted = [
            [window(zone2, tiles, -dy, -dx, big) for dy, dx in TAPS] for big in (True, False)
        ]
        for rows, left in ((slice(0, 784), shifted[0]), (slice(784, ROWS), shifted[1])):
            value = dot(jnp.concatenate(left, axis=1), band[0:depth, :], ((1,), (1,)))
            for t in range(start, end):
                part = value[:, (t - start) * 128 : (t - start) * 128 + 128]
                if t < started:
                    buf_a[t, rows, :] += part
                else:
                    buf_a[t, rows, :] = part
        started = end
        masks = span_masks(span)
        left = jnp.concatenate(
            [window(zone1, range(start, end), 0, 0, big) for big in (True, False)], axis=0
        )
        pieces = []
        for tap in range(9):
            right = jnp.concatenate([shifted[0][tap], shifted[1][tap]], axis=0)
            value = dot(left, right, ((0,), (0,)))
            piece = jnp.zeros((GROUP_WIDTH, 256), F32)
            for g, inside in zip(span_groups(span), masks):
                row = g * GROUP_WIDTH - start * 128
                piece = jnp.where(inside, value[row : row + GROUP_WIDTH], piece)
            pieces.append(piece)
        pieces.append(jnp.zeros((8, 256), F32))
        value = jnp.concatenate(pieces, axis=0).astype(BF16)
        for half in range(2):
            rows = slice(half * 256, half * 256 + 256)
            put_blocks(kernel_grads[half], 2 * span, 256, 0, value[rows, :128])
            put_blocks(kernel_grads[half], 2 * span + 1, 256, 0, value[rows, 128:])
        if span == 0:
            each(last3, head)
        elif span == 1:
            each(last4, head)
            factor.spread1(factor_column, factor_sums)
        elif span == 2:
            each(last2, back)
        else:
            for k in two:
                kernel_sum[k][0]()
            factor.spread0(factor_sums)
    pl.semaphore_signal(
        free, 1, device_id={"ch": 1 - lax.axis_index("ch")}, device_id_type=MESH
    )
    load_pixels = [
        fetch(pixels_any, zone2.at[:, mine_rows], load.at[1]),
        fetch(pixels_far_any, zone2.at[:, far_rows], load.at[2]),
    ]
    load_first.wait()

    def first_slopes(j):
        average, scale = row_of(consts1, 0, j), row_of(consts1, 1, j)
        gain, shift = row_of(consts1, 2, j), row_of(consts1, 3, j)
        total = jnp.zeros((IMGS, 128), F32)
        total_normed = jnp.zeros((IMGS, 128), F32)
        for tile in range(ROWS_IMG):
            rows = slice(tile * 8, tile * 8 + 8)
            x = buf_b[j, pl.ds(natural_row(tile), IMGS, stride=ROWS_IMG), :]
            normed = (x - average) * scale
            pre = normed * gain + shift
            grad = buf_a[j, rows, :] * slope_of(pre, sigmoid(pre))
            if tile >= BIG_ROWS:
                grad = grad * mask10[(tile - BIG_ROWS) % 10]
            buf_a[j, rows, :] = grad
            total = total + grad
            total_normed = total_normed + grad * normed
        local[0, pl.ds(j, 1), :] = jnp.sum(total, axis=0, keepdims=True)
        local[1, pl.ds(j, 1), :] = jnp.sum(total_normed, axis=0, keepdims=True)

    for_tiles(first_slopes)
    gather = Gather(n, local, sums1, send, recv)
    gather.start()
    each(last3, back)
    gather.wait()
    back_constants(n, sums1, consts1, first_vectors)

    def tile_swap(j):
        return swap(zone1.at[j, mine_rows], zone1.at[j, far_rows], swap_s.at[j], swap_r.at[j])

    def first_step(j):
        average, scale = row_of(consts1, 0, j), row_of(consts1, 1, j)
        less, slope, front = row_of(consts1, 5, j), row_of(consts1, 6, j), row_of(consts1, 7, j)
        for tile in range(ROWS_IMG):
            there = pl.ds(natural_row(tile), IMGS, stride=ROWS_IMG)
            normed = (buf_b[j, there, :] - average) * scale
            grad = front * (buf_a[j, tile * 8 : tile * 8 + 8, :] - less - normed * slope)
            if tile >= BIG_ROWS:
                grad = grad * mask10[(tile - BIG_ROWS) % 10]
            turned[there, :] = grad
        zone1[j, 0:ROWS, :] = turned[...].astype(BF16)
        tile_swap(j).start()

    pl.semaphore_wait(free, 1)
    for_tiles(first_step)
    load_merged = fetch(merged_any, buf_a, load.at[0])
    for s in load_pixels:
        s.wait()
    for part in range(4):
        side = slice(0, ROWS) if part % 2 == 0 else slice(ROWS, 2 * ROWS)
        weight_grad(
            tile_span(lambda t: zone2[t, side, :]),
            lambda t: zone1[t, 0:ROWS, :],
            grads[part],
            (0, 1) if part < 2 else (2, 3),
        )
        if part < 2:
            first[part][0]()
    for k in two:
        kernel_sum[k][1]()
    load_merged.wait()
    loads[3].wait()
    for t, (a, b) in enumerate(SPANS):
        left = jnp.concatenate([zone1[j, 0:ROWS, :] for j in range(TILES)], axis=1)[:, :HALF]
        put_span(buf_a, t, slice(0, ROWS), dot(left, weight[a:b, :], ((1,), (1,))), add=True)
    for_tiles(lambda j: tile_swap(j).wait())
    loads[4].wait()
    for t, (a, b) in enumerate(SPANS):
        left = jnp.concatenate([zone1[j, ROWS : 2 * ROWS, :] for j in range(TILES)], axis=1)
        put_span(
            buf_a, t, slice(0, ROWS), dot(left[:, :HALF], weight_far[a:b, :], ((1,), (1,))), add=True
        )
    store = fetch(buf_a, pixels_grad, load.at[0])

    def stage(sums, ks, number):
        for k in ks:
            sums[k][number]()

    stage(first, head, 1)
    stage(first, back, 0)
    stage(kernel_sum, two, 2)
    stage(first, head, 2)
    each(last4, back)
    stage(first, back, 1)
    stage(kernel_sum, two, 3)
    stage(first, head, 3)
    stage(first, back, 2)
    stage(kernel_sum, two, 4)
    stage(first, head, 4)
    stage(kernel_sum, two, 5)
    stage(first, head, 5)
    stage(first, back, 3)
    stage(first, back, 4)
    stage(first, back, 5)
    for part in (*firsts, *lasts, *kernels, factor):
        part.settle()
    store.wait()


def spread_kernel(*refs):
    lasts, firsts, pixels_wide = refs[0:4], refs[4:8], refs[8]
    last_out, first_out, pixels_out = refs[9:12]
    ch = lax.axis_index("ch")
    j = pl.program_id(0)
    for sums, out in ((lasts, last_out), (firsts, first_out)):
        for late in range(2):

            @pl.when((j >= 4) == bool(late))
            def _():
                for k, place in ((0, ch), (1, 1 - ch)):
                    rows = pl.ds(pl.multiple_of(place * HALF, 8), HALF)
                    out[rows, :] = sums[2 * late + k][0, 0:HALF, :].astype(F32)

    pixels_out[...] = pixels_wide[0]


def finish_kernel(low_half, high_half, ahead, back, group_out, squeeze_w, squeeze_b, excite_w, excite_b):
    ch = lax.axis_index("ch")
    se = squeeze_w.shape[1]
    split = low_half.shape[1]
    for j in range(TILES):
        width = 128 if j < 7 else LAST
        lanes = slice(j * 128, j * 128 + width)
        group_out[0:split, lanes] = low_half[j, :, 0:width].astype(F32)
        rest = 9 * GROUP_WIDTH - split
        group_out[split:, lanes] = high_half[j, :, 0:width].astype(F32)[:rest]
    n = ahead.shape[0]

    def columns(factors, start, tiles, width):
        whole = factors[...].astype(F32).reshape(n, -1, IMGS, 128)
        parts = [whole[:, t].reshape(n * IMGS, 128) for t in range(start, start + tiles)]
        return jnp.concatenate(parts, axis=1)[:, :width]

    excite_all, squeeze_all = columns(back, 0, 8, HALF), columns(back, 8, 2, se)
    squeeze_b[...] = jnp.sum(squeeze_all, axis=0, keepdims=True)
    excite_b[...] = jnp.sum(excite_all, axis=0, keepdims=True)
    excite_all, squeeze_all = excite_all.astype(BF16), squeeze_all.astype(BF16)
    for start, place in ((0, ch), (8, 1 - ch)):
        rows = pl.ds(pl.multiple_of(place * HALF, 8), HALF)
        squeeze_w[rows, :] = dot(columns(ahead, start, 8, HALF).astype(BF16), squeeze_all, ((0,), (0,)))
    own, far = columns(ahead, 16, 2, se), columns(ahead, 18, 2, se)
    for k, left in enumerate((jnp.where(ch == 0, own, far), jnp.where(ch == 0, far, own))):
        excite_w[k * se : (k + 1) * se, :] = dot(left.astype(BF16), excite_all, ((0,), (0,)))


def call(kernel, ins, outs, scratch, ident=None, in_specs=None, out_specs=None, grid=()):
    params = {"vmem_limit_bytes": VMEM_LIMIT}
    if ident is not None:
        params.update(collective_id=ident, has_side_effects=True)
    return pl.pallas_call(
        kernel,
        grid=grid,
        out_shape=[jax.ShapeDtypeStruct(shape, dtype) for shape, dtype in outs],
        in_specs=in_specs or [VMEM] * len(ins),
        out_specs=out_specs or [VMEM] * len(outs),
        scratch_shapes=scratch,
        compiler_params=pltpu.CompilerParams(**params),
    )(*ins)


def body(
    n,
    pixels,
    crop_counts,
    first_weight,
    first_gain,
    first_shift,
    group_weight,
    group_gain,
    group_shift,
    squeeze_weight,
    squeeze_bias,
    excite_weight,
    excite_bias,
    last_weight,
    last_gain,
    last_shift,
    output_grad,
):
    me = lax.axis_index("img")
    assert pixels.shape == (ROWS, HALF)
    se = squeeze_weight.shape[1]
    wide = (TILES, ROWS, 128)
    stat = (n, 2, TILES, 128)
    sem = DMA((n - 1,))

    local_counts = lax.dynamic_slice_in_dim(crop_counts, me * IMGS, IMGS)
    counts = jnp.broadcast_to(local_counts[:, None], (IMGS, 128))
    live = jnp.sum((BIG_ROWS + 9 * crop_counts).reshape(n, IMGS), axis=1).astype(F32)
    live = jnp.broadcast_to(live[:, None, None], (n, TILES, 128))
    gains = jnp.stack(
        [first_gain, first_shift, group_gain, group_shift, last_gain, last_shift]
    )
    kernel = group_weight.reshape(9 * GROUP_WIDTH, HALF)
    local = pltpu.VMEM((2, TILES, 128), F32)
    consts = pltpu.VMEM((8, TILES, 128), F32)
    vectors = ((2, TILES, 128), F32)
    bands = [pltpu.VMEM(((e - s) * 128, 9 * 256), BF16) for s, e in WINDOWS]
    mask10 = pltpu.VMEM((10, IMGS, 128), F32)
    mask = pltpu.VMEM((ROWS, 128), F32)
    small = (TILES, IMGS, 128)
    wide_buf = pltpu.VMEM(wide, F32)
    tall = (ROWS, HALF)
    ahead_shape = part_extents(n, ORDERS[0]) + (AHEAD_TILES * IMGS, 128)
    back_shape = part_extents(n, ORDERS[0]) + (BACK_TILES * IMGS, 128)
    split_shapes = [(2 * HALF, se)] * 2 + [(2 * se, HALF)] * 2
    (
        first,
        pixels_tiles,
        pixels_far,
        padded,
        group,
        scaled,
        scaled_far,
        last,
        merged_grad,
        block_out,
        first_far,
        last_far,
        *rest,
    ) = call(
        functools.partial(forward_kernel, n),
        (
            pixels,
            first_weight,
            last_weight,
            kernel,
            squeeze_weight,
            excite_weight,
            output_grad,
            counts,
            live,
            gains,
            squeeze_bias[None],
            excite_bias[None],
        ),
        [
            (wide, F32),
            (wide, BF16),
            (wide, BF16),
            ((TILES, PAD_ROWS, 128), BF16),
            (wide, F32),
            (wide, BF16),
            (wide, BF16),
            (wide, F32),
            (wide, F32),
            (tall, BF16),
            ((HALF, HALF), BF16),
            ((HALF, HALF), BF16),
        ]
        + [(shape, BF16) for shape in split_shapes]
        + [(stat, F32)] * 4
        + [(small, F32)] * 2
        + [((IMGS, se), F32)] * 3
        + [(small, F32), (ahead_shape, BF16)],
        [
            consts,
            local,
            local,
            wide_buf,
            wide_buf,
            pltpu.VMEM(tall, BF16),
            pltpu.VMEM(tall, BF16),
            pltpu.VMEM((2 * HALF, HALF), BF16),
            pltpu.VMEM((TILES, 2 * ROWS, 128), BF16),
            pltpu.VMEM((9 * GROUP_WIDTH, HALF), BF16),
            pltpu.VMEM((2 * HALF, se), F32),
            pltpu.VMEM((2 * se, HALF), F32),
            *(pltpu.VMEM(shape, BF16) for shape in split_shapes),
            mask,
            mask,
            mask10,
            *bands,
            DMA((6,)),
            DMA((14,)),
            DMA((6,)),
            DMA((6,)),
            DMA((TILES,)),
            DMA((TILES,)),
            DMA((2,)),
            DMA((2,)),
            *[sem] * 8,
            pltpu.VMEM(ahead_shape[2:], BF16),
            pltpu.VMEM(ahead_shape[3:], BF16),
            *part_sems(n, 1),
        ],
        0,
        in_specs=[ANY] * 7 + [VMEM] * 5,
        out_specs=[ANY] * 16 + [VMEM] * 10 + [ANY],
    )
    splits, rest = rest[:4], rest[4:]
    stats1, stats2, stats3, sums3, pooled, pooled_far = rest[:6]
    squeezed, squeezed_far, squeeze_pre, excited, ahead_sums = rest[6:]

    def vmem(shape, dtype=BF16):
        return pltpu.VMEM(shape, dtype)

    shapes = [part_shape(n, order, 4 * 1024) for order in ORDERS]
    rooms = [Part.room(n, order, shape) for order, shape in zip(ORDERS, shapes)]
    low_buf = vmem(wide)
    weight_buf = vmem((HALF, HALF))
    pre_grad, sums2, excite_grad, squeeze_grad, vectors3, *carry = call(
        functools.partial(last_grad_kernel, n),
        (
            last,
            merged_grad,
            group,
            scaled,
            scaled_far,
            last_weight,
            last_far,
            stats3,
            live,
            sums3,
            stats2,
            counts,
            gains,
            excited,
            squeeze_pre,
            *splits,
        ),
        [(wide, F32), (stat, F32), (small, F32), ((IMGS, se), F32), vectors]
        + [(rooms[k][3], BF16) for k in range(2)]
        + [(rooms[k][4], BF16) for k in range(2)]
        + [(rooms[k][1], BF16) for k in (2, 3)],
        [
            consts,
            consts,
            local,
            wide_buf,
            wide_buf,
            low_buf,
            low_buf,
            low_buf,
            low_buf,
            weight_buf,
            weight_buf,
            local,
            mask,
            mask10,
            *(vmem(shape) for shape in split_shapes),
            vmem((IMGS, se), F32),
            vmem((IMGS, se), F32),
            vmem((IMGS, HALF), F32),
            vmem((IMGS, HALF), F32),
            vmem(small, F32),
            *(vmem(shape) for shape in shapes),
            *(vmem(room[0]) for room in rooms),
            *(vmem(room[1]) for room in rooms[:2]),
            *(vmem(room[2]) for room in rooms[:2]),
            DMA((10,)),
            DMA((TILES,)),
            DMA((TILES,)),
            DMA((2,)),
            DMA((2,)),
            sem,
            sem,
            *part_sems(n, 4),
        ],
        4,
        in_specs=[ANY] * 7 + [VMEM] * 8 + [ANY] * 4,
        out_specs=[ANY] + [VMEM] * 10,
    )
    done1, arrive2, mid3 = carry[0:2], carry[2:4], carry[4:6]
    kernel_shapes = [part_shape(n, order, TILES * 256) for order in KERNEL_ORDERS]
    kernel_rooms = [
        Part.room(n, order, shape) for order, shape in zip(KERNEL_ORDERS, kernel_shapes)
    ]
    kernel_shapes = [part_shape(n, order, TILES * 256) for order in KERNEL_ORDERS]
    kernel_rooms = [
        Part.room(n, order, shape) for order, shape in zip(KERNEL_ORDERS, kernel_shapes)
    ]
    zone = vmem((TILES, 2 * ROWS, 128))
    pixels_wide, vectors2, vectors1, *carry = call(
        functools.partial(tail_kernel, n),
        (
            pre_grad,
            group,
            padded,
            first,
            pixels_tiles,
            pixels_far,
            first_weight,
            first_far,
            merged_grad,
            stats2,
            live,
            sums2,
            counts,
            gains,
            kernel,
            stats1,
            *done1,
            *arrive2,
            *mid3,
            excite_grad,
            squeeze_grad,
        ),
        [(wide, F32), vectors, vectors]
        + [(shape, BF16) for shape in shapes * 2 + kernel_shapes]
        + [(back_shape, BF16)],
        [
            consts,
            consts,
            local,
            mask10,
            local,
            vmem(stat, F32),
            wide_buf,
            wide_buf,
            zone,
            zone,
            weight_buf,
            weight_buf,
            vmem((ROWS, 128), F32),
            vmem((512, 9 * 256)),
            vmem((512, 9 * 256)),
            *(vmem(rooms[k][kind]) for kind in (2, 3, 4) for k in (2, 3)),
            *(vmem(room[5]) for room in rooms),
            *(vmem(shape) for shape in shapes),
            *(vmem(shape) for room in rooms for shape in room),
            *(vmem(shape) for shape in kernel_shapes),
            *(vmem(shape) for room in kernel_rooms for shape in room),
            vmem(back_shape[2:]),
            vmem(back_shape[3:]),
            DMA((5,)),
            DMA((TILES,)),
            DMA((TILES,)),
            sem,
            sem,
            pltpu.SemaphoreType.REGULAR,
            *part_sems(n, 11),
        ],
        5,
        in_specs=[ANY] * 9 + [VMEM] * 15,
        out_specs=[ANY, VMEM, VMEM] + [ANY] * 11,
    )
    sums = [s.reshape(4, 1024, 128) for s in carry[0:8]]
    kernel_sums = [s.reshape(TILES, 256, 128) for s in carry[8:10]]
    late = pl.BlockSpec((1, 1024, 128), lambda j: (jnp.maximum(j - 4, 0), 0, 0))
    early = pl.BlockSpec((1, 1024, 128), lambda j: (jnp.minimum(j, 3), 0, 0))
    last_weight_grad, first_weight_grad, pixels_grad = call(
        spread_kernel,
        (*sums, pixels_wide),
        [((2 * HALF, HALF), F32), ((2 * HALF, HALF), F32), ((ROWS, HALF), F32)],
        [],
        in_specs=[early, early, late, late] * 2 + [pl.BlockSpec((1, ROWS, 128), lambda j: (j, 0, 0))],
        out_specs=[
            pl.BlockSpec((2 * HALF, 128), lambda j: (0, j)),
            pl.BlockSpec((2 * HALF, 128), lambda j: (0, j)),
            pl.BlockSpec((ROWS, 128), lambda j: (0, j)),
        ],
        grid=(TILES,),
    )
    group_weight_grad, squeeze_weight_grad, squeeze_bias_grad, excite_weight_grad, excite_bias_grad = call(
        finish_kernel,
        (*kernel_sums, ahead_sums.reshape(n, -1, 128), carry[10].reshape(n, -1, 128)),
        [
            ((9 * GROUP_WIDTH, HALF), F32),
            ((2 * HALF, se), F32),
            ((1, se), F32),
            ((2 * se, HALF), F32),
            ((1, HALF), F32),
        ],
        [],
    )
    group_weight_grad = group_weight_grad.reshape(3, 3, GROUP_WIDTH, HALF)
    squeeze_bias_grad, excite_bias_grad = squeeze_bias_grad[0], excite_bias_grad[0]

    def pair(vector):
        flat = vector.reshape(2, 1024)[:, :HALF]
        return flat[0], flat[1]

    first_gain_grad, first_shift_grad = pair(vectors1)
    group_gain_grad, group_shift_grad = pair(vectors2)
    last_gain_grad, last_shift_grad = pair(vectors3)
    return (
        block_out,
        pixels_grad,
        first_weight_grad,
        first_gain_grad,
        first_shift_grad,
        group_weight_grad,
        group_gain_grad,
        group_shift_grad,
        squeeze_weight_grad,
        squeeze_bias_grad,
        excite_weight_grad,
        excite_bias_grad,
        last_weight_grad,
        last_gain_grad,
        last_shift_grad,
    )


def solution(mesh):
    wide = P("img", "ch")
    matrix, vector = P(None, "ch"), P("ch")
    cube = P(None, None, None, "ch")
    weights = (matrix, vector, vector, cube, vector, vector, matrix, vector, matrix, vector, matrix, vector, vector)
    return jax.shard_map(
        functools.partial(body, mesh.shape["img"]),
        mesh=mesh,
        in_specs=(wide, P(), *weights, wide),
        out_specs=(wide, wide, *weights),
        check_vma=False,
    )
```

```python
import functools

import jax
import jax.numpy as jnp
from jax import lax
from jax.experimental import pallas as pl
from jax.experimental.pallas import tpu as pltpu
from jax.sharding import PartitionSpec as P


GROUP_WIDTH = 56
ROWS_IMG = 188
BIG_ROWS = 98
IMGS = 8
ROWS = IMGS * ROWS_IMG
HALF = 1008
TILES = 8
LAST = HALF - 7 * 128
EPSILON = 1e-05
F32 = jnp.float32
BF16 = jnp.bfloat16
MESH = pl.DeviceIdType.MESH
VMEM = pl.BlockSpec(memory_space=pltpu.VMEM)
ANY = pl.BlockSpec(memory_space=pl.ANY)
VMEM_LIMIT = 60 * 1024 * 1024
SPANS = ((0, 256), (256, 512), (512, 768), (768, 1008))
WINDOWS = ((0, 3), (1, 5), (3, 7), (5, 8))
BIG_PAD = 73 * 16
PAD_ROWS = BIG_PAD + 21 * 80
TAPS = tuple((dy, dx) for dy in (-1, 0, 1) for dx in (-1, 0, 1))
DMA = pltpu.SemaphoreType.DMA


def big_place(y, x):
    return (1 + (y + 1) * 8 + x) * 16


def small_place(y, x):
    return BIG_PAD + (1 + (y + 1) * 4 + x) * 80


def natural_row(tile):
    if tile < BIG_ROWS:
        return (tile % 2) * 49 + tile // 2
    tile = tile - BIG_ROWS
    return BIG_ROWS + (tile % 10) * 9 + tile // 10


def padded_row(tile):
    if tile < BIG_ROWS:
        pixel = tile // 2
        return big_place(pixel // 7, pixel % 7) + (tile % 2) * 8
    tile = tile - BIG_ROWS
    pixel = tile // 10
    return small_place(pixel // 3, pixel % 3) + (tile % 10) * 8


REAL_ROWS = frozenset(padded_row(tile) for tile in range(0, ROWS_IMG, 2))
ZERO_ROWS = tuple(row for row in range(0, PAD_ROWS, 16) if row not in REAL_ROWS)


def sigmoid(v):
    return 0.5 + 0.5 * jnp.tanh(0.5 * v)


def slope_of(v, s):
    return s * (1.0 + v * (1.0 - s))


def dot(a, b, dims=((1,), (0,)), **kw):
    return lax.dot_general(a, b, (dims, ((), ())), preferred_element_type=F32, **kw)


def for_each(count, step):
    if count <= 16:
        for index in range(count):
            step(index)
    else:
        lax.fori_loop(0, count, lambda index, _: (step(index), 0)[1], 0)


def for_tiles(step):
    lax.fori_loop(0, TILES, lambda j, _: (step(j), 0)[1], 0)


def for_ragged_tiles(step):
    def full(j, _):
        step(j, pl.ds(pl.multiple_of(j * 128, 128), 128), 128)
        return 0

    lax.fori_loop(0, TILES - 1, full, 0)
    step(TILES - 1, pl.ds(7 * 128, LAST), LAST)


def greet(n, all_images=True, partner=True):
    barrier = pltpu.get_barrier_semaphore()
    me = lax.axis_index("img")
    count = 0
    if all_images:
        for_each(
            n - 1,
            lambda d: pl.semaphore_signal(
                barrier, 1, device_id={"img": lax.rem(me + d + 1, n)}, device_id_type=MESH
            ),
        )
        count += n - 1
    if partner:
        pl.semaphore_signal(
            barrier, 1, device_id={"ch": 1 - lax.axis_index("ch")}, device_id_type=MESH
        )
        count += 1
    return lambda: pl.semaphore_wait(barrier, count)


class Gather:
    def __init__(self, n, source, target, send, recv):
        self.n, self.source, self.target, self.send, self.recv = n, source, target, send, recv
        self.me = lax.axis_index("img")

    def copy(self, d):
        return pltpu.make_async_remote_copy(
            src_ref=self.source,
            dst_ref=self.target.at[self.me],
            send_sem=self.send.at[d],
            recv_sem=self.recv.at[d],
            device_id={"img": lax.rem(self.me + d + 1, self.n)},
            device_id_type=MESH,
        )

    def start(self):
        for_each(self.n - 1, lambda d: self.copy(d).start())
        self.target[self.me] = self.source[...]

    def wait(self):
        for_each(self.n - 1, lambda d: self.copy(d).wait())


def swap(source, target, send, recv):
    return pltpu.make_async_remote_copy(
        src_ref=source,
        dst_ref=target,
        send_sem=send,
        recv_sem=recv,
        device_id={"ch": 1 - lax.axis_index("ch")},
        device_id_type=MESH,
    )


def put_span(ref, span, rows, value, add=False):
    left, right = value[:, :128], value[:, 128:]
    width = right.shape[1]
    if add:
        ref[2 * span, rows, :] += left
        ref[2 * span + 1, rows, 0:width] += right
    else:
        ref[2 * span, rows, :] = left
        ref[2 * span + 1, rows, 0:width] = right


def norm_constants(n, stats, live, gain_shift, consts):
    def total(step):
        return lax.fori_loop(0, n, lambda i, acc: acc + step(i), jnp.zeros((TILES, 128), F32))

    number = total(lambda i: live[i])
    average = total(lambda i: live[i] * stats[i, 0]) / number

    def centred(i):
        off = stats[i, 0] - average
        return stats[i, 1] + live[i] * off * off

    variance = total(centred) / number
    consts[0] = average
    consts[1] = lax.rsqrt(variance + EPSILON)
    consts[2] = gain_shift[0]
    consts[3] = gain_shift[1]
    consts[4] = number


def back_constants(n, sums, consts, grads):
    shift_grad = lax.fori_loop(
        0, n, lambda i, acc: acc + sums[i, 0], jnp.zeros((TILES, 128), F32)
    )
    gain_grad = lax.fori_loop(
        0, n, lambda i, acc: acc + sums[i, 1], jnp.zeros((TILES, 128), F32)
    )
    grads[0] = gain_grad
    grads[1] = shift_grad
    consts[5] = shift_grad / consts[4]
    consts[6] = gain_grad / consts[4]
    consts[7] = consts[1] * consts[2]


def row_of(consts, k, j):
    return consts[k, pl.ds(j, 1), :]


def natural_stats(ref, mask, count, local):
    def step(j):
        x = ref[j]
        m = mask[...]
        average = jnp.sum(x * m, axis=0, keepdims=True) / count
        off = x - average
        local[0, pl.ds(j, 1), :] = average
        local[1, pl.ds(j, 1), :] = jnp.sum(m * off * off, axis=0, keepdims=True)

    for_tiles(step)


def crop_sum(value, mask10):
    big = jnp.sum(value[:BIG_ROWS], axis=0)
    small = jnp.sum(value[BIG_ROWS:].reshape(9, 10, IMGS, 128), axis=0)
    return big + jnp.sum(small * mask10[...], axis=0)


def crop_stats(ref, mask10, count, local):
    def step(j):
        x = ref[j].reshape(ROWS_IMG, IMGS, 128)
        average = jnp.sum(crop_sum(x, mask10), axis=0, keepdims=True) / count
        off = x - average[None]
        local[0, pl.ds(j, 1), :] = average
        local[1, pl.ds(j, 1), :] = jnp.sum(crop_sum(off * off, mask10), axis=0, keepdims=True)

    for_tiles(step)


def window(ref, tiles, dy, dx, big):
    pieces = []
    for y in range(7 if big else 3):
        start = big_place(y + dy, dx) if big else small_place(y + dy, dx)
        rows = slice(start, start + (112 if big else 240))
        pieces.append(jnp.concatenate([ref[t, rows, :] for t in tiles], axis=1))
    return jnp.concatenate(pieces, axis=0)


def span_groups(span):
    return range(span * 256 // GROUP_WIDTH, min(18, (span * 256 + 255) // GROUP_WIDTH + 1))


def span_masks(span):
    lane = lax.broadcasted_iota(jnp.int32, (GROUP_WIDTH, 256), 1) + span * 256
    return [(lane >= g * GROUP_WIDTH) & (lane < (g + 1) * GROUP_WIDTH) for g in span_groups(span)]


def tap_rows(kernel, tap, span):
    first = tap * GROUP_WIDTH
    start = first // 16 * 16
    end = min(9 * GROUP_WIDTH, (first + GROUP_WIDTH + 15) // 16 * 16)
    a, b = SPANS[span]
    piece = kernel[start:end, a:b].astype(F32)[first - start : first - start + GROUP_WIDTH]
    if b - a < 256:
        piece = jnp.concatenate([piece, jnp.zeros((GROUP_WIDTH, 256 - (b - a)), F32)], axis=1)
    return piece


def build_band(kernel, span, band):
    first, end = WINDOWS[span]
    depth = (end - first) * 128
    groups = span_groups(span)
    masks = span_masks(span)
    head = groups[0] * GROUP_WIDTH - first * 128
    tail = depth - head - len(groups) * GROUP_WIDTH
    for tap in range(9):
        piece = tap_rows(kernel, tap, span)
        parts = [jnp.where(m, piece, 0.0) for m in masks]
        if head:
            parts.insert(0, jnp.zeros((head, 256), F32))
        if tail:
            parts.append(jnp.zeros((tail, 256), F32))
        band[0:depth, tap * 256 : tap * 256 + 256] = jnp.concatenate(parts, axis=0).astype(BF16)


def zero_pads(ref, j):
    for row in ZERO_ROWS:
        ref[j, row : row + 16, :] = jnp.zeros((16, 128), BF16)


def halves(value):
    high = value.astype(BF16)
    return high, (value - high.astype(F32)).astype(BF16)


def fine_dot(left, right_high, right_low, dims=((1,), (0,))):
    high, low = halves(left)
    both = jnp.concatenate([high.astype(F32), low.astype(F32)], axis=0).astype(BF16)
    value = dot(both, right_high, dims)
    return value[:IMGS] + value[IMGS:] + dot(both, right_low, dims)[:IMGS]


def load_vectors(gain, shift, norm):
    norm[...] = jnp.zeros_like(norm)
    for k, row in enumerate((gain, shift)):
        for j in range(TILES):
            width = 128 if j < 7 else LAST
            norm[k, j : j + 1, 0:width] = row[:, j * 128 : j * 128 + width]


def load_counts(n, crops, counts, live):
    me = lax.axis_index("img")
    for image in range(IMGS):
        counts[image : image + 1, :] = jnp.full((1, 128), crops[me * IMGS + image], jnp.int32)

    def device(d):
        total = crops[d * IMGS]
        for image in range(1, IMGS):
            total = total + crops[d * IMGS + image]
        rows = (IMGS * BIG_ROWS + 9 * total).astype(F32)
        live[d] = jnp.full((TILES, 128), rows, F32)

    for_each(n, device)


def live_slots(counts, mask10):
    for slot in range(10):
        mask10[slot] = (counts[...] > slot).astype(F32)


def natural_mask(mask10, mask):
    for tile in range(ROWS_IMG):
        there = pl.ds(natural_row(tile), IMGS, stride=ROWS_IMG)
        if tile < BIG_ROWS:
            mask[there, :] = jnp.ones((IMGS, 128), F32)
        else:
            mask[there, :] = mask10[(tile - BIG_ROWS) % 10]


def forward_kernel(n, *refs):
    r = Refs(refs)
    pixels_any, weight1_any, weight3_any, kernel_any, squeeze_any, excite_any, output_any = r.take(7)
    crops, vectors, squeeze_b, excite_b = r.take(), r.take(6), r.take(), r.take()
    first_out, pixels_out, far_out, padded_out, group_out, scaled_out, scaled_far_out = r.take(7)
    last_out, merged_out, block_out = r.take(3)
    far1, far3 = r.take(2)
    split_outs = r.take(4)
    stats1, stats2, stats3, sums3 = r.take(4)
    pooled, pooled_far, squeezed, squeezed_far, squeeze_pre, excited = r.take(6)
    factor_sums = r.take()
    counts, live, norms = r.take(), r.take(), r.take(3)
    consts, local, buf_a, buf_b, pixels, far, weight, zone = r.take(8)
    kernel_low, squeeze_w, excite_w = r.take(3)
    splits = r.take(4)
    turned, mask, mask10 = r.take(3)
    bands = r.take(4)
    load, store, swap_s, swap_r, tile_s, tile_r, small_s, small_r = r.take(8)
    gathers = [r.take(2) for _ in range(4)]
    factor_column, factors = r.take(2)
    factor = Part(n, ORDERS[0], r.take(2))
    ch = lax.axis_index("ch")
    wait_all = greet(n)
    loads = [
        fetch(source, target, load.at[k])
        for k, (source, target) in enumerate(
            (
                (pixels_any, pixels),
                (weight1_any, weight),
                (kernel_any, kernel_low),
                (squeeze_any, squeeze_w),
                (excite_any, excite_w),
            )
        )
    ]
    own = pl.multiple_of(ch * HALF, 16)
    away = pl.multiple_of((1 - ch) * HALF, 16)
    load_counts(n, crops, counts, live)
    for k in range(3):
        load_vectors(vectors[2 * k], vectors[2 * k + 1], norms[k])
    live_slots(counts, mask10)
    natural_mask(mask10, mask)
    count = live[lax.axis_index("img")][0:1, :]
    wait_all()
    chunks = ((0, 384), (384, 384), (768, 384), (1152, 352))
    swaps = []
    for k, (start, size) in enumerate(chunks):
        rows = pl.ds(start, size)
        swaps.append(swap(pixels_any.at[rows], far.at[rows], swap_s.at[k], swap_r.at[k]))
        swaps[-1].start()
    loads[0].wait()
    loads[1].wait()
    for t, (a, b) in enumerate(SPANS):
        put_span(buf_a, t, slice(0, ROWS), dot(pixels[...], weight[pl.ds(own, HALF), a:b]))
    buf_a[7, :, LAST:128] = jnp.zeros((ROWS, 128 - LAST), F32)
    for k, (start, size) in enumerate(chunks):
        swaps[k].wait()
        rows = slice(start, start + size)
        for t, (a, b) in enumerate(SPANS):
            put_span(buf_a, t, rows, dot(far[rows, :], weight[pl.ds(away, HALF), a:b]), add=True)
    natural_stats(buf_a, mask, count, local)
    gather = Gather(n, local, stats1, *gathers[0])
    gather.start()
    weight_swaps = [
        swap(w.at[pl.ds(away, HALF)], f, swap_s.at[4 + k], swap_r.at[4 + k])
        for k, (w, f) in enumerate(((weight1_any, far1), (weight3_any, far3)))
    ]
    for s in weight_swaps:
        s.start()
    load_weight = fetch(weight3_any, weight, load.at[0])
    mine_rows, far_rows = pl.ds(0, ROWS), pl.ds(ROWS, ROWS)
    for source, start in ((pixels, 0), (far, ROWS)):
        for j in range(TILES):
            width = 128 if j < 7 else LAST
            lanes = slice(j * 128, j * 128 + width)
            zone[j, start : start + ROWS, 0:width] = source[:, lanes]
    zone[7, :, LAST:128] = jnp.zeros((2 * ROWS, 128 - LAST), BF16)
    store_pixels = [
        fetch(zone.at[:, mine_rows], pixels_out, store.at[0]),
        fetch(zone.at[:, far_rows], far_out, store.at[12]),
    ]
    stores = []
    store_first = fetch(buf_a, first_out, store.at[1])
    loads[2].wait()
    for span in range(4):
        build_band(kernel_low, span, bands[span])
    loads[3].wait()
    loads[4].wait()
    for k, w in enumerate((squeeze_w, excite_w)):
        splits[2 * k][...], splits[2 * k + 1][...] = halves(w[...])
    stores += [fetch(splits[k], split_outs[k], store.at[2 + k]) for k in range(4)]
    load_output = fetch(output_any, far, load.at[1])
    for s in store_pixels:
        s.wait()
    gather.wait()
    norm_constants(n, stats1, live, norms[0], consts)

    def activate_first(j):
        average = row_of(consts, 0, j)
        scale = row_of(consts, 1, j) * row_of(consts, 2, j)
        shift = row_of(consts, 3, j)
        zero_pads(zone, j)
        for tile in range(0, ROWS_IMG, 2):
            both = []
            for half in range(2):
                x = buf_a[j, pl.ds(natural_row(tile + half), IMGS, stride=ROWS_IMG), :]
                pre = (x - average) * scale + shift
                both.append(pre * sigmoid(pre))
            row = padded_row(tile)
            zone[j, row : row + 16, :] = jnp.concatenate(both, axis=0).astype(BF16)

    for_tiles(activate_first)
    store_padded = fetch(zone.at[:, pl.ds(0, PAD_ROWS)], padded_out, store.at[6])
    for span, (start, end) in enumerate(WINDOWS):
        tiles = range(start, end)
        right = jnp.concatenate(
            [bands[span][:, tap * 256 : tap * 256 + 256] for tap in range(9)], axis=0
        )
        for big in (True, False):
            left = jnp.concatenate([window(zone, tiles, dy, dx, big) for dy, dx in TAPS], axis=1)
            rows = slice(0, 784) if big else slice(784, ROWS)
            put_span(buf_b, span, rows, dot(left, right))
    crop_stats(buf_b, mask10, count, local)
    gather = Gather(n, local, stats2, *gathers[1])
    gather.start()
    store_group = fetch(buf_b, group_out, store.at[7])
    store_first.wait()
    store_padded.wait()
    gather.wait()
    norm_constants(n, stats2, live, norms[1], consts)
    inverse = 1.0 / (BIG_ROWS + 9.0 * counts[...].astype(F32))

    def activate_group(j):
        average = row_of(consts, 0, j)
        scale = row_of(consts, 1, j) * row_of(consts, 2, j)
        pre = (buf_b[j] - average) * scale + row_of(consts, 3, j)
        value = pre * sigmoid(pre)
        buf_a[j] = value
        pooled[j] = crop_sum(value.reshape(ROWS_IMG, IMGS, 128), mask10) * inverse

    for_tiles(activate_group)
    pool_swap = swap(pooled, pooled_far, small_s.at[0], small_r.at[0])
    pool_swap.start()
    pool_swap.wait()
    mine = jnp.concatenate([pooled[j] for j in range(TILES)], axis=1)[:, :HALF]
    theirs = jnp.concatenate([pooled_far[j] for j in range(TILES)], axis=1)[:, :HALF]
    is_low = ch == 0
    high, low = splits[0], splits[1]
    pre = (
        fine_dot(jnp.where(is_low, mine, theirs), high[0:HALF, :], low[0:HALF, :])
        + fine_dot(jnp.where(is_low, theirs, mine), high[HALF:, :], low[HALF:, :])
        + squeeze_b[...]
    )
    squeeze_pre[...] = pre
    squeezed[...] = pre * sigmoid(pre)
    squeeze_swap = swap(squeezed, squeezed_far, small_s.at[1], small_r.at[1])
    squeeze_swap.start()
    squeeze_swap.wait()
    mine, theirs = squeezed[...], squeezed_far[...]
    width = mine.shape[1]
    high, low = splits[2], splits[3]
    gate = sigmoid(
        fine_dot(jnp.where(is_low, mine, theirs), high[0:width, :], low[0:width, :])
        + fine_dot(jnp.where(is_low, theirs, mine), high[width:, :], low[width:, :])
        + excite_b[...]
    )
    excited[7] = jnp.zeros((IMGS, 128), F32)
    for j in range(TILES - 1):
        excited[j] = gate[:, j * 128 : j * 128 + 128]
    excited[7, :, 0:LAST] = gate[:, 7 * 128 :]
    pack_factors((pooled, pooled_far), (squeezed, squeezed_far), factors)
    factor_column[factor.place[2]] = factors[...]
    factor.spread2(factor_column)

    def tile_swap(j):
        return swap(zone.at[j, mine_rows], zone.at[j, far_rows], tile_s.at[j], tile_r.at[j])

    def apply(j):
        gate_j = excited[j]
        for tile in range(ROWS_IMG):
            turned[pl.ds(natural_row(tile), IMGS, stride=ROWS_IMG), :] = (
                buf_a[j, tile * 8 : tile * 8 + 8, :] * gate_j
            )
        zone[j, 0:ROWS, :] = turned[...].astype(BF16)
        tile_swap(j).start()

    for_tiles(apply)
    stores.append(fetch(zone.at[:, mine_rows], scaled_out, store.at[8]))
    load_weight.wait()
    store_group.wait()
    for t, (a, b) in enumerate(SPANS):
        left = jnp.concatenate([zone[j, 0:ROWS, :] for j in range(TILES)], axis=1)[:, :HALF]
        put_span(buf_b, t, slice(0, ROWS), dot(left, weight[pl.ds(own, HALF), a:b]))
    buf_b[7, :, LAST:128] = jnp.zeros((ROWS, 128 - LAST), F32)
    factor.spread1(factor_column, factor_sums)
    for_tiles(lambda j: tile_swap(j).wait())
    stores.append(fetch(zone.at[:, far_rows], scaled_far_out, store.at[9]))
    for t, (a, b) in enumerate(SPANS):
        left = jnp.concatenate([zone[j, ROWS : 2 * ROWS, :] for j in range(TILES)], axis=1)[:, :HALF]
        put_span(buf_b, t, slice(0, ROWS), dot(left, weight[pl.ds(away, HALF), a:b]), add=True)
    natural_stats(buf_b, mask, count, local)
    gather = Gather(n, local, stats3, *gathers[2])
    gather.start()
    stores.append(fetch(buf_b, last_out, store.at[10]))
    factor.spread0(factor_sums)
    buf_a[7, :, LAST:128] = jnp.zeros((ROWS, 128 - LAST), F32)
    load_output.wait()
    gather.wait()
    norm_constants(n, stats3, live, norms[2], consts)
    local[...] = jnp.zeros_like(local)

    def merge(j, lanes, width):
        def vec(k):
            return consts[k, pl.ds(j, 1), 0:width]

        m = mask[:, 0:width]
        normed = (buf_b[j, :, 0:width] - vec(0)) * vec(1)
        merged = pixels[:, lanes].astype(F32) + normed * vec(2) + vec(3)
        s = sigmoid(merged)
        grad = far[:, lanes].astype(F32) * m * slope_of(merged, s)
        far[:, lanes] = (merged * s * m).astype(BF16)
        buf_a[j, :, 0:width] = grad
        local[0, pl.ds(j, 1), 0:width] = jnp.sum(grad, axis=0, keepdims=True)
        local[1, pl.ds(j, 1), 0:width] = jnp.sum(grad * normed, axis=0, keepdims=True)

    for_ragged_tiles(merge)
    gather = Gather(n, local, sums3, *gathers[3])
    gather.start()
    stores.append(fetch(buf_a, merged_out, store.at[11]))
    stores.append(fetch(far, block_out, store.at[13]))
    for s in weight_swaps + stores:
        s.wait()
    factor.settle()
    gather.wait()


def part_extents(n, order):
    sizes = image_axes(n)
    return tuple(sizes[a] for a in order)


def part_shape(n, order, rows):
    return part_extents(n, order) + (rows // n, 128)


def put_blocks(target, tile, tile_rows, start, value):
    _, e1, e2, rows, _ = target.shape
    size = value.shape[0]
    first = start
    while first < start + size:
        block = tile * (tile_rows // rows) + first // rows
        inside = first % rows
        take = min(rows - inside, start + size - first)
        place = (block // (e1 * e2), block // e2 % e1, block % e2)
        target[place[0], place[1], place[2], inside : inside + take, :] = value[
            first - start : first - start + take
        ]
        first += take


def weight_grad(left_span, right_tiles, target, spans):
    for a, b in SPANS:
        left = left_span(a, b)
        for k, span in enumerate(spans):
            right = jnp.concatenate([right_tiles(2 * span), right_tiles(2 * span + 1)], axis=1)
            value = dot(left, right, ((0,), (0,))).astype(BF16)
            put_blocks(target, 2 * k, 1024, a, value[:, :128])
            put_blocks(target, 2 * k + 1, 1024, a, value[:, 128:])


def tile_span(tile):
    def span(a, b):
        tiles = range(a // 128, (b + 127) // 128)
        return jnp.concatenate([tile(t) for t in tiles], axis=1)[:, : b - a]

    return span


def image_axes(n):
    return {16: (2, 2, 4), 128: (4, 4, 8)}.get(n, (n, 1, 1))


class Part:
    def __init__(self, n, order, sems):
        sizes = image_axes(n)
        strides = (1, sizes[0], sizes[0] * sizes[1])
        self.me = lax.axis_index("img")
        self.sizes = [sizes[a] for a in order]
        self.strides = [strides[a] for a in order]
        self.place = [lax.rem(self.me // s, e) for s, e in zip(self.strides, self.sizes)]
        self.sems = sems
        self.live = []

    def send(self, axis, stage, source, target):
        for d in range(1, self.sizes[axis]):
            q = lax.rem(self.place[axis] + d, self.sizes[axis])
            peer = self.me + (q - self.place[axis]) * self.strides[axis]
            copy = pltpu.make_async_remote_copy(
                src_ref=source(q),
                dst_ref=target(d),
                send_sem=self.sems[0].at[stage, d],
                recv_sem=self.sems[1].at[stage, d],
                device_id={"img": peer},
                device_id_type=MESH,
            )
            copy.start()
            self.live.append(copy)

    def keep(self, source, target, stage):
        copy = pltpu.make_async_copy(source, target, self.sems[0].at[stage, 0])
        copy.start()
        self.live.append(copy)

    def settle(self):
        for copy in self.live:
            copy.wait()
        self.live = []

    def add(self, target, own, arrived):
        total = own[...].astype(F32)
        for block in arrived:
            total = total + block[...].astype(F32)
        target[...] = total.astype(BF16)

    def send0(self, source, r0):
        self.send(0, 0, lambda q: source.at[q], lambda d: r0.at[d - 1])

    def sum0(self, source, r0, a0):
        self.settle()
        for k in range(self.sizes[1]):
            self.add(
                a0.at[k],
                source.at[self.place[0], k],
                [r0.at[d, k] for d in range(self.sizes[0] - 1)],
            )

    def send1(self, a0, r1):
        self.send(1, 1, lambda q: a0.at[q], lambda d: r1.at[d - 1])

    def sum1(self, a0, r1, a1):
        self.settle()
        self.add(a1, a0.at[self.place[1]], [r1.at[d] for d in range(self.sizes[1] - 1)])

    def send2(self, a1, r2):
        self.send(2, 2, lambda q: a1.at[q], lambda d: r2.at[d - 1])

    def sum2(self, a1, r2, column):
        self.settle()
        p2 = self.place[2]
        self.add(column.at[p2], a1.at[p2], [r2.at[d] for d in range(self.sizes[2] - 1)])

    def spread2(self, column):
        block = column.at[self.place[2]]
        self.send(2, 3, lambda q: block, lambda d: block)

    def spread1(self, column, result):
        self.settle()
        block = result.at[self.place[0], self.place[1]]
        self.send(1, 4, lambda q: column, lambda d: block)
        self.keep(column, block, 4)

    def spread0(self, result):
        self.settle()
        block = result.at[self.place[0]]
        self.send(0, 5, lambda q: block, lambda d: block)

    @staticmethod
    def room(n, order, shape):
        e0, e1, e2, rows, lanes = shape
        return (
            (max(e0 - 1, 1), e1, e2, rows, lanes),
            (e1, e2, rows, lanes),
            (max(e1 - 1, 1), e2, rows, lanes),
            (e2, rows, lanes),
            (max(e2 - 1, 1), rows, lanes),
            (e2, rows, lanes),
        )


def part_sems(n, count):
    most = max(image_axes(n))
    return [DMA((6, most)) for _ in range(2 * count)]


def fetch(source, target, sem):
    copy = pltpu.make_async_copy(source, target, sem)
    copy.start()
    return copy


class Refs:
    def __init__(self, refs):
        self.refs = list(refs)

    def take(self, count=None):
        if count is None:
            return self.refs.pop(0)
        head, self.refs = self.refs[:count], self.refs[count:]
        return head


ORDERS = ((0, 1, 2), (1, 0, 2), (0, 1, 2), (1, 0, 2))
KERNEL_ORDERS = ORDERS[:2]
AHEAD_TILES = 20
BACK_TILES = 10


def last_grad_kernel(n, *refs):
    r = Refs(refs)
    last_any, merged_any, group_any, scaled_any, scaled_far_any, weight_any, weight_far_any = r.take(7)
    stats3, live, sums3 = r.take(3)
    stats2, counts, norm2, norm3, excited, squeeze_pre = r.take(6)
    split_anys = r.take(4)
    pre_grad, sums2, excite_grad, squeeze_grad, vectors = r.take(5)
    done1, arrive2, mid3 = r.take(2), r.take(2), r.take(2)
    consts, consts2, local, buf_a, buf_b, low, low_far, scaled, scaled_far = r.take(9)
    weight, weight_far, mask, mask10 = r.take(4)
    splits = r.take(4)
    terms, terms_in, pool_terms, pool_in, pool_tiles = r.take(5)
    grads, rooms, mid1, arrive1 = r.take(4), r.take(4), r.take(2), r.take(2)
    load, swap_s, swap_r, small_s, small_r, send, recv = r.take(7)
    sems = r.take(8)
    ch = lax.axis_index("ch")
    own = pl.multiple_of(ch * HALF, 16)
    wait_all = greet(n)
    loads = [
        fetch(source, target, load.at[k])
        for k, (source, target) in enumerate(
            (
                (last_any, buf_a),
                (merged_any, buf_b),
                (scaled_any, scaled),
                (scaled_far_any, scaled_far),
                (weight_any.at[pl.ds(own, HALF)], weight),
                (weight_far_any, weight_far),
                *zip(split_anys, splits),
            )
        )
    ]
    live_slots(counts, mask10)
    natural_mask(mask10, mask)
    inverse = 1.0 / (BIG_ROWS + 9.0 * counts[...].astype(F32))
    norm_constants(n, stats3, live, norm3, consts)
    back_constants(n, sums3, consts, vectors)
    norm_constants(n, stats2, live, norm2, consts2)
    parts = [Part(n, order, sems[2 * k : 2 * k + 2]) for k, order in enumerate(ORDERS)]
    wait_all()
    loads[0].wait()
    loads[1].wait()

    def step(j):
        normed = (buf_a[j] - row_of(consts, 0, j)) * row_of(consts, 1, j)
        inner = buf_b[j] - row_of(consts, 5, j) - normed * row_of(consts, 6, j)
        low[j] = (mask[...] * row_of(consts, 7, j) * inner).astype(BF16)
        swap(low.at[j], low_far.at[j], swap_s.at[j], swap_r.at[j]).start()

    for_tiles(step)
    load_group = fetch(group_any, buf_a, load.at[0])
    for part in range(4):
        if part < 2:
            loads[2 + part].wait()
        rows = (scaled, scaled_far)[part % 2]
        left = tile_span(lambda t: rows[t])
        weight_grad(left, lambda t: low[t], grads[part], (0, 1) if part < 2 else (2, 3))
        if part < 2:
            parts[part].send0(grads[part], rooms[part])
    loads[4].wait()
    for t, (a, b) in enumerate(SPANS):
        left = jnp.concatenate([low[j] for j in range(TILES)], axis=1)[:, :HALF]
        put_span(buf_b, t, slice(0, ROWS), dot(left, weight[a:b, :], ((1,), (1,))))
    buf_b[7, :, LAST:128] = jnp.zeros((ROWS, 128 - LAST), F32)
    for_tiles(lambda j: swap(low.at[j], low_far.at[j], swap_s.at[j], swap_r.at[j]).wait())
    loads[5].wait()
    for t, (a, b) in enumerate(SPANS):
        left = jnp.concatenate([low_far[j] for j in range(TILES)], axis=1)[:, :HALF]
        put_span(
            buf_b, t, slice(0, ROWS), dot(left, weight_far[a:b, :], ((1,), (1,))), add=True
        )
    load_group.wait()

    def gate_sum(j):
        average = row_of(consts2, 0, j)
        scale = row_of(consts2, 1, j) * row_of(consts2, 2, j)
        shift = row_of(consts2, 3, j)
        total = jnp.zeros((IMGS, 128), F32)
        for tile in range(ROWS_IMG):
            pre = (buf_a[j, tile * 8 : tile * 8 + 8, :] - average) * scale + shift
            act = pre * sigmoid(pre)
            total = total + act * buf_b[j, pl.ds(natural_row(tile), IMGS, stride=ROWS_IMG), :]
        gate = excited[j]
        excite_grad[j] = total * gate * (1.0 - gate)

    for_tiles(gate_sum)
    for k in range(2):
        parts[k].sum0(grads[k], rooms[k], mid1[k])
        parts[k].send1(mid1[k], arrive1[k])
    wide = jnp.concatenate([excite_grad[j] for j in range(TILES)], axis=1)[:, :HALF]
    width = squeeze_pre.shape[1]
    is_low = ch == 0
    for k in range(6, 10):
        loads[k].wait()
    across = ((1,), (1,))
    high, low_part = splits[2], splits[3]
    part0 = fine_dot(wide, high[0:width, :], low_part[0:width, :], across)
    part1 = fine_dot(wide, high[width:, :], low_part[width:, :], across)
    terms[...] = jnp.where(is_low, part1, part0)
    term_swap = swap(terms, terms_in, small_s.at[0], small_r.at[0])
    term_swap.start()
    term_swap.wait()
    pre = squeeze_pre[...]
    grad = (jnp.where(is_low, part0, part1) + terms_in[...]) * slope_of(pre, sigmoid(pre))
    squeeze_grad[...] = grad
    high, low_part = splits[0], splits[1]
    pool0 = fine_dot(grad, high[0:HALF, :], low_part[0:HALF, :], across)
    pool1 = fine_dot(grad, high[HALF:, :], low_part[HALF:, :], across)
    pool_terms[...] = jnp.where(is_low, pool1, pool0)
    pool_swap = swap(pool_terms, pool_in, small_s.at[1], small_r.at[1])
    pool_swap.start()
    pool_swap.wait()
    for k in range(2):
        parts[k].sum1(mid1[k], arrive1[k], done1[k])
        parts[k].send2(done1[k], arrive2[k])
        parts[k + 2].send0(grads[k + 2], rooms[k + 2])
    pool = jnp.where(is_low, pool0, pool1) + pool_in[...]
    pool_tiles[7, :, LAST:128] = jnp.zeros((IMGS, 128 - LAST), F32)
    for j in range(TILES):
        part = pool[:, j * 128 : min(HALF, j * 128 + 128)]
        pool_tiles[j, :, 0 : part.shape[1]] = part * inverse[:, 0 : part.shape[1]]

    def slopes(j):
        average, scale = row_of(consts2, 0, j), row_of(consts2, 1, j)
        gain, shift = row_of(consts2, 2, j), row_of(consts2, 3, j)
        gate, pooled = excited[j], pool_tiles[j]
        total = jnp.zeros((IMGS, 128), F32)
        total_normed = jnp.zeros((IMGS, 128), F32)
        for tile in range(ROWS_IMG):
            rows = slice(tile * 8, tile * 8 + 8)
            normed = (buf_a[j, rows, :] - average) * scale
            pre = normed * gain + shift
            lead = pooled if tile < BIG_ROWS else pooled * mask10[(tile - BIG_ROWS) % 10]
            act = buf_b[j, pl.ds(natural_row(tile), IMGS, stride=ROWS_IMG), :] * gate + lead
            grad = act * slope_of(pre, sigmoid(pre))
            buf_a[j, rows, :] = grad
            total = total + grad
            total_normed = total_normed + grad * normed
        local[0, pl.ds(j, 1), :] = jnp.sum(total, axis=0, keepdims=True)
        local[1, pl.ds(j, 1), :] = jnp.sum(total_normed, axis=0, keepdims=True)

    for_tiles(slopes)
    gather = Gather(n, local, sums2, send, recv)
    gather.start()
    store = fetch(buf_a, pre_grad, load.at[0])
    gather.wait()
    for k in range(2):
        parts[k].settle()
        parts[k + 2].sum0(grads[k + 2], rooms[k + 2], mid3[k])
    store.wait()


def pack_factors(wides, narrows, factors):
    tiles = [part[j] for part in wides for j in range(TILES)]
    for part in narrows:
        rest = part[:, 128:]
        blank = jnp.zeros((IMGS, 128 - rest.shape[1]), F32)
        tiles += [part[:, 0:128], jnp.concatenate([rest, blank], axis=1)]
    for k in range(0, len(tiles), 2):
        both = jnp.concatenate(tiles[k : k + 2], axis=0)
        factors[k * IMGS : (k + 2) * IMGS, :] = both.astype(BF16)


def tail_kernel(n, *refs):
    r = Refs(refs)
    pre_any, group_any, padded_any, first_any = r.take(4)
    pixels_any, pixels_far_any, weight_any, weight_far_any, merged_any = r.take(5)
    stats2, live, sums2, counts, norm1, norm2, kernel, stats1 = r.take(8)
    done1, arrive2, mid3 = r.take(2), r.take(2), r.take(2)
    factor_parts = r.take(2)
    pixels_grad, group_vectors, first_vectors = r.take(3)
    last_sums, first_sums, kernel_sums = r.take(4), r.take(4), r.take(2)
    factor_sums = r.take()
    consts, consts1, mask10, local, sums1 = r.take(5)
    buf_a, buf_b, zone1, zone2, weight, weight_far, turned = r.take(7)
    bands = r.take(2)
    arrive3, done3, arrive4, last_columns = r.take(2), r.take(2), r.take(2), r.take(4)
    grads = r.take(4)
    first_rooms = [r.take(6) for _ in range(4)]
    kernel_grads = r.take(2)
    kernel_rooms = [r.take(6) for _ in range(2)]
    factor_column, factors = r.take(2)
    load, swap_s, swap_r, send, recv, free = r.take(6)
    sems = [r.take(2) for _ in range(11)]
    own = pl.multiple_of(lax.axis_index("ch") * HALF, 16)
    mine_rows, far_rows = pl.ds(0, ROWS), pl.ds(ROWS, ROWS)
    wait_all = greet(n)
    loads = [
        fetch(source, target, load.at[k])
        for k, (source, target) in enumerate(
            (
                (pre_any, buf_a),
                (group_any, buf_b),
                (padded_any, zone1.at[:, pl.ds(0, PAD_ROWS)]),
                (weight_any.at[pl.ds(own, HALF)], weight),
                (weight_far_any, weight_far),
            )
        )
    ]
    firsts = [Part(n, order, sems[k]) for k, order in enumerate(ORDERS)]
    lasts = [Part(n, order, sems[4 + k]) for k, order in enumerate(ORDERS)]
    kernels = [Part(n, KERNEL_ORDERS[k], sems[8 + k]) for k in range(2)]
    factor = Part(n, ORDERS[0], sems[10])
    live_slots(counts, mask10)
    norm_constants(n, stats2, live, norm2, consts)
    back_constants(n, sums2, consts, group_vectors)
    norm_constants(n, stats1, live, norm1, consts1)
    wait_all()

    def each(step, ks):
        for k in ks:
            step(k)

    def last1(k):
        lasts[k].sum1(mid3[k - 2], arrive3[k - 2], done3[k - 2])
        lasts[k].send2(done3[k - 2], arrive4[k - 2])

    def last2(k):
        lasts[k].sum2((*done1, *done3)[k], (*arrive2, *arrive4)[k], last_columns[k])
        lasts[k].spread2(last_columns[k])

    def last3(k):
        lasts[k].spread1(last_columns[k], last_sums[k])

    def last4(k):
        lasts[k].spread0(last_sums[k])

    def reducer(part, source, room, result):
        r0, a0, r1, a1, r2, column = room

        def stage0():
            part.send0(source, r0)

        def stage1():
            part.sum0(source, r0, a0)
            part.send1(a0, r1)

        def stage2():
            part.sum1(a0, r1, a1)
            part.send2(a1, r2)

        def stage3():
            part.sum2(a1, r2, column)
            part.spread2(column)

        return (
            stage0,
            stage1,
            stage2,
            stage3,
            lambda: part.spread1(column, result),
            lambda: part.spread0(result),
        )

    first = [reducer(firsts[k], grads[k], first_rooms[k], first_sums[k]) for k in range(4)]
    kernel_sum = [
        reducer(kernels[k], kernel_grads[k], kernel_rooms[k], kernel_sums[k]) for k in range(2)
    ]
    head, back, two = (0, 1), (2, 3), range(2)
    each(last2, head)
    for k in two:
        lasts[k + 2].send1(mid3[k], arrive3[k])
    for span in range(2):
        build_band(kernel, span, bands[span])
    loads[0].wait()
    loads[1].wait()

    def group_step(j):
        average, scale = row_of(consts, 0, j), row_of(consts, 1, j)
        less, slope, front = row_of(consts, 5, j), row_of(consts, 6, j), row_of(consts, 7, j)
        zero_pads(zone2, j)
        for tile in range(0, ROWS_IMG, 2):
            both = []
            for half in range(2):
                rows = slice(tile * 8 + half * 8, tile * 8 + half * 8 + 8)
                normed = (buf_b[j, rows, :] - average) * scale
                grad = front * (buf_a[j, rows, :] - less - normed * slope)
                if tile >= BIG_ROWS:
                    grad = grad * mask10[(tile + half - BIG_ROWS) % 10]
                both.append(grad)
            row = padded_row(tile)
            zone2[j, row : row + 16, :] = jnp.concatenate(both, axis=0).astype(BF16)

    for_tiles(group_step)
    load_first = fetch(first_any, buf_b, load.at[0])
    each(last1, back)
    pack_factors(factor_parts[:1], factor_parts[1:], factors)
    factor_column[factor.place[2]] = factors[...]
    factor.spread2(factor_column)
    loads[2].wait()
    started = 0
    for span, (start, end) in enumerate(WINDOWS):
        tiles = (2 * span, 2 * span + 1)
        depth = (end - start) * 128
        band = bands[span % 2]
        if span >= 2:
            build_band(kernel, span, band)
        shifted = [
            [window(zone2, tiles, -dy, -dx, big) for dy, dx in TAPS] for big in (True, False)
        ]
        for rows, left in ((slice(0, 784), shifted[0]), (slice(784, ROWS), shifted[1])):
            value = dot(jnp.concatenate(left, axis=1), band[0:depth, :], ((1,), (1,)))
            for t in range(start, end):
                part = value[:, (t - start) * 128 : (t - start) * 128 + 128]
                if t < started:
                    buf_a[t, rows, :] += part
                else:
                    buf_a[t, rows, :] = part
        started = end
        masks = span_masks(span)
        left = jnp.concatenate(
            [window(zone1, range(start, end), 0, 0, big) for big in (True, False)], axis=0
        )
        pieces = []
        for tap in range(9):
            right = jnp.concatenate([shifted[0][tap], shifted[1][tap]], axis=0)
            value = dot(left, right, ((0,), (0,)))
            piece = jnp.zeros((GROUP_WIDTH, 256), F32)
            for g, inside in zip(span_groups(span), masks):
                row = g * GROUP_WIDTH - start * 128
                piece = jnp.where(inside, value[row : row + GROUP_WIDTH], piece)
            pieces.append(piece)
        pieces.append(jnp.zeros((8, 256), F32))
        value = jnp.concatenate(pieces, axis=0).astype(BF16)
        for half in range(2):
            rows = slice(half * 256, half * 256 + 256)
            put_blocks(kernel_grads[half], 2 * span, 256, 0, value[rows, :128])
            put_blocks(kernel_grads[half], 2 * span + 1, 256, 0, value[rows, 128:])
        if span == 0:
            each(last3, head)
        elif span == 1:
            each(last4, head)
            factor.spread1(factor_column, factor_sums)
        elif span == 2:
            each(last2, back)
        else:
            for k in two:
                kernel_sum[k][0]()
            factor.spread0(factor_sums)
    pl.semaphore_signal(
        free, 1, device_id={"ch": 1 - lax.axis_index("ch")}, device_id_type=MESH
    )
    load_pixels = [
        fetch(pixels_any, zone2.at[:, mine_rows], load.at[1]),
        fetch(pixels_far_any, zone2.at[:, far_rows], load.at[2]),
    ]
    load_first.wait()

    def first_slopes(j):
        average, scale = row_of(consts1, 0, j), row_of(consts1, 1, j)
        gain, shift = row_of(consts1, 2, j), row_of(consts1, 3, j)
        total = jnp.zeros((IMGS, 128), F32)
        total_normed = jnp.zeros((IMGS, 128), F32)
        for tile in range(ROWS_IMG):
            rows = slice(tile * 8, tile * 8 + 8)
            x = buf_b[j, pl.ds(natural_row(tile), IMGS, stride=ROWS_IMG), :]
            normed = (x - average) * scale
            pre = normed * gain + shift
            grad = buf_a[j, rows, :] * slope_of(pre, sigmoid(pre))
            if tile >= BIG_ROWS:
                grad = grad * mask10[(tile - BIG_ROWS) % 10]
            buf_a[j, rows, :] = grad
            total = total + grad
            total_normed = total_normed + grad * normed
        local[0, pl.ds(j, 1), :] = jnp.sum(total, axis=0, keepdims=True)
        local[1, pl.ds(j, 1), :] = jnp.sum(total_normed, axis=0, keepdims=True)

    for_tiles(first_slopes)
    gather = Gather(n, local, sums1, send, recv)
    gather.start()
    each(last3, back)
    gather.wait()
    back_constants(n, sums1, consts1, first_vectors)

    def tile_swap(j):
        return swap(zone1.at[j, mine_rows], zone1.at[j, far_rows], swap_s.at[j], swap_r.at[j])

    def first_step(j):
        average, scale = row_of(consts1, 0, j), row_of(consts1, 1, j)
        less, slope, front = row_of(consts1, 5, j), row_of(consts1, 6, j), row_of(consts1, 7, j)
        for tile in range(ROWS_IMG):
            there = pl.ds(natural_row(tile), IMGS, stride=ROWS_IMG)
            normed = (buf_b[j, there, :] - average) * scale
            grad = front * (buf_a[j, tile * 8 : tile * 8 + 8, :] - less - normed * slope)
            if tile >= BIG_ROWS:
                grad = grad * mask10[(tile - BIG_ROWS) % 10]
            turned[there, :] = grad
        zone1[j, 0:ROWS, :] = turned[...].astype(BF16)
        tile_swap(j).start()

    pl.semaphore_wait(free, 1)
    for_tiles(first_step)
    load_merged = fetch(merged_any, buf_a, load.at[0])
    for s in load_pixels:
        s.wait()
    for part in range(4):
        side = slice(0, ROWS) if part % 2 == 0 else slice(ROWS, 2 * ROWS)
        weight_grad(
            tile_span(lambda t: zone2[t, side, :]),
            lambda t: zone1[t, 0:ROWS, :],
            grads[part],
            (0, 1) if part < 2 else (2, 3),
        )
        if part < 2:
            first[part][0]()
    for k in two:
        kernel_sum[k][1]()
    load_merged.wait()
    loads[3].wait()
    for t, (a, b) in enumerate(SPANS):
        left = jnp.concatenate([zone1[j, 0:ROWS, :] for j in range(TILES)], axis=1)[:, :HALF]
        put_span(buf_a, t, slice(0, ROWS), dot(left, weight[a:b, :], ((1,), (1,))), add=True)
    for_tiles(lambda j: tile_swap(j).wait())
    loads[4].wait()
    for t, (a, b) in enumerate(SPANS):
        left = jnp.concatenate([zone1[j, ROWS : 2 * ROWS, :] for j in range(TILES)], axis=1)
        put_span(
            buf_a, t, slice(0, ROWS), dot(left[:, :HALF], weight_far[a:b, :], ((1,), (1,))), add=True
        )
    store = fetch(buf_a, pixels_grad, load.at[0])

    def stage(sums, ks, number):
        for k in ks:
            sums[k][number]()

    stage(first, head, 1)
    stage(first, back, 0)
    stage(kernel_sum, two, 2)
    stage(first, head, 2)
    each(last4, back)
    stage(first, back, 1)
    stage(kernel_sum, two, 3)
    stage(first, head, 3)
    stage(first, back, 2)
    stage(kernel_sum, two, 4)
    stage(first, head, 4)
    stage(kernel_sum, two, 5)
    stage(first, head, 5)
    stage(first, back, 3)
    stage(first, back, 4)
    stage(first, back, 5)
    for part in (*firsts, *lasts, *kernels, factor):
        part.settle()
    store.wait()


def finish_kernel(*refs):
    r = Refs(refs)
    lasts, firsts, pixels_wide, kernels = r.take(4), r.take(4), r.take(), r.take(2)
    ahead, back, vectors = r.take(), r.take(), r.take(3)
    last_out, first_out, pixels_out, group_out, excite_w, excite_b = r.take(6)
    squeeze_w, squeeze_b, rows_out = r.take(), r.take(), r.take(6)
    behind, left0, left1 = r.take(3)
    ch = lax.axis_index("ch")
    j = pl.program_id(0)
    n = ahead.shape[0]
    se = squeeze_w.shape[1]

    @pl.when(j == 0)
    def _():
        behind[...] = back[...].astype(F32)
        before = ahead[...].astype(F32).reshape(n, AHEAD_TILES, IMGS, 128)

        def columns(start, tiles, width):
            parts = [before[:, t].reshape(n * IMGS, 128) for t in range(start, start + tiles)]
            return jnp.concatenate(parts, axis=1)[:, :width]

        tiles = [behind[:, t * IMGS : (t + 1) * IMGS, :].reshape(n * IMGS, 128) for t in (8, 9)]
        squeeze_all = jnp.concatenate(tiles, axis=1)[:, :se]
        squeeze_b[...] = jnp.sum(squeeze_all, axis=0, keepdims=True)
        squeeze_all = squeeze_all.astype(BF16)
        for start, place in ((0, ch), (8, 1 - ch)):
            rows = pl.ds(pl.multiple_of(place * HALF, 8), HALF)
            left = columns(start, 8, HALF).astype(BF16)
            squeeze_w[rows, :] = dot(left, squeeze_all, ((0,), (0,)))
        own, far = columns(16, 2, se), columns(18, 2, se)
        left0[...] = jnp.where(ch == 0, own, far).astype(BF16)
        left1[...] = jnp.where(ch == 0, far, own).astype(BF16)

    for sums, out in ((lasts, last_out), (firsts, first_out)):
        for late in range(2):

            @pl.when((j >= 4) == bool(late))
            def _():
                for k, place in ((0, ch), (1, 1 - ch)):
                    rows = pl.ds(pl.multiple_of(place * HALF, 8), HALF)
                    out[rows, :] = sums[2 * late + k][0, 0:HALF, :].astype(F32)

    pixels_out[...] = pixels_wide[0]
    split = kernels[0].shape[1]
    group_out[0:split, :] = kernels[0][0].astype(F32)
    group_out[split:, :] = kernels[1][0].astype(F32)[: 9 * GROUP_WIDTH - split]
    rows = pl.ds(pl.multiple_of(j * IMGS, IMGS), IMGS)
    excite = behind[:, rows, :].reshape(n * IMGS, 128)
    excite_b[...] = jnp.sum(excite, axis=0, keepdims=True)
    for k, left in enumerate((left0, left1)):
        excite_w[k * se : (k + 1) * se, :] = dot(left[...], excite.astype(BF16), ((0,), (0,)))
    for k in range(6):
        rows_out[k][...] = vectors[k // 2][k % 2, pl.ds(j, 1), :]


def call(kernel, ins, outs, scratch, ident=None, in_specs=None, out_specs=None, grid=()):
    params = {"vmem_limit_bytes": VMEM_LIMIT}
    if ident is not None:
        params.update(collective_id=ident, has_side_effects=True)
    return pl.pallas_call(
        kernel,
        grid=grid,
        out_shape=[jax.ShapeDtypeStruct(shape, dtype) for shape, dtype in outs],
        in_specs=in_specs or [VMEM] * len(ins),
        out_specs=out_specs or [VMEM] * len(outs),
        scratch_shapes=scratch,
        compiler_params=pltpu.CompilerParams(**params),
    )(*ins)


def body(
    n,
    pixels,
    crop_counts,
    first_weight,
    first_gain,
    first_shift,
    group_weight,
    group_gain,
    group_shift,
    squeeze_weight,
    squeeze_bias,
    excite_weight,
    excite_bias,
    last_weight,
    last_gain,
    last_shift,
    output_grad,
):
    assert pixels.shape == (ROWS, HALF)
    se = squeeze_weight.shape[1]
    wide = (TILES, ROWS, 128)
    stat = (n, 2, TILES, 128)
    sem = DMA((n - 1,))

    kernel = group_weight.reshape(9 * GROUP_WIDTH, HALF)
    local = pltpu.VMEM((2, TILES, 128), F32)
    consts = pltpu.VMEM((8, TILES, 128), F32)
    vectors = ((2, TILES, 128), F32)
    bands = [pltpu.VMEM(((e - s) * 128, 9 * 256), BF16) for s, e in WINDOWS]
    mask10 = pltpu.VMEM((10, IMGS, 128), F32)
    mask = pltpu.VMEM((ROWS, 128), F32)
    small = (TILES, IMGS, 128)
    wide_buf = pltpu.VMEM(wide, F32)
    tall = (ROWS, HALF)
    ahead_shape = part_extents(n, ORDERS[0]) + (AHEAD_TILES * IMGS, 128)
    back_shape = part_extents(n, ORDERS[0]) + (BACK_TILES * IMGS, 128)
    split_shapes = [(2 * HALF, se)] * 2 + [(2 * se, HALF)] * 2
    (
        first,
        pixels_tiles,
        pixels_far,
        padded,
        group,
        scaled,
        scaled_far,
        last,
        merged_grad,
        block_out,
        first_far,
        last_far,
        *rest,
    ) = call(
        functools.partial(forward_kernel, n),
        (
            pixels,
            first_weight,
            last_weight,
            kernel,
            squeeze_weight,
            excite_weight,
            output_grad,
            crop_counts,
            first_gain[None],
            first_shift[None],
            group_gain[None],
            group_shift[None],
            last_gain[None],
            last_shift[None],
            squeeze_bias[None],
            excite_bias[None],
        ),
        [
            (wide, F32),
            (wide, BF16),
            (wide, BF16),
            ((TILES, PAD_ROWS, 128), BF16),
            (wide, F32),
            (wide, BF16),
            (wide, BF16),
            (wide, F32),
            (wide, F32),
            (tall, BF16),
            ((HALF, HALF), BF16),
            ((HALF, HALF), BF16),
        ]
        + [(shape, BF16) for shape in split_shapes]
        + [(stat, F32)] * 4
        + [(small, F32)] * 2
        + [((IMGS, se), F32)] * 3
        + [(small, F32), (ahead_shape, BF16), ((IMGS, 128), jnp.int32), ((n, TILES, 128), F32)]
        + [vectors] * 3,
        [
            consts,
            local,
            wide_buf,
            wide_buf,
            pltpu.VMEM(tall, BF16),
            pltpu.VMEM(tall, BF16),
            pltpu.VMEM((2 * HALF, HALF), BF16),
            pltpu.VMEM((TILES, 2 * ROWS, 128), BF16),
            pltpu.VMEM((9 * GROUP_WIDTH, HALF), BF16),
            pltpu.VMEM((2 * HALF, se), F32),
            pltpu.VMEM((2 * se, HALF), F32),
            *(pltpu.VMEM(shape, BF16) for shape in split_shapes),
            mask,
            mask,
            mask10,
            *bands,
            DMA((6,)),
            DMA((14,)),
            DMA((6,)),
            DMA((6,)),
            DMA((TILES,)),
            DMA((TILES,)),
            DMA((2,)),
            DMA((2,)),
            *[sem] * 8,
            pltpu.VMEM(ahead_shape[2:], BF16),
            pltpu.VMEM(ahead_shape[3:], BF16),
            *part_sems(n, 1),
        ],
        0,
        in_specs=[ANY] * 7 + [pl.BlockSpec(memory_space=pltpu.SMEM)] + [VMEM] * 8,
        out_specs=[ANY] * 16 + [VMEM] * 10 + [ANY] + [VMEM] * 5,
    )
    splits, rest = rest[:4], rest[4:]
    stats1, stats2, stats3, sums3, pooled, pooled_far = rest[:6]
    squeezed, squeezed_far, squeeze_pre, excited, ahead_sums = rest[6:11]
    counts, live, norm1, norm2, norm3 = rest[11:]

    def vmem(shape, dtype=BF16):
        return pltpu.VMEM(shape, dtype)

    shapes = [part_shape(n, order, 4 * 1024) for order in ORDERS]
    rooms = [Part.room(n, order, shape) for order, shape in zip(ORDERS, shapes)]
    low_buf = vmem(wide)
    weight_buf = vmem((HALF, HALF))
    pre_grad, sums2, excite_grad, squeeze_grad, vectors3, *carry = call(
        functools.partial(last_grad_kernel, n),
        (
            last,
            merged_grad,
            group,
            scaled,
            scaled_far,
            last_weight,
            last_far,
            stats3,
            live,
            sums3,
            stats2,
            counts,
            norm2,
            norm3,
            excited,
            squeeze_pre,
            *splits,
        ),
        [(wide, F32), (stat, F32), (small, F32), ((IMGS, se), F32), vectors]
        + [(rooms[k][3], BF16) for k in range(2)]
        + [(rooms[k][4], BF16) for k in range(2)]
        + [(rooms[k][1], BF16) for k in (2, 3)],
        [
            consts,
            consts,
            local,
            wide_buf,
            wide_buf,
            low_buf,
            low_buf,
            low_buf,
            low_buf,
            weight_buf,
            weight_buf,
            mask,
            mask10,
            *(vmem(shape) for shape in split_shapes),
            vmem((IMGS, se), F32),
            vmem((IMGS, se), F32),
            vmem((IMGS, HALF), F32),
            vmem((IMGS, HALF), F32),
            vmem(small, F32),
            *(vmem(shape) for shape in shapes),
            *(vmem(room[0]) for room in rooms),
            *(vmem(room[1]) for room in rooms[:2]),
            *(vmem(room[2]) for room in rooms[:2]),
            DMA((10,)),
            DMA((TILES,)),
            DMA((TILES,)),
            DMA((2,)),
            DMA((2,)),
            sem,
            sem,
            *part_sems(n, 4),
        ],
        4,
        in_specs=[ANY] * 7 + [VMEM] * 9 + [ANY] * 4,
        out_specs=[ANY] + [VMEM] * 10,
    )
    done1, arrive2, mid3 = carry[0:2], carry[2:4], carry[4:6]
    kernel_shapes = [part_shape(n, order, TILES * 256) for order in KERNEL_ORDERS]
    kernel_rooms = [
        Part.room(n, order, shape) for order, shape in zip(KERNEL_ORDERS, kernel_shapes)
    ]
    kernel_shapes = [part_shape(n, order, TILES * 256) for order in KERNEL_ORDERS]
    kernel_rooms = [
        Part.room(n, order, shape) for order, shape in zip(KERNEL_ORDERS, kernel_shapes)
    ]
    zone = vmem((TILES, 2 * ROWS, 128))
    pixels_wide, vectors2, vectors1, *carry = call(
        functools.partial(tail_kernel, n),
        (
            pre_grad,
            group,
            padded,
            first,
            pixels_tiles,
            pixels_far,
            first_weight,
            first_far,
            merged_grad,
            stats2,
            live,
            sums2,
            counts,
            norm1,
            norm2,
            kernel,
            stats1,
            *done1,
            *arrive2,
            *mid3,
            excite_grad,
            squeeze_grad,
        ),
        [(wide, F32), vectors, vectors]
        + [(shape, BF16) for shape in shapes * 2 + kernel_shapes]
        + [(back_shape, BF16)],
        [
            consts,
            consts,
            mask10,
            local,
            vmem(stat, F32),
            wide_buf,
            wide_buf,
            zone,
            zone,
            weight_buf,
            weight_buf,
            vmem((ROWS, 128), F32),
            vmem((512, 9 * 256)),
            vmem((512, 9 * 256)),
            *(vmem(rooms[k][kind]) for kind in (2, 3, 4) for k in (2, 3)),
            *(vmem(room[5]) for room in rooms),
            *(vmem(shape) for shape in shapes),
            *(vmem(shape) for room in rooms for shape in room),
            *(vmem(shape) for shape in kernel_shapes),
            *(vmem(shape) for room in kernel_rooms for shape in room),
            vmem(back_shape[2:]),
            vmem(back_shape[3:]),
            DMA((5,)),
            DMA((TILES,)),
            DMA((TILES,)),
            sem,
            sem,
            pltpu.SemaphoreType.REGULAR,
            *part_sems(n, 11),
        ],
        5,
        in_specs=[ANY] * 9 + [VMEM] * 16,
        out_specs=[ANY, VMEM, VMEM] + [ANY] * 11,
    )
    sums = [s.reshape(4, 1024, 128) for s in carry[0:8]]
    kernel_sums = [s.reshape(TILES, 256, 128) for s in carry[8:10]]
    late = pl.BlockSpec((1, 1024, 128), lambda j: (jnp.maximum(j - 4, 0), 0, 0))
    early = pl.BlockSpec((1, 1024, 128), lambda j: (jnp.minimum(j, 3), 0, 0))

    def by_tile(rows):
        return pl.BlockSpec((rows, 128), lambda j: (0, j))

    def whole(shape):
        return pl.BlockSpec(shape, lambda j: (0,) * len(shape))

    ahead_all, back_all = ahead_sums.reshape(n, -1, 128), carry[10].reshape(n, -1, 128)
    half_kernel = pl.BlockSpec((1, 256, 128), lambda j: (j, 0, 0))
    results = call(
        finish_kernel,
        (*sums, pixels_wide, *kernel_sums, ahead_all, back_all, vectors1, vectors2, vectors3),
        [
            ((2 * HALF, HALF), F32),
            ((2 * HALF, HALF), F32),
            ((ROWS, HALF), F32),
            ((9 * GROUP_WIDTH, HALF), F32),
            ((2 * se, HALF), F32),
            ((1, HALF), F32),
            ((2 * HALF, se), F32),
            ((1, se), F32),
        ]
        + [((1, HALF), F32)] * 6,
        [
            vmem(back_all.shape, F32),
            vmem((n * IMGS, se)),
            vmem((n * IMGS, se)),
        ],
        in_specs=[early, early, late, late] * 2
        + [pl.BlockSpec((1, ROWS, 128), lambda j: (j, 0, 0)), half_kernel, half_kernel]
        + [whole(ahead_all.shape), whole(back_all.shape)]
        + [whole(vectors[0])] * 3,
        out_specs=[
            by_tile(2 * HALF),
            by_tile(2 * HALF),
            by_tile(ROWS),
            by_tile(9 * GROUP_WIDTH),
            by_tile(2 * se),
            by_tile(1),
            whole((2 * HALF, se)),
            whole((1, se)),
        ]
        + [by_tile(1)] * 6,
        grid=(TILES,),
    )
    last_weight_grad, first_weight_grad, pixels_grad, group_weight_grad = results[:4]
    excite_weight_grad, excite_bias_grad, squeeze_weight_grad, squeeze_bias_grad = results[4:8]
    rows = [result[0] for result in results[8:]]
    first_gain_grad, first_shift_grad = rows[0:2]
    group_gain_grad, group_shift_grad = rows[2:4]
    last_gain_grad, last_shift_grad = rows[4:6]
    group_weight_grad = group_weight_grad.reshape(3, 3, GROUP_WIDTH, HALF)
    squeeze_bias_grad, excite_bias_grad = squeeze_bias_grad[0], excite_bias_grad[0]
    return (
        block_out,
        pixels_grad,
        first_weight_grad,
        first_gain_grad,
        first_shift_grad,
        group_weight_grad,
        group_gain_grad,
        group_shift_grad,
        squeeze_weight_grad,
        squeeze_bias_grad,
        excite_weight_grad,
        excite_bias_grad,
        last_weight_grad,
        last_gain_grad,
        last_shift_grad,
    )


def solution(mesh):
    wide = P("img", "ch")
    matrix, vector = P(None, "ch"), P("ch")
    cube = P(None, None, None, "ch")
    weights = (matrix, vector, vector, cube, vector, vector, matrix, vector, matrix, vector, matrix, vector, vector)
    return jax.shard_map(
        functools.partial(body, mesh.shape["img"]),
        mesh=mesh,
        in_specs=(wide, P(), *weights, wide),
        out_specs=(wide, wide, *weights),
        check_vma=False,
    )
```

```python
import functools

import jax
import jax.numpy as jnp
from jax import lax
from jax.experimental import pallas as pl
from jax.experimental.pallas import tpu as pltpu
from jax.sharding import PartitionSpec as P


GROUP_WIDTH = 56
ROWS_IMG = 188
BIG_ROWS = 98
IMGS = 8
ROWS = IMGS * ROWS_IMG
HALF = 1008
TILES = 8
LAST = HALF - 7 * 128
EPSILON = 1e-05
F32 = jnp.float32
BF16 = jnp.bfloat16
MESH = pl.DeviceIdType.MESH
VMEM = pl.BlockSpec(memory_space=pltpu.VMEM)
ANY = pl.BlockSpec(memory_space=pl.ANY)
VMEM_LIMIT = 60 * 1024 * 1024
SPANS = ((0, 256), (256, 512), (512, 768), (768, 1008))
WINDOWS = ((0, 3), (1, 5), (3, 7), (5, 8))
BIG_PAD = 73 * 16
PAD_ROWS = BIG_PAD + 21 * 80
TAPS = tuple((dy, dx) for dy in (-1, 0, 1) for dx in (-1, 0, 1))
DMA = pltpu.SemaphoreType.DMA


def big_place(y, x):
    return (1 + (y + 1) * 8 + x) * 16


def small_place(y, x):
    return BIG_PAD + (1 + (y + 1) * 4 + x) * 80


def natural_row(tile):
    if tile < BIG_ROWS:
        return (tile % 2) * 49 + tile // 2
    tile = tile - BIG_ROWS
    return BIG_ROWS + (tile % 10) * 9 + tile // 10


def padded_row(tile):
    if tile < BIG_ROWS:
        pixel = tile // 2
        return big_place(pixel // 7, pixel % 7) + (tile % 2) * 8
    tile = tile - BIG_ROWS
    pixel = tile // 10
    return small_place(pixel // 3, pixel % 3) + (tile % 10) * 8


REAL_ROWS = frozenset(padded_row(tile) for tile in range(0, ROWS_IMG, 2))
ZERO_ROWS = tuple(row for row in range(0, PAD_ROWS, 16) if row not in REAL_ROWS)


def sigmoid(v):
    return 0.5 + 0.5 * jnp.tanh(0.5 * v)


def slope_of(v, s):
    return s * (1.0 + v * (1.0 - s))


def dot(a, b, dims=((1,), (0,)), **kw):
    return lax.dot_general(a, b, (dims, ((), ())), preferred_element_type=F32, **kw)


def for_each(count, step):
    if count <= 16:
        for index in range(count):
            step(index)
    else:
        lax.fori_loop(0, count, lambda index, _: (step(index), 0)[1], 0)


def for_tiles(step):
    lax.fori_loop(0, TILES, lambda j, _: (step(j), 0)[1], 0)


def for_ragged_tiles(step):
    def full(j, _):
        step(j, pl.ds(pl.multiple_of(j * 128, 128), 128), 128)
        return 0

    lax.fori_loop(0, TILES - 1, full, 0)
    step(TILES - 1, pl.ds(7 * 128, LAST), LAST)


def greet(n, all_images=True, partner=True):
    barrier = pltpu.get_barrier_semaphore()
    me = lax.axis_index("img")
    count = 0
    if all_images:
        for_each(
            n - 1,
            lambda d: pl.semaphore_signal(
                barrier, 1, device_id={"img": lax.rem(me + d + 1, n)}, device_id_type=MESH
            ),
        )
        count += n - 1
    if partner:
        pl.semaphore_signal(
            barrier, 1, device_id={"ch": 1 - lax.axis_index("ch")}, device_id_type=MESH
        )
        count += 1
    return lambda: pl.semaphore_wait(barrier, count)


class Gather:
    def __init__(self, n, source, target, send, recv):
        self.n, self.source, self.target, self.send, self.recv = n, source, target, send, recv
        self.me = lax.axis_index("img")

    def copy(self, d):
        return pltpu.make_async_remote_copy(
            src_ref=self.source,
            dst_ref=self.target.at[self.me],
            send_sem=self.send.at[d],
            recv_sem=self.recv.at[d],
            device_id={"img": lax.rem(self.me + d + 1, self.n)},
            device_id_type=MESH,
        )

    def start(self):
        for_each(self.n - 1, lambda d: self.copy(d).start())
        self.target[self.me] = self.source[...]

    def wait(self):
        for_each(self.n - 1, lambda d: self.copy(d).wait())


def swap(source, target, send, recv):
    return pltpu.make_async_remote_copy(
        src_ref=source,
        dst_ref=target,
        send_sem=send,
        recv_sem=recv,
        device_id={"ch": 1 - lax.axis_index("ch")},
        device_id_type=MESH,
    )


def put_span(ref, span, rows, value, add=False):
    left, right = value[:, :128], value[:, 128:]
    width = right.shape[1]
    if add:
        ref[2 * span, rows, :] += left
        ref[2 * span + 1, rows, 0:width] += right
    else:
        ref[2 * span, rows, :] = left
        ref[2 * span + 1, rows, 0:width] = right


def norm_constants(n, stats, live, gain_shift, consts):
    def total(step):
        return lax.fori_loop(0, n, lambda i, acc: acc + step(i), jnp.zeros((TILES, 128), F32))

    number = total(lambda i: live[i])
    average = total(lambda i: live[i] * stats[i, 0]) / number

    def centred(i):
        off = stats[i, 0] - average
        return stats[i, 1] + live[i] * off * off

    variance = total(centred) / number
    consts[0] = average
    consts[1] = lax.rsqrt(variance + EPSILON)
    consts[2] = gain_shift[0]
    consts[3] = gain_shift[1]
    consts[4] = number


def back_constants(n, sums, consts, grads):
    shift_grad = lax.fori_loop(
        0, n, lambda i, acc: acc + sums[i, 0], jnp.zeros((TILES, 128), F32)
    )
    gain_grad = lax.fori_loop(
        0, n, lambda i, acc: acc + sums[i, 1], jnp.zeros((TILES, 128), F32)
    )
    grads[0] = gain_grad
    grads[1] = shift_grad
    consts[5] = shift_grad / consts[4]
    consts[6] = gain_grad / consts[4]
    consts[7] = consts[1] * consts[2]


def row_of(consts, k, j):
    return consts[k, pl.ds(j, 1), :]


def natural_stats(ref, mask, count, local):
    def step(j):
        x = ref[j]
        m = mask[...]
        average = jnp.sum(x * m, axis=0, keepdims=True) / count
        off = x - average
        local[0, pl.ds(j, 1), :] = average
        local[1, pl.ds(j, 1), :] = jnp.sum(m * off * off, axis=0, keepdims=True)

    for_tiles(step)


def crop_sum(value, mask10):
    big = jnp.sum(value[:BIG_ROWS], axis=0)
    small = jnp.sum(value[BIG_ROWS:].reshape(9, 10, IMGS, 128), axis=0)
    return big + jnp.sum(small * mask10[...], axis=0)


def crop_stats(ref, mask10, count, local):
    def step(j):
        x = ref[j].reshape(ROWS_IMG, IMGS, 128)
        average = jnp.sum(crop_sum(x, mask10), axis=0, keepdims=True) / count
        off = x - average[None]
        local[0, pl.ds(j, 1), :] = average
        local[1, pl.ds(j, 1), :] = jnp.sum(crop_sum(off * off, mask10), axis=0, keepdims=True)

    for_tiles(step)


def window(ref, tiles, dy, dx, big):
    pieces = []
    for y in range(7 if big else 3):
        start = big_place(y + dy, dx) if big else small_place(y + dy, dx)
        rows = slice(start, start + (112 if big else 240))
        pieces.append(jnp.concatenate([ref[t, rows, :] for t in tiles], axis=1))
    return jnp.concatenate(pieces, axis=0)


def span_groups(span):
    return range(span * 256 // GROUP_WIDTH, min(18, (span * 256 + 255) // GROUP_WIDTH + 1))


def span_masks(span):
    lane = lax.broadcasted_iota(jnp.int32, (GROUP_WIDTH, 256), 1) + span * 256
    return [(lane >= g * GROUP_WIDTH) & (lane < (g + 1) * GROUP_WIDTH) for g in span_groups(span)]


def tap_rows(kernel, tap, span):
    first = tap * GROUP_WIDTH
    start = first // 16 * 16
    end = min(9 * GROUP_WIDTH, (first + GROUP_WIDTH + 15) // 16 * 16)
    a, b = SPANS[span]
    piece = kernel[start:end, a:b].astype(F32)[first - start : first - start + GROUP_WIDTH]
    if b - a < 256:
        piece = jnp.concatenate([piece, jnp.zeros((GROUP_WIDTH, 256 - (b - a)), F32)], axis=1)
    return piece


def build_band(kernel, span, band):
    first, end = WINDOWS[span]
    depth = (end - first) * 128
    groups = span_groups(span)
    masks = span_masks(span)
    head = groups[0] * GROUP_WIDTH - first * 128
    tail = depth - head - len(groups) * GROUP_WIDTH
    for tap in range(9):
        piece = tap_rows(kernel, tap, span)
        parts = [jnp.where(m, piece, 0.0) for m in masks]
        if head:
            parts.insert(0, jnp.zeros((head, 256), F32))
        if tail:
            parts.append(jnp.zeros((tail, 256), F32))
        band[0:depth, tap * 256 : tap * 256 + 256] = jnp.concatenate(parts, axis=0).astype(BF16)


def zero_pads(ref, j):
    for row in ZERO_ROWS:
        ref[j, row : row + 16, :] = jnp.zeros((16, 128), BF16)


def halves(value):
    high = value.astype(BF16)
    return high, (value - high.astype(F32)).astype(BF16)


def fine_dot(left, right_high, right_low, dims=((1,), (0,))):
    high, low = halves(left)
    both = jnp.concatenate([high.astype(F32), low.astype(F32)], axis=0).astype(BF16)
    value = dot(both, right_high, dims)
    return value[:IMGS] + value[IMGS:] + dot(both, right_low, dims)[:IMGS]


def load_vectors(gain, shift, norm):
    norm[...] = jnp.zeros_like(norm)
    for k, row in enumerate((gain, shift)):
        for j in range(TILES):
            width = 128 if j < 7 else LAST
            norm[k, j : j + 1, 0:width] = row[:, j * 128 : j * 128 + width]


def load_counts(n, crops, counts, live):
    me = lax.axis_index("img")
    for image in range(IMGS):
        counts[image : image + 1, :] = jnp.full((1, 128), crops[me * IMGS + image], jnp.int32)

    def device(d):
        total = crops[d * IMGS]
        for image in range(1, IMGS):
            total = total + crops[d * IMGS + image]
        rows = (IMGS * BIG_ROWS + 9 * total).astype(F32)
        live[d] = jnp.full((TILES, 128), rows, F32)

    for_each(n, device)


def live_slots(counts, mask10):
    for slot in range(10):
        mask10[slot] = (counts[...] > slot).astype(F32)


def natural_mask(mask10, mask):
    for tile in range(ROWS_IMG):
        there = pl.ds(natural_row(tile), IMGS, stride=ROWS_IMG)
        if tile < BIG_ROWS:
            mask[there, :] = jnp.ones((IMGS, 128), F32)
        else:
            mask[there, :] = mask10[(tile - BIG_ROWS) % 10]


def forward_kernel(n, *refs):
    r = Refs(refs)
    pixels_any, weight1_any, weight3_any, kernel_any, squeeze_any, excite_any, output_any = r.take(7)
    crops, vectors, squeeze_b, excite_b = r.take(), r.take(6), r.take(), r.take()
    first_out, pixels_out, far_out, padded_out, group_out, scaled_out, scaled_far_out = r.take(7)
    last_out, merged_out, block_out = r.take(3)
    far1, far3 = r.take(2)
    split_outs = r.take(4)
    stats1, stats2, stats3, sums3 = r.take(4)
    pooled, pooled_far, squeezed, squeezed_far, squeeze_pre, excited = r.take(6)
    factor_sums = r.take()
    counts, live, norms = r.take(), r.take(), r.take(3)
    consts, local, buf_a, buf_b, pixels, far, weight, zone = r.take(8)
    kernel_low, squeeze_w, excite_w = r.take(3)
    splits = r.take(4)
    turned, mask, mask10 = r.take(3)
    bands = r.take(4)
    load, store, swap_s, swap_r, tile_s, tile_r, small_s, small_r = r.take(8)
    gathers = [r.take(2) for _ in range(4)]
    factor_column, factors = r.take(2)
    factor = Part(n, ORDERS[0], r.take(2))
    ch = lax.axis_index("ch")
    wait_all = greet(n)
    loads = [
        fetch(source, target, load.at[k])
        for k, (source, target) in enumerate(
            (
                (pixels_any, pixels),
                (weight1_any, weight),
                (kernel_any, kernel_low),
                (squeeze_any, squeeze_w),
                (excite_any, excite_w),
            )
        )
    ]
    own = pl.multiple_of(ch * HALF, 16)
    away = pl.multiple_of((1 - ch) * HALF, 16)
    wait_all()
    chunks = ((0, 384), (384, 384), (768, 384), (1152, 352))
    swaps = []
    for k, (start, size) in enumerate(chunks):
        rows = pl.ds(start, size)
        swaps.append(swap(pixels_any.at[rows], far.at[rows], swap_s.at[k], swap_r.at[k]))
        swaps[-1].start()
    load_counts(n, crops, counts, live)
    for k in range(3):
        load_vectors(vectors[2 * k], vectors[2 * k + 1], norms[k])
    live_slots(counts, mask10)
    natural_mask(mask10, mask)
    count = live[lax.axis_index("img")][0:1, :]
    loads[0].wait()
    loads[1].wait()
    for t, (a, b) in enumerate(SPANS):
        put_span(buf_a, t, slice(0, ROWS), dot(pixels[...], weight[pl.ds(own, HALF), a:b]))
    buf_a[7, :, LAST:128] = jnp.zeros((ROWS, 128 - LAST), F32)
    for k, (start, size) in enumerate(chunks):
        swaps[k].wait()
        rows = slice(start, start + size)
        for t, (a, b) in enumerate(SPANS):
            put_span(buf_a, t, rows, dot(far[rows, :], weight[pl.ds(away, HALF), a:b]), add=True)
    natural_stats(buf_a, mask, count, local)
    gather = Gather(n, local, stats1, *gathers[0])
    gather.start()
    weight_swaps = [
        swap(w.at[pl.ds(away, HALF)], f, swap_s.at[4 + k], swap_r.at[4 + k])
        for k, (w, f) in enumerate(((weight1_any, far1), (weight3_any, far3)))
    ]
    for s in weight_swaps:
        s.start()
    load_weight = fetch(weight3_any, weight, load.at[0])
    mine_rows, far_rows = pl.ds(0, ROWS), pl.ds(ROWS, ROWS)
    for source, start in ((pixels, 0), (far, ROWS)):
        for j in range(TILES):
            width = 128 if j < 7 else LAST
            lanes = slice(j * 128, j * 128 + width)
            zone[j, start : start + ROWS, 0:width] = source[:, lanes]
    zone[7, :, LAST:128] = jnp.zeros((2 * ROWS, 128 - LAST), BF16)
    store_pixels = [
        fetch(zone.at[:, mine_rows], pixels_out, store.at[0]),
        fetch(zone.at[:, far_rows], far_out, store.at[12]),
    ]
    stores = []
    store_first = fetch(buf_a, first_out, store.at[1])
    loads[2].wait()
    for span in range(4):
        build_band(kernel_low, span, bands[span])
    loads[3].wait()
    loads[4].wait()
    for k, w in enumerate((squeeze_w, excite_w)):
        splits[2 * k][...], splits[2 * k + 1][...] = halves(w[...])
    stores += [fetch(splits[k], split_outs[k], store.at[2 + k]) for k in range(4)]
    load_output = fetch(output_any, far, load.at[1])
    for s in store_pixels:
        s.wait()
    gather.wait()
    norm_constants(n, stats1, live, norms[0], consts)

    def activate_first(j):
        average = row_of(consts, 0, j)
        scale = row_of(consts, 1, j) * row_of(consts, 2, j)
        shift = row_of(consts, 3, j)
        zero_pads(zone, j)
        for tile in range(0, ROWS_IMG, 2):
            both = []
            for half in range(2):
                x = buf_a[j, pl.ds(natural_row(tile + half), IMGS, stride=ROWS_IMG), :]
                pre = (x - average) * scale + shift
                both.append(pre * sigmoid(pre))
            row = padded_row(tile)
            zone[j, row : row + 16, :] = jnp.concatenate(both, axis=0).astype(BF16)

    for_tiles(activate_first)
    store_padded = fetch(zone.at[:, pl.ds(0, PAD_ROWS)], padded_out, store.at[6])
    for span, (start, end) in enumerate(WINDOWS):
        tiles = range(start, end)
        right = jnp.concatenate(
            [bands[span][:, tap * 256 : tap * 256 + 256] for tap in range(9)], axis=0
        )
        for big in (True, False):
            left = jnp.concatenate([window(zone, tiles, dy, dx, big) for dy, dx in TAPS], axis=1)
            rows = slice(0, 784) if big else slice(784, ROWS)
            put_span(buf_b, span, rows, dot(left, right))
    crop_stats(buf_b, mask10, count, local)
    gather = Gather(n, local, stats2, *gathers[1])
    gather.start()
    store_group = fetch(buf_b, group_out, store.at[7])
    store_first.wait()
    store_padded.wait()
    gather.wait()
    norm_constants(n, stats2, live, norms[1], consts)
    inverse = 1.0 / (BIG_ROWS + 9.0 * counts[...].astype(F32))

    def activate_group(j):
        average = row_of(consts, 0, j)
        scale = row_of(consts, 1, j) * row_of(consts, 2, j)
        pre = (buf_b[j] - average) * scale + row_of(consts, 3, j)
        value = pre * sigmoid(pre)
        buf_a[j] = value
        pooled[j] = crop_sum(value.reshape(ROWS_IMG, IMGS, 128), mask10) * inverse

    for_tiles(activate_group)
    pool_swap = swap(pooled, pooled_far, small_s.at[0], small_r.at[0])
    pool_swap.start()
    pool_swap.wait()
    mine = jnp.concatenate([pooled[j] for j in range(TILES)], axis=1)[:, :HALF]
    theirs = jnp.concatenate([pooled_far[j] for j in range(TILES)], axis=1)[:, :HALF]
    is_low = ch == 0
    high, low = splits[0], splits[1]
    pre = (
        fine_dot(jnp.where(is_low, mine, theirs), high[0:HALF, :], low[0:HALF, :])
        + fine_dot(jnp.where(is_low, theirs, mine), high[HALF:, :], low[HALF:, :])
        + squeeze_b[...]
    )
    squeeze_pre[...] = pre
    squeezed[...] = pre * sigmoid(pre)
    squeeze_swap = swap(squeezed, squeezed_far, small_s.at[1], small_r.at[1])
    squeeze_swap.start()
    squeeze_swap.wait()
    mine, theirs = squeezed[...], squeezed_far[...]
    width = mine.shape[1]
    high, low = splits[2], splits[3]
    gate = sigmoid(
        fine_dot(jnp.where(is_low, mine, theirs), high[0:width, :], low[0:width, :])
        + fine_dot(jnp.where(is_low, theirs, mine), high[width:, :], low[width:, :])
        + excite_b[...]
    )
    excited[7] = jnp.zeros((IMGS, 128), F32)
    for j in range(TILES - 1):
        excited[j] = gate[:, j * 128 : j * 128 + 128]
    excited[7, :, 0:LAST] = gate[:, 7 * 128 :]
    pack_factors((pooled, pooled_far), (squeezed, squeezed_far), factors)
    factor_column[factor.place[2]] = factors[...]
    factor.spread2(factor_column)

    def tile_swap(j):
        return swap(zone.at[j, mine_rows], zone.at[j, far_rows], tile_s.at[j], tile_r.at[j])

    def apply(j):
        gate_j = excited[j]
        for tile in range(ROWS_IMG):
            turned[pl.ds(natural_row(tile), IMGS, stride=ROWS_IMG), :] = (
                buf_a[j, tile * 8 : tile * 8 + 8, :] * gate_j
            )
        zone[j, 0:ROWS, :] = turned[...].astype(BF16)
        tile_swap(j).start()

    for_tiles(apply)
    stores.append(fetch(zone.at[:, mine_rows], scaled_out, store.at[8]))
    load_weight.wait()
    store_group.wait()
    for t, (a, b) in enumerate(SPANS):
        left = jnp.concatenate([zone[j, 0:ROWS, :] for j in range(TILES)], axis=1)[:, :HALF]
        put_span(buf_b, t, slice(0, ROWS), dot(left, weight[pl.ds(own, HALF), a:b]))
    buf_b[7, :, LAST:128] = jnp.zeros((ROWS, 128 - LAST), F32)
    factor.spread1(factor_column, factor_sums)
    for_tiles(lambda j: tile_swap(j).wait())
    stores.append(fetch(zone.at[:, far_rows], scaled_far_out, store.at[9]))
    for t, (a, b) in enumerate(SPANS):
        left = jnp.concatenate([zone[j, ROWS : 2 * ROWS, :] for j in range(TILES)], axis=1)[:, :HALF]
        put_span(buf_b, t, slice(0, ROWS), dot(left, weight[pl.ds(away, HALF), a:b]), add=True)
    natural_stats(buf_b, mask, count, local)
    gather = Gather(n, local, stats3, *gathers[2])
    gather.start()
    stores.append(fetch(buf_b, last_out, store.at[10]))
    factor.spread0(factor_sums)
    buf_a[7, :, LAST:128] = jnp.zeros((ROWS, 128 - LAST), F32)
    load_output.wait()
    gather.wait()
    norm_constants(n, stats3, live, norms[2], consts)
    local[...] = jnp.zeros_like(local)

    def merge(j, lanes, width):
        def vec(k):
            return consts[k, pl.ds(j, 1), 0:width]

        m = mask[:, 0:width]
        normed = (buf_b[j, :, 0:width] - vec(0)) * vec(1)
        merged = pixels[:, lanes].astype(F32) + normed * vec(2) + vec(3)
        s = sigmoid(merged)
        grad = far[:, lanes].astype(F32) * m * slope_of(merged, s)
        far[:, lanes] = (merged * s * m).astype(BF16)
        buf_a[j, :, 0:width] = grad
        local[0, pl.ds(j, 1), 0:width] = jnp.sum(grad, axis=0, keepdims=True)
        local[1, pl.ds(j, 1), 0:width] = jnp.sum(grad * normed, axis=0, keepdims=True)

    for_ragged_tiles(merge)
    gather = Gather(n, local, sums3, *gathers[3])
    gather.start()
    stores.append(fetch(buf_a, merged_out, store.at[11]))
    stores.append(fetch(far, block_out, store.at[13]))
    for s in weight_swaps + stores:
        s.wait()
    factor.settle()
    gather.wait()


def part_extents(n, order):
    sizes = image_axes(n)
    return tuple(sizes[a] for a in order)


def part_shape(n, order, rows):
    return part_extents(n, order) + (rows // n, 128)


def put_blocks(target, tile, tile_rows, start, value):
    _, e1, e2, rows, _ = target.shape
    size = value.shape[0]
    first = start
    while first < start + size:
        block = tile * (tile_rows // rows) + first // rows
        inside = first % rows
        take = min(rows - inside, start + size - first)
        place = (block // (e1 * e2), block // e2 % e1, block % e2)
        target[place[0], place[1], place[2], inside : inside + take, :] = value[
            first - start : first - start + take
        ]
        first += take


def weight_grad(left_span, right_tiles, target, spans):
    for a, b in SPANS:
        left = left_span(a, b)
        for k, span in enumerate(spans):
            right = jnp.concatenate([right_tiles(2 * span), right_tiles(2 * span + 1)], axis=1)
            value = dot(left, right, ((0,), (0,))).astype(BF16)
            put_blocks(target, 2 * k, 1024, a, value[:, :128])
            put_blocks(target, 2 * k + 1, 1024, a, value[:, 128:])


def tile_span(tile):
    def span(a, b):
        tiles = range(a // 128, (b + 127) // 128)
        return jnp.concatenate([tile(t) for t in tiles], axis=1)[:, : b - a]

    return span


def image_axes(n):
    return {16: (2, 2, 4), 128: (4, 4, 8)}.get(n, (n, 1, 1))


class Part:
    def __init__(self, n, order, sems):
        sizes = image_axes(n)
        strides = (1, sizes[0], sizes[0] * sizes[1])
        self.me = lax.axis_index("img")
        self.sizes = [sizes[a] for a in order]
        self.strides = [strides[a] for a in order]
        self.place = [lax.rem(self.me // s, e) for s, e in zip(self.strides, self.sizes)]
        self.sems = sems
        self.live = []

    def send(self, axis, stage, source, target):
        for d in range(1, self.sizes[axis]):
            q = lax.rem(self.place[axis] + d, self.sizes[axis])
            peer = self.me + (q - self.place[axis]) * self.strides[axis]
            copy = pltpu.make_async_remote_copy(
                src_ref=source(q),
                dst_ref=target(d),
                send_sem=self.sems[0].at[stage, d],
                recv_sem=self.sems[1].at[stage, d],
                device_id={"img": peer},
                device_id_type=MESH,
            )
            copy.start()
            self.live.append(copy)

    def keep(self, source, target, stage):
        copy = pltpu.make_async_copy(source, target, self.sems[0].at[stage, 0])
        copy.start()
        self.live.append(copy)

    def settle(self):
        for copy in self.live:
            copy.wait()
        self.live = []

    def add(self, target, own, arrived):
        total = own[...].astype(F32)
        for block in arrived:
            total = total + block[...].astype(F32)
        target[...] = total.astype(BF16)

    def send0(self, source, r0):
        self.send(0, 0, lambda q: source.at[q], lambda d: r0.at[d - 1])

    def sum0(self, source, r0, a0):
        self.settle()
        for k in range(self.sizes[1]):
            self.add(
                a0.at[k],
                source.at[self.place[0], k],
                [r0.at[d, k] for d in range(self.sizes[0] - 1)],
            )

    def send1(self, a0, r1):
        self.send(1, 1, lambda q: a0.at[q], lambda d: r1.at[d - 1])

    def sum1(self, a0, r1, a1):
        self.settle()
        self.add(a1, a0.at[self.place[1]], [r1.at[d] for d in range(self.sizes[1] - 1)])

    def send2(self, a1, r2):
        self.send(2, 2, lambda q: a1.at[q], lambda d: r2.at[d - 1])

    def sum2(self, a1, r2, column):
        self.settle()
        p2 = self.place[2]
        self.add(column.at[p2], a1.at[p2], [r2.at[d] for d in range(self.sizes[2] - 1)])

    def spread2(self, column):
        block = column.at[self.place[2]]
        self.send(2, 3, lambda q: block, lambda d: block)

    def spread1(self, column, result):
        self.settle()
        block = result.at[self.place[0], self.place[1]]
        self.send(1, 4, lambda q: column, lambda d: block)
        self.keep(column, block, 4)

    def spread0(self, result):
        self.settle()
        block = result.at[self.place[0]]
        self.send(0, 5, lambda q: block, lambda d: block)

    @staticmethod
    def room(n, order, shape):
        e0, e1, e2, rows, lanes = shape
        return (
            (max(e0 - 1, 1), e1, e2, rows, lanes),
            (e1, e2, rows, lanes),
            (max(e1 - 1, 1), e2, rows, lanes),
            (e2, rows, lanes),
            (max(e2 - 1, 1), rows, lanes),
            (e2, rows, lanes),
        )


def part_sems(n, count):
    most = max(image_axes(n))
    return [DMA((6, most)) for _ in range(2 * count)]


def fetch(source, target, sem):
    copy = pltpu.make_async_copy(source, target, sem)
    copy.start()
    return copy


class Refs:
    def __init__(self, refs):
        self.refs = list(refs)

    def take(self, count=None):
        if count is None:
            return self.refs.pop(0)
        head, self.refs = self.refs[:count], self.refs[count:]
        return head


ORDERS = ((0, 1, 2), (1, 0, 2), (0, 1, 2), (1, 0, 2))
KERNEL_ORDERS = ORDERS[:2]
AHEAD_TILES = 20
BACK_TILES = 10


def last_grad_kernel(n, *refs):
    r = Refs(refs)
    last_any, merged_any, group_any, scaled_any, scaled_far_any, weight_any, weight_far_any = r.take(7)
    stats3, live, sums3 = r.take(3)
    stats2, counts, norm2, norm3, excited, squeeze_pre = r.take(6)
    split_anys = r.take(4)
    pre_grad, sums2, excite_grad, squeeze_grad, vectors = r.take(5)
    done1, arrive2, mid3 = r.take(2), r.take(2), r.take(2)
    consts, consts2, local, buf_a, buf_b, low, low_far, scaled, scaled_far = r.take(9)
    weight, weight_far, mask, mask10 = r.take(4)
    splits = r.take(4)
    terms, terms_in, pool_terms, pool_in, pool_tiles = r.take(5)
    grads, rooms, mid1, arrive1 = r.take(4), r.take(4), r.take(2), r.take(2)
    load, swap_s, swap_r, small_s, small_r, send, recv = r.take(7)
    sems = r.take(8)
    ch = lax.axis_index("ch")
    own = pl.multiple_of(ch * HALF, 16)
    wait_all = greet(n)
    loads = [
        fetch(source, target, load.at[k])
        for k, (source, target) in enumerate(
            (
                (last_any, buf_a),
                (merged_any, buf_b),
                (scaled_any, scaled),
                (scaled_far_any, scaled_far),
                (weight_any.at[pl.ds(own, HALF)], weight),
                (weight_far_any, weight_far),
                *zip(split_anys, splits),
            )
        )
    ]
    live_slots(counts, mask10)
    natural_mask(mask10, mask)
    inverse = 1.0 / (BIG_ROWS + 9.0 * counts[...].astype(F32))
    norm_constants(n, stats3, live, norm3, consts)
    back_constants(n, sums3, consts, vectors)
    norm_constants(n, stats2, live, norm2, consts2)
    parts = [Part(n, order, sems[2 * k : 2 * k + 2]) for k, order in enumerate(ORDERS)]
    wait_all()
    loads[0].wait()
    loads[1].wait()

    def step(j):
        normed = (buf_a[j] - row_of(consts, 0, j)) * row_of(consts, 1, j)
        inner = buf_b[j] - row_of(consts, 5, j) - normed * row_of(consts, 6, j)
        low[j] = (mask[...] * row_of(consts, 7, j) * inner).astype(BF16)
        swap(low.at[j], low_far.at[j], swap_s.at[j], swap_r.at[j]).start()

    for_tiles(step)
    load_group = fetch(group_any, buf_a, load.at[0])
    for part in range(4):
        if part < 2:
            loads[2 + part].wait()
        rows = (scaled, scaled_far)[part % 2]
        left = tile_span(lambda t: rows[t])
        weight_grad(left, lambda t: low[t], grads[part], (0, 1) if part < 2 else (2, 3))
        if part < 2:
            parts[part].send0(grads[part], rooms[part])
    loads[4].wait()
    for t, (a, b) in enumerate(SPANS):
        left = jnp.concatenate([low[j] for j in range(TILES)], axis=1)[:, :HALF]
        put_span(buf_b, t, slice(0, ROWS), dot(left, weight[a:b, :], ((1,), (1,))))
    buf_b[7, :, LAST:128] = jnp.zeros((ROWS, 128 - LAST), F32)
    for_tiles(lambda j: swap(low.at[j], low_far.at[j], swap_s.at[j], swap_r.at[j]).wait())
    loads[5].wait()
    for t, (a, b) in enumerate(SPANS):
        left = jnp.concatenate([low_far[j] for j in range(TILES)], axis=1)[:, :HALF]
        put_span(
            buf_b, t, slice(0, ROWS), dot(left, weight_far[a:b, :], ((1,), (1,))), add=True
        )
    load_group.wait()

    def gate_sum(j):
        average = row_of(consts2, 0, j)
        scale = row_of(consts2, 1, j) * row_of(consts2, 2, j)
        shift = row_of(consts2, 3, j)
        total = jnp.zeros((IMGS, 128), F32)
        for tile in range(ROWS_IMG):
            pre = (buf_a[j, tile * 8 : tile * 8 + 8, :] - average) * scale + shift
            act = pre * sigmoid(pre)
            total = total + act * buf_b[j, pl.ds(natural_row(tile), IMGS, stride=ROWS_IMG), :]
        gate = excited[j]
        excite_grad[j] = total * gate * (1.0 - gate)

    for_tiles(gate_sum)
    for k in range(2):
        parts[k].sum0(grads[k], rooms[k], mid1[k])
        parts[k].send1(mid1[k], arrive1[k])
    wide = jnp.concatenate([excite_grad[j] for j in range(TILES)], axis=1)[:, :HALF]
    width = squeeze_pre.shape[1]
    is_low = ch == 0
    for k in range(6, 10):
        loads[k].wait()
    across = ((1,), (1,))
    high, low_part = splits[2], splits[3]
    part0 = fine_dot(wide, high[0:width, :], low_part[0:width, :], across)
    part1 = fine_dot(wide, high[width:, :], low_part[width:, :], across)
    terms[...] = jnp.where(is_low, part1, part0)
    term_swap = swap(terms, terms_in, small_s.at[0], small_r.at[0])
    term_swap.start()
    term_swap.wait()
    pre = squeeze_pre[...]
    grad = (jnp.where(is_low, part0, part1) + terms_in[...]) * slope_of(pre, sigmoid(pre))
    squeeze_grad[...] = grad
    high, low_part = splits[0], splits[1]
    pool0 = fine_dot(grad, high[0:HALF, :], low_part[0:HALF, :], across)
    pool1 = fine_dot(grad, high[HALF:, :], low_part[HALF:, :], across)
    pool_terms[...] = jnp.where(is_low, pool1, pool0)
    pool_swap = swap(pool_terms, pool_in, small_s.at[1], small_r.at[1])
    pool_swap.start()
    pool_swap.wait()
    for k in range(2):
        parts[k].sum1(mid1[k], arrive1[k], done1[k])
        parts[k].send2(done1[k], arrive2[k])
        parts[k + 2].send0(grads[k + 2], rooms[k + 2])
    pool = jnp.where(is_low, pool0, pool1) + pool_in[...]
    pool_tiles[7, :, LAST:128] = jnp.zeros((IMGS, 128 - LAST), F32)
    for j in range(TILES):
        part = pool[:, j * 128 : min(HALF, j * 128 + 128)]
        pool_tiles[j, :, 0 : part.shape[1]] = part * inverse[:, 0 : part.shape[1]]

    def slopes(j):
        average, scale = row_of(consts2, 0, j), row_of(consts2, 1, j)
        gain, shift = row_of(consts2, 2, j), row_of(consts2, 3, j)
        gate, pooled = excited[j], pool_tiles[j]
        total = jnp.zeros((IMGS, 128), F32)
        total_normed = jnp.zeros((IMGS, 128), F32)
        for tile in range(ROWS_IMG):
            rows = slice(tile * 8, tile * 8 + 8)
            normed = (buf_a[j, rows, :] - average) * scale
            pre = normed * gain + shift
            lead = pooled if tile < BIG_ROWS else pooled * mask10[(tile - BIG_ROWS) % 10]
            act = buf_b[j, pl.ds(natural_row(tile), IMGS, stride=ROWS_IMG), :] * gate + lead
            grad = act * slope_of(pre, sigmoid(pre))
            buf_a[j, rows, :] = grad
            total = total + grad
            total_normed = total_normed + grad * normed
        local[0, pl.ds(j, 1), :] = jnp.sum(total, axis=0, keepdims=True)
        local[1, pl.ds(j, 1), :] = jnp.sum(total_normed, axis=0, keepdims=True)

    for_tiles(slopes)
    gather = Gather(n, local, sums2, send, recv)
    gather.start()
    store = fetch(buf_a, pre_grad, load.at[0])
    gather.wait()
    for k in range(2):
        parts[k].settle()
        parts[k + 2].sum0(grads[k + 2], rooms[k + 2], mid3[k])
    store.wait()


def pack_factors(wides, narrows, factors):
    tiles = [part[j] for part in wides for j in range(TILES)]
    for part in narrows:
        rest = part[:, 128:]
        blank = jnp.zeros((IMGS, 128 - rest.shape[1]), F32)
        tiles += [part[:, 0:128], jnp.concatenate([rest, blank], axis=1)]
    for k in range(0, len(tiles), 2):
        both = jnp.concatenate(tiles[k : k + 2], axis=0)
        factors[k * IMGS : (k + 2) * IMGS, :] = both.astype(BF16)


def tail_kernel(n, *refs):
    r = Refs(refs)
    pre_any, group_any, padded_any, first_any = r.take(4)
    pixels_any, pixels_far_any, weight_any, weight_far_any, merged_any = r.take(5)
    stats2, live, sums2, counts, norm1, norm2, kernel, stats1 = r.take(8)
    done1, arrive2, mid3 = r.take(2), r.take(2), r.take(2)
    factor_parts = r.take(2)
    pixels_grad, group_vectors, first_vectors = r.take(3)
    last_sums, first_sums, kernel_sums = r.take(4), r.take(4), r.take(2)
    factor_sums = r.take()
    consts, consts1, mask10, local, sums1 = r.take(5)
    buf_a, buf_b, zone1, zone2, weight, weight_far, turned = r.take(7)
    bands = r.take(2)
    arrive3, done3, arrive4, last_columns = r.take(2), r.take(2), r.take(2), r.take(4)
    grads = r.take(4)
    first_rooms = [r.take(6) for _ in range(4)]
    kernel_grads = r.take(2)
    kernel_rooms = [r.take(6) for _ in range(2)]
    factor_column, factors = r.take(2)
    load, swap_s, swap_r, send, recv, free = r.take(6)
    sems = [r.take(2) for _ in range(11)]
    own = pl.multiple_of(lax.axis_index("ch") * HALF, 16)
    mine_rows, far_rows = pl.ds(0, ROWS), pl.ds(ROWS, ROWS)
    wait_all = greet(n)
    loads = [
        fetch(source, target, load.at[k])
        for k, (source, target) in enumerate(
            (
                (pre_any, buf_a),
                (group_any, buf_b),
                (padded_any, zone1.at[:, pl.ds(0, PAD_ROWS)]),
                (weight_any.at[pl.ds(own, HALF)], weight),
                (weight_far_any, weight_far),
            )
        )
    ]
    firsts = [Part(n, order, sems[k]) for k, order in enumerate(ORDERS)]
    lasts = [Part(n, order, sems[4 + k]) for k, order in enumerate(ORDERS)]
    kernels = [Part(n, KERNEL_ORDERS[k], sems[8 + k]) for k in range(2)]
    factor = Part(n, ORDERS[0], sems[10])
    live_slots(counts, mask10)
    norm_constants(n, stats2, live, norm2, consts)
    back_constants(n, sums2, consts, group_vectors)
    norm_constants(n, stats1, live, norm1, consts1)
    wait_all()

    def each(step, ks):
        for k in ks:
            step(k)

    def last1(k):
        lasts[k].sum1(mid3[k - 2], arrive3[k - 2], done3[k - 2])
        lasts[k].send2(done3[k - 2], arrive4[k - 2])

    def last2(k):
        lasts[k].sum2((*done1, *done3)[k], (*arrive2, *arrive4)[k], last_columns[k])
        lasts[k].spread2(last_columns[k])

    def last3(k):
        lasts[k].spread1(last_columns[k], last_sums[k])

    def last4(k):
        lasts[k].spread0(last_sums[k])

    def reducer(part, source, room, result):
        r0, a0, r1, a1, r2, column = room

        def stage0():
            part.send0(source, r0)

        def stage1():
            part.sum0(source, r0, a0)
            part.send1(a0, r1)

        def stage2():
            part.sum1(a0, r1, a1)
            part.send2(a1, r2)

        def stage3():
            part.sum2(a1, r2, column)
            part.spread2(column)

        return (
            stage0,
            stage1,
            stage2,
            stage3,
            lambda: part.spread1(column, result),
            lambda: part.spread0(result),
        )

    first = [reducer(firsts[k], grads[k], first_rooms[k], first_sums[k]) for k in range(4)]
    kernel_sum = [
        reducer(kernels[k], kernel_grads[k], kernel_rooms[k], kernel_sums[k]) for k in range(2)
    ]
    head, back, two = (0, 1), (2, 3), range(2)
    each(last2, head)
    for k in two:
        lasts[k + 2].send1(mid3[k], arrive3[k])
    for span in range(2):
        build_band(kernel, span, bands[span])
    loads[0].wait()
    loads[1].wait()

    def group_step(j):
        average, scale = row_of(consts, 0, j), row_of(consts, 1, j)
        less, slope, front = row_of(consts, 5, j), row_of(consts, 6, j), row_of(consts, 7, j)
        zero_pads(zone2, j)
        for tile in range(0, ROWS_IMG, 2):
            both = []
            for half in range(2):
                rows = slice(tile * 8 + half * 8, tile * 8 + half * 8 + 8)
                normed = (buf_b[j, rows, :] - average) * scale
                grad = front * (buf_a[j, rows, :] - less - normed * slope)
                if tile >= BIG_ROWS:
                    grad = grad * mask10[(tile + half - BIG_ROWS) % 10]
                both.append(grad)
            row = padded_row(tile)
            zone2[j, row : row + 16, :] = jnp.concatenate(both, axis=0).astype(BF16)

    for_tiles(group_step)
    load_first = fetch(first_any, buf_b, load.at[0])
    each(last1, back)
    pack_factors(factor_parts[:1], factor_parts[1:], factors)
    factor_column[factor.place[2]] = factors[...]
    factor.spread2(factor_column)
    loads[2].wait()
    started = 0
    for span, (start, end) in enumerate(WINDOWS):
        tiles = (2 * span, 2 * span + 1)
        depth = (end - start) * 128
        band = bands[span % 2]
        if span >= 2:
            build_band(kernel, span, band)
        shifted = [
            [window(zone2, tiles, -dy, -dx, big) for dy, dx in TAPS] for big in (True, False)
        ]
        for rows, left in ((slice(0, 784), shifted[0]), (slice(784, ROWS), shifted[1])):
            value = dot(jnp.concatenate(left, axis=1), band[0:depth, :], ((1,), (1,)))
            for t in range(start, end):
                part = value[:, (t - start) * 128 : (t - start) * 128 + 128]
                if t < started:
                    buf_a[t, rows, :] += part
                else:
                    buf_a[t, rows, :] = part
        started = end
        masks = span_masks(span)
        left = jnp.concatenate(
            [window(zone1, range(start, end), 0, 0, big) for big in (True, False)], axis=0
        )
        pieces = []
        for tap in range(9):
            right = jnp.concatenate([shifted[0][tap], shifted[1][tap]], axis=0)
            value = dot(left, right, ((0,), (0,)))
            piece = jnp.zeros((GROUP_WIDTH, 256), F32)
            for g, inside in zip(span_groups(span), masks):
                row = g * GROUP_WIDTH - start * 128
                piece = jnp.where(inside, value[row : row + GROUP_WIDTH], piece)
            pieces.append(piece)
        pieces.append(jnp.zeros((8, 256), F32))
        value = jnp.concatenate(pieces, axis=0).astype(BF16)
        for half in range(2):
            rows = slice(half * 256, half * 256 + 256)
            put_blocks(kernel_grads[half], 2 * span, 256, 0, value[rows, :128])
            put_blocks(kernel_grads[half], 2 * span + 1, 256, 0, value[rows, 128:])
        if span == 0:
            each(last3, head)
        elif span == 1:
            each(last4, head)
            factor.spread1(factor_column, factor_sums)
        elif span == 2:
            each(last2, back)
        else:
            for k in two:
                kernel_sum[k][0]()
            factor.spread0(factor_sums)
    pl.semaphore_signal(
        free, 1, device_id={"ch": 1 - lax.axis_index("ch")}, device_id_type=MESH
    )
    load_pixels = [
        fetch(pixels_any, zone2.at[:, mine_rows], load.at[1]),
        fetch(pixels_far_any, zone2.at[:, far_rows], load.at[2]),
    ]
    load_first.wait()

    def first_slopes(j):
        average, scale = row_of(consts1, 0, j), row_of(consts1, 1, j)
        gain, shift = row_of(consts1, 2, j), row_of(consts1, 3, j)
        total = jnp.zeros((IMGS, 128), F32)
        total_normed = jnp.zeros((IMGS, 128), F32)
        for tile in range(ROWS_IMG):
            rows = slice(tile * 8, tile * 8 + 8)
            x = buf_b[j, pl.ds(natural_row(tile), IMGS, stride=ROWS_IMG), :]
            normed = (x - average) * scale
            pre = normed * gain + shift
            grad = buf_a[j, rows, :] * slope_of(pre, sigmoid(pre))
            if tile >= BIG_ROWS:
                grad = grad * mask10[(tile - BIG_ROWS) % 10]
            buf_a[j, rows, :] = grad
            total = total + grad
            total_normed = total_normed + grad * normed
        local[0, pl.ds(j, 1), :] = jnp.sum(total, axis=0, keepdims=True)
        local[1, pl.ds(j, 1), :] = jnp.sum(total_normed, axis=0, keepdims=True)

    for_tiles(first_slopes)
    gather = Gather(n, local, sums1, send, recv)
    gather.start()
    each(last3, back)
    gather.wait()
    back_constants(n, sums1, consts1, first_vectors)

    def tile_swap(j):
        return swap(zone1.at[j, mine_rows], zone1.at[j, far_rows], swap_s.at[j], swap_r.at[j])

    def first_step(j):
        average, scale = row_of(consts1, 0, j), row_of(consts1, 1, j)
        less, slope, front = row_of(consts1, 5, j), row_of(consts1, 6, j), row_of(consts1, 7, j)
        for tile in range(ROWS_IMG):
            there = pl.ds(natural_row(tile), IMGS, stride=ROWS_IMG)
            normed = (buf_b[j, there, :] - average) * scale
            grad = front * (buf_a[j, tile * 8 : tile * 8 + 8, :] - less - normed * slope)
            if tile >= BIG_ROWS:
                grad = grad * mask10[(tile - BIG_ROWS) % 10]
            turned[there, :] = grad
        zone1[j, 0:ROWS, :] = turned[...].astype(BF16)
        tile_swap(j).start()

    pl.semaphore_wait(free, 1)
    for_tiles(first_step)
    load_merged = fetch(merged_any, buf_a, load.at[0])
    for s in load_pixels:
        s.wait()
    for part in range(4):
        side = slice(0, ROWS) if part % 2 == 0 else slice(ROWS, 2 * ROWS)
        weight_grad(
            tile_span(lambda t: zone2[t, side, :]),
            lambda t: zone1[t, 0:ROWS, :],
            grads[part],
            (0, 1) if part < 2 else (2, 3),
        )
        if part < 2:
            first[part][0]()
    for k in two:
        kernel_sum[k][1]()
    load_merged.wait()
    loads[3].wait()
    for t, (a, b) in enumerate(SPANS):
        left = jnp.concatenate([zone1[j, 0:ROWS, :] for j in range(TILES)], axis=1)[:, :HALF]
        put_span(buf_a, t, slice(0, ROWS), dot(left, weight[a:b, :], ((1,), (1,))), add=True)
    for_tiles(lambda j: tile_swap(j).wait())
    loads[4].wait()
    for t, (a, b) in enumerate(SPANS):
        left = jnp.concatenate([zone1[j, ROWS : 2 * ROWS, :] for j in range(TILES)], axis=1)
        put_span(
            buf_a, t, slice(0, ROWS), dot(left[:, :HALF], weight_far[a:b, :], ((1,), (1,))), add=True
        )
    store = fetch(buf_a, pixels_grad, load.at[0])

    def stage(sums, ks, number):
        for k in ks:
            sums[k][number]()

    stage(first, head, 1)
    stage(first, back, 0)
    stage(kernel_sum, two, 2)
    stage(first, head, 2)
    each(last4, back)
    stage(first, back, 1)
    stage(kernel_sum, two, 3)
    stage(first, head, 3)
    stage(first, back, 2)
    stage(kernel_sum, two, 4)
    stage(first, head, 4)
    stage(kernel_sum, two, 5)
    stage(first, head, 5)
    stage(first, back, 3)
    stage(first, back, 4)
    stage(first, back, 5)
    for part in (*firsts, *lasts, *kernels, factor):
        part.settle()
    store.wait()


def finish_kernel(*refs):
    r = Refs(refs)
    lasts, firsts, pixels_wide, kernels = r.take(4), r.take(4), r.take(), r.take(2)
    ahead, back, vectors = r.take(), r.take(), r.take(3)
    last_out, first_out, pixels_out, group_out, excite_w, excite_b = r.take(6)
    squeeze_w, squeeze_b, rows_out = r.take(), r.take(), r.take(6)
    behind, left0, left1 = r.take(3)
    ch = lax.axis_index("ch")
    j = pl.program_id(0)
    n = ahead.shape[0]
    se = squeeze_w.shape[1]

    @pl.when(j == 0)
    def _():
        behind[...] = back[...].astype(F32)
        before = ahead[...].astype(F32).reshape(n, AHEAD_TILES, IMGS, 128)

        def columns(start, tiles, width):
            parts = [before[:, t].reshape(n * IMGS, 128) for t in range(start, start + tiles)]
            return jnp.concatenate(parts, axis=1)[:, :width]

        tiles = [behind[:, t * IMGS : (t + 1) * IMGS, :].reshape(n * IMGS, 128) for t in (8, 9)]
        squeeze_all = jnp.concatenate(tiles, axis=1)[:, :se]
        squeeze_b[...] = jnp.sum(squeeze_all, axis=0, keepdims=True)
        squeeze_all = squeeze_all.astype(BF16)
        for start, place in ((0, ch), (8, 1 - ch)):
            rows = pl.ds(pl.multiple_of(place * HALF, 8), HALF)
            left = columns(start, 8, HALF).astype(BF16)
            squeeze_w[rows, :] = dot(left, squeeze_all, ((0,), (0,)))
        own, far = columns(16, 2, se), columns(18, 2, se)
        left0[...] = jnp.where(ch == 0, own, far).astype(BF16)
        left1[...] = jnp.where(ch == 0, far, own).astype(BF16)

    for sums, out in ((lasts, last_out), (firsts, first_out)):
        for late in range(2):

            @pl.when((j >= 4) == bool(late))
            def _():
                for k, place in ((0, ch), (1, 1 - ch)):
                    rows = pl.ds(pl.multiple_of(place * HALF, 8), HALF)
                    out[rows, :] = sums[2 * late + k][0, 0:HALF, :].astype(F32)

    pixels_out[...] = pixels_wide[0]
    split = kernels[0].shape[1]
    group_out[0:split, :] = kernels[0][0].astype(F32)
    group_out[split:, :] = kernels[1][0].astype(F32)[: 9 * GROUP_WIDTH - split]
    rows = pl.ds(pl.multiple_of(j * IMGS, IMGS), IMGS)
    excite = behind[:, rows, :].reshape(n * IMGS, 128)
    excite_b[...] = jnp.sum(excite, axis=0, keepdims=True)
    for k, left in enumerate((left0, left1)):
        excite_w[k * se : (k + 1) * se, :] = dot(left[...], excite.astype(BF16), ((0,), (0,)))
    for k in range(6):
        rows_out[k][...] = vectors[k // 2][k % 2, pl.ds(j, 1), :]


def call(kernel, ins, outs, scratch, ident=None, in_specs=None, out_specs=None, grid=()):
    params = {"vmem_limit_bytes": VMEM_LIMIT}
    if ident is not None:
        params.update(collective_id=ident, has_side_effects=True)
    return pl.pallas_call(
        kernel,
        grid=grid,
        out_shape=[jax.ShapeDtypeStruct(shape, dtype) for shape, dtype in outs],
        in_specs=in_specs or [VMEM] * len(ins),
        out_specs=out_specs or [VMEM] * len(outs),
        scratch_shapes=scratch,
        compiler_params=pltpu.CompilerParams(**params),
    )(*ins)


def body(
    n,
    pixels,
    crop_counts,
    first_weight,
    first_gain,
    first_shift,
    group_weight,
    group_gain,
    group_shift,
    squeeze_weight,
    squeeze_bias,
    excite_weight,
    excite_bias,
    last_weight,
    last_gain,
    last_shift,
    output_grad,
):
    assert pixels.shape == (ROWS, HALF)
    se = squeeze_weight.shape[1]
    wide = (TILES, ROWS, 128)
    stat = (n, 2, TILES, 128)
    sem = DMA((n - 1,))

    kernel = group_weight.reshape(9 * GROUP_WIDTH, HALF)
    local = pltpu.VMEM((2, TILES, 128), F32)
    consts = pltpu.VMEM((8, TILES, 128), F32)
    vectors = ((2, TILES, 128), F32)
    bands = [pltpu.VMEM(((e - s) * 128, 9 * 256), BF16) for s, e in WINDOWS]
    mask10 = pltpu.VMEM((10, IMGS, 128), F32)
    mask = pltpu.VMEM((ROWS, 128), F32)
    small = (TILES, IMGS, 128)
    wide_buf = pltpu.VMEM(wide, F32)
    tall = (ROWS, HALF)
    ahead_shape = part_extents(n, ORDERS[0]) + (AHEAD_TILES * IMGS, 128)
    back_shape = part_extents(n, ORDERS[0]) + (BACK_TILES * IMGS, 128)
    split_shapes = [(2 * HALF, se)] * 2 + [(2 * se, HALF)] * 2
    (
        first,
        pixels_tiles,
        pixels_far,
        padded,
        group,
        scaled,
        scaled_far,
        last,
        merged_grad,
        block_out,
        first_far,
        last_far,
        *rest,
    ) = call(
        functools.partial(forward_kernel, n),
        (
            pixels,
            first_weight,
            last_weight,
            kernel,
            squeeze_weight,
            excite_weight,
            output_grad,
            crop_counts,
            first_gain[None],
            first_shift[None],
            group_gain[None],
            group_shift[None],
            last_gain[None],
            last_shift[None],
            squeeze_bias[None],
            excite_bias[None],
        ),
        [
            (wide, F32),
            (wide, BF16),
            (wide, BF16),
            ((TILES, PAD_ROWS, 128), BF16),
            (wide, F32),
            (wide, BF16),
            (wide, BF16),
            (wide, F32),
            (wide, F32),
            (tall, BF16),
            ((HALF, HALF), BF16),
            ((HALF, HALF), BF16),
        ]
        + [(shape, BF16) for shape in split_shapes]
        + [(stat, F32)] * 4
        + [(small, F32)] * 2
        + [((IMGS, se), F32)] * 3
        + [(small, F32), (ahead_shape, BF16), ((IMGS, 128), jnp.int32), ((n, TILES, 128), F32)]
        + [vectors] * 3,
        [
            consts,
            local,
            wide_buf,
            wide_buf,
            pltpu.VMEM(tall, BF16),
            pltpu.VMEM(tall, BF16),
            pltpu.VMEM((2 * HALF, HALF), BF16),
            pltpu.VMEM((TILES, 2 * ROWS, 128), BF16),
            pltpu.VMEM((9 * GROUP_WIDTH, HALF), BF16),
            pltpu.VMEM((2 * HALF, se), F32),
            pltpu.VMEM((2 * se, HALF), F32),
            *(pltpu.VMEM(shape, BF16) for shape in split_shapes),
            mask,
            mask,
            mask10,
            *bands,
            DMA((6,)),
            DMA((14,)),
            DMA((6,)),
            DMA((6,)),
            DMA((TILES,)),
            DMA((TILES,)),
            DMA((2,)),
            DMA((2,)),
            *[sem] * 8,
            pltpu.VMEM(ahead_shape[2:], BF16),
            pltpu.VMEM(ahead_shape[3:], BF16),
            *part_sems(n, 1),
        ],
        0,
        in_specs=[ANY] * 7 + [pl.BlockSpec(memory_space=pltpu.SMEM)] + [VMEM] * 8,
        out_specs=[ANY] * 16 + [VMEM] * 10 + [ANY] + [VMEM] * 5,
    )
    splits, rest = rest[:4], rest[4:]
    stats1, stats2, stats3, sums3, pooled, pooled_far = rest[:6]
    squeezed, squeezed_far, squeeze_pre, excited, ahead_sums = rest[6:11]
    counts, live, norm1, norm2, norm3 = rest[11:]

    def vmem(shape, dtype=BF16):
        return pltpu.VMEM(shape, dtype)

    shapes = [part_shape(n, order, 4 * 1024) for order in ORDERS]
    rooms = [Part.room(n, order, shape) for order, shape in zip(ORDERS, shapes)]
    low_buf = vmem(wide)
    weight_buf = vmem((HALF, HALF))
    pre_grad, sums2, excite_grad, squeeze_grad, vectors3, *carry = call(
        functools.partial(last_grad_kernel, n),
        (
            last,
            merged_grad,
            group,
            scaled,
            scaled_far,
            last_weight,
            last_far,
            stats3,
            live,
            sums3,
            stats2,
            counts,
            norm2,
            norm3,
            excited,
            squeeze_pre,
            *splits,
        ),
        [(wide, F32), (stat, F32), (small, F32), ((IMGS, se), F32), vectors]
        + [(rooms[k][3], BF16) for k in range(2)]
        + [(rooms[k][4], BF16) for k in range(2)]
        + [(rooms[k][1], BF16) for k in (2, 3)],
        [
            consts,
            consts,
            local,
            wide_buf,
            wide_buf,
            low_buf,
            low_buf,
            low_buf,
            low_buf,
            weight_buf,
            weight_buf,
            mask,
            mask10,
            *(vmem(shape) for shape in split_shapes),
            vmem((IMGS, se), F32),
            vmem((IMGS, se), F32),
            vmem((IMGS, HALF), F32),
            vmem((IMGS, HALF), F32),
            vmem(small, F32),
            *(vmem(shape) for shape in shapes),
            *(vmem(room[0]) for room in rooms),
            *(vmem(room[1]) for room in rooms[:2]),
            *(vmem(room[2]) for room in rooms[:2]),
            DMA((10,)),
            DMA((TILES,)),
            DMA((TILES,)),
            DMA((2,)),
            DMA((2,)),
            sem,
            sem,
            *part_sems(n, 4),
        ],
        4,
        in_specs=[ANY] * 7 + [VMEM] * 9 + [ANY] * 4,
        out_specs=[ANY] + [VMEM] * 10,
    )
    done1, arrive2, mid3 = carry[0:2], carry[2:4], carry[4:6]
    kernel_shapes = [part_shape(n, order, TILES * 256) for order in KERNEL_ORDERS]
    kernel_rooms = [
        Part.room(n, order, shape) for order, shape in zip(KERNEL_ORDERS, kernel_shapes)
    ]
    kernel_shapes = [part_shape(n, order, TILES * 256) for order in KERNEL_ORDERS]
    kernel_rooms = [
        Part.room(n, order, shape) for order, shape in zip(KERNEL_ORDERS, kernel_shapes)
    ]
    zone = vmem((TILES, 2 * ROWS, 128))
    pixels_wide, vectors2, vectors1, *carry = call(
        functools.partial(tail_kernel, n),
        (
            pre_grad,
            group,
            padded,
            first,
            pixels_tiles,
            pixels_far,
            first_weight,
            first_far,
            merged_grad,
            stats2,
            live,
            sums2,
            counts,
            norm1,
            norm2,
            kernel,
            stats1,
            *done1,
            *arrive2,
            *mid3,
            excite_grad,
            squeeze_grad,
        ),
        [(wide, F32), vectors, vectors]
        + [(shape, BF16) for shape in shapes * 2 + kernel_shapes]
        + [(back_shape, BF16)],
        [
            consts,
            consts,
            mask10,
            local,
            vmem(stat, F32),
            wide_buf,
            wide_buf,
            zone,
            zone,
            weight_buf,
            weight_buf,
            vmem((ROWS, 128), F32),
            vmem((512, 9 * 256)),
            vmem((512, 9 * 256)),
            *(vmem(rooms[k][kind]) for kind in (2, 3, 4) for k in (2, 3)),
            *(vmem(room[5]) for room in rooms),
            *(vmem(shape) for shape in shapes),
            *(vmem(shape) for room in rooms for shape in room),
            *(vmem(shape) for shape in kernel_shapes),
            *(vmem(shape) for room in kernel_rooms for shape in room),
            vmem(back_shape[2:]),
            vmem(back_shape[3:]),
            DMA((5,)),
            DMA((TILES,)),
            DMA((TILES,)),
            sem,
            sem,
            pltpu.SemaphoreType.REGULAR,
            *part_sems(n, 11),
        ],
        5,
        in_specs=[ANY] * 9 + [VMEM] * 16,
        out_specs=[ANY, VMEM, VMEM] + [ANY] * 11,
    )
    sums = [s.reshape(4, 1024, 128) for s in carry[0:8]]
    kernel_sums = [s.reshape(TILES, 256, 128) for s in carry[8:10]]
    late = pl.BlockSpec((1, 1024, 128), lambda j: (jnp.maximum(j - 4, 0), 0, 0))
    early = pl.BlockSpec((1, 1024, 128), lambda j: (jnp.minimum(j, 3), 0, 0))

    def by_tile(rows):
        return pl.BlockSpec((rows, 128), lambda j: (0, j))

    def whole(shape):
        return pl.BlockSpec(shape, lambda j: (0,) * len(shape))

    ahead_all, back_all = ahead_sums.reshape(n, -1, 128), carry[10].reshape(n, -1, 128)
    half_kernel = pl.BlockSpec((1, 256, 128), lambda j: (j, 0, 0))
    results = call(
        finish_kernel,
        (*sums, pixels_wide, *kernel_sums, ahead_all, back_all, vectors1, vectors2, vectors3),
        [
            ((2 * HALF, HALF), F32),
            ((2 * HALF, HALF), F32),
            ((ROWS, HALF), F32),
            ((9 * GROUP_WIDTH, HALF), F32),
            ((2 * se, HALF), F32),
            ((1, HALF), F32),
            ((2 * HALF, se), F32),
            ((1, se), F32),
        ]
        + [((1, HALF), F32)] * 6,
        [
            vmem(back_all.shape, F32),
            vmem((n * IMGS, se)),
            vmem((n * IMGS, se)),
        ],
        in_specs=[early, early, late, late] * 2
        + [pl.BlockSpec((1, ROWS, 128), lambda j: (j, 0, 0)), half_kernel, half_kernel]
        + [whole(ahead_all.shape), whole(back_all.shape)]
        + [whole(vectors[0])] * 3,
        out_specs=[
            by_tile(2 * HALF),
            by_tile(2 * HALF),
            by_tile(ROWS),
            by_tile(9 * GROUP_WIDTH),
            by_tile(2 * se),
            by_tile(1),
            whole((2 * HALF, se)),
            whole((1, se)),
        ]
        + [by_tile(1)] * 6,
        grid=(TILES,),
    )
    last_weight_grad, first_weight_grad, pixels_grad, group_weight_grad = results[:4]
    excite_weight_grad, excite_bias_grad, squeeze_weight_grad, squeeze_bias_grad = results[4:8]
    rows = [result[0] for result in results[8:]]
    first_gain_grad, first_shift_grad = rows[0:2]
    group_gain_grad, group_shift_grad = rows[2:4]
    last_gain_grad, last_shift_grad = rows[4:6]
    group_weight_grad = group_weight_grad.reshape(3, 3, GROUP_WIDTH, HALF)
    squeeze_bias_grad, excite_bias_grad = squeeze_bias_grad[0], excite_bias_grad[0]
    return (
        block_out,
        pixels_grad,
        first_weight_grad,
        first_gain_grad,
        first_shift_grad,
        group_weight_grad,
        group_gain_grad,
        group_shift_grad,
        squeeze_weight_grad,
        squeeze_bias_grad,
        excite_weight_grad,
        excite_bias_grad,
        last_weight_grad,
        last_gain_grad,
        last_shift_grad,
    )


def solution(mesh):
    wide = P("img", "ch")
    matrix, vector = P(None, "ch"), P("ch")
    cube = P(None, None, None, "ch")
    weights = (matrix, vector, vector, cube, vector, vector, matrix, vector, matrix, vector, matrix, vector, vector)
    return jax.shard_map(
        functools.partial(body, mesh.shape["img"]),
        mesh=mesh,
        in_specs=(wide, P(), *weights, wide),
        out_specs=(wide, wide, *weights),
        check_vma=False,
    )
```
